32 devices in a mesh: items: 8 (over y, x, core), blk: 4 (over z).
Axes of the slice: x: 2, y: 2, z: 4, core: 2. Of those that a mesh axis runs over, the one named last changes fastest.
Arguments:
- tokens: bfloat16 [24, 832, 768], P('items', 'blk'), may hold values from -6 to 6
- cap_lengths: int32 [24], P('items'), may hold values from 8 to 512, as said below
- first_gain: float32 [768], replicated, may hold values from 0.1 to 1.9
- first_shift: float32 [768], replicated, may hold values from -3 to 3
- query_weight: bfloat16 [768, 768], replicated, may hold values from -0.4375 to 0.4375
- query_bias: float32 [768], replicated, may hold values from -3 to 3
- key_weight: bfloat16 [768, 768], replicated, may hold values from -0.21875 to 0.21875
- value_weight: bfloat16 [768, 768], replicated, may hold values from -0.21875 to 0.21875
- value_bias: float32 [768], replicated, may hold values from -3 to 3
- out_weight: bfloat16 [768, 768], replicated, may hold values from -0.625 to 0.625
- out_bias: float32 [768], replicated, may hold values from -3 to 3
- second_gain: float32 [768], replicated, may hold values from 0.1 to 1.9
- second_shift: float32 [768], replicated, may hold values from -3 to 3
- inner_weight: bfloat16 [768, 3072], replicated, may hold values from -0.21875 to 0.21875
- inner_bias: float32 [3072], replicated, may hold values from -3 to 3
- outer_weight: bfloat16 [3072, 768], replicated, may hold values from -0.109375 to 0.109375
- outer_bias: float32 [768], replicated, may hold values from -3 to 3
- cotangent: bfloat16 [24, 832, 768], P('items', 'blk'), may hold values from -6 to 6
Outputs:
- layer_out: bfloat16 [24, 832, 768], P('items', 'blk')
- grad_tokens: bfloat16 [24, 832, 768], P('items', 'blk')
- grad_first_gain: float32 [768], replicated
- grad_first_shift: float32 [768], replicated
- grad_query_weight: float32 [768, 768], replicated
- grad_query_bias: float32 [768], replicated
- grad_key_weight: float32 [768, 768], replicated
- grad_value_weight: float32 [768, 768], replicated
- grad_value_bias: float32 [768], replicated
- grad_out_weight: float32 [768, 768], replicated
- grad_out_bias: float32 [768], replicated
- grad_second_gain: float32 [768], replicated
- grad_second_shift: float32 [768], replicated
- grad_inner_weight: float32 [768, 3072], replicated
- grad_inner_bias: float32 [3072], replicated
- grad_outer_weight: float32 [3072, 768], replicated
- grad_outer_bias: float32 [768], replicated
The draws below stay inside these ranges and needn't reach their ends.
Inputs may be any that keep to these rules, and one draw needn't show every extreme that they name: `cap_lengths`: in each aligned block of 3 items exactly one item, drawn from the seed, has 512 caption rows; the others are mostly short.
All inputs are finite; a program needn't handle non-finite values.
Results may differ from the reference program's by a relative error of at most 0.014.
The reference program's roundings to bfloat16 on the way count: a program that leaves them out, or rounds other values in their place, can miss the bound.
Values may be sent and summed in bfloat16 or wider, within the bound.
No kernel may reach another device: no remote copies, remote signals or barrier semaphores. Data moves between devices by JAX's collectives and lax.ppermute only.
A program may use at most 256 MiB of HBM per device.

```python
import math
import jax
import jax.numpy as jnp
from jax import lax

D = 768
HD = 64
FF = 3072
SEQ = 832
IMG = 197
CAP = 512
MIN_CAP = 8
ITEM_DEV = 3
ITEMS = 24


def draw_cap_lengths(key, part):
    key = jax.random.fold_in(key, 11)
    draw_one, draw_two, draw_three, draw_four = jax.random.split(key, 4)
    span_count = CAP - MIN_CAP + 1
    tail_draw = jax.random.randint(draw_one, (ITEMS,), 0, span_count)
    tail_draw = jnp.minimum(tail_draw, jax.random.randint(draw_two, (ITEMS,), 0, span_count))
    tail_draw = jnp.minimum(tail_draw, jax.random.randint(draw_three, (ITEMS,), 0, span_count))
    group_count = ITEMS // ITEM_DEV
    chosen = jax.random.randint(draw_four, (group_count,), 0, ITEM_DEV)
    slot_index = jnp.arange(ITEMS, dtype=jnp.int32)
    longest = slot_index % ITEM_DEV == chosen[slot_index // ITEM_DEV]
    return jnp.where(longest, CAP, MIN_CAP + tail_draw).astype(jnp.int32)


def block_scale(own_key, extent, shards, least, largest):
    def one(dim, blocks):
        draws = jax.random.uniform(jax.random.fold_in(jax.random.fold_in(own_key, 6), dim), (blocks,), jnp.float32, least / len(shards), largest / len(shards))
        return jnp.repeat(jnp.exp(draws), extent[dim] // blocks).reshape((-1,) + (1,) * (len(extent) - dim - 1))

    factor_of = one(*shards[0])
    for cut in shards[1:]:
        factor_of = factor_of * one(*cut)
    return factor_of


def normal_values(rng, shape, scale, reach, pieces=(), kind=jnp.bfloat16):
    drawn = scale * jax.random.normal(rng, shape, jnp.float32)
    if pieces:
        drawn = drawn * block_scale(rng, shape, pieces, -0.22, 0.18)
    return jnp.clip(drawn, -reach, reach).astype(kind)


def setup_inputs(seed: int = 0) -> dict:
    streams_of = jax.random.split(jax.random.key(seed), 19)
    tokens = normal_values(streams_of[0], (ITEMS, SEQ, D), 1.0, 6.0, ((0, 8), (1, 4)))
    cap_lengths = draw_cap_lengths(jax.random.fold_in(streams_of[18], 71), 0)
    first_gain = jnp.clip(1.0 + 0.18 * jax.random.normal(streams_of[2], (D,), jnp.float32), 0.1, 1.9)
    first_shift = normal_values(streams_of[3], (D,), 0.3, 3.0, (), jnp.float32)
    query_weight = normal_values(streams_of[4], (D, D), (D // 4) ** -0.5, 0.4375)
    query_bias = normal_values(streams_of[5], (D,), 0.5, 3.0, (), jnp.float32)
    key_weight = normal_values(streams_of[6], (D, D), D ** -0.5, 0.21875)
    value_weight = normal_values(streams_of[7], (D, D), D ** -0.5, 0.21875)
    value_bias = normal_values(streams_of[8], (D,), 0.5, 3.0, (), jnp.float32)
    out_weight = normal_values(streams_of[9], (D, D), (D // 8) ** -0.5, 0.625)
    out_bias = normal_values(streams_of[10], (D,), 0.3, 3.0, (), jnp.float32)
    second_gain = jnp.clip(1.0 + 0.18 * jax.random.normal(streams_of[11], (D,), jnp.float32), 0.1, 1.9)
    second_shift = normal_values(streams_of[12], (D,), 0.3, 3.0, (), jnp.float32)
    inner_weight = normal_values(streams_of[13], (D, FF), D ** -0.5, 0.21875)
    inner_bias = normal_values(streams_of[14], (FF,), 0.5, 3.0, (), jnp.float32)
    outer_weight = normal_values(streams_of[15], (FF, D), FF ** -0.5, 0.109375)
    outer_bias = normal_values(streams_of[16], (D,), 0.3, 3.0, (), jnp.float32)
    cotangent = normal_values(streams_of[17], (ITEMS, SEQ, D), 1.0, 6.0, ((0, 8), (1, 4)))
    return dict(tokens=tokens, cap_lengths=cap_lengths, first_gain=first_gain, first_shift=first_shift, query_weight=query_weight, query_bias=query_bias, key_weight=key_weight, value_weight=value_weight, value_bias=value_bias, out_weight=out_weight, out_bias=out_bias, second_gain=second_gain, second_shift=second_shift, inner_weight=inner_weight, inner_bias=inner_bias, outer_weight=outer_weight, outer_bias=outer_bias, cotangent=cotangent)


@jax.custom_vjp
def low(v):
    return lax.optimization_barrier(v.astype(jnp.bfloat16)).astype(jnp.float32)

@jax.custom_vjp
def low_back(v):
    return v

def low_keep(v):
    return (low(v), None)

def low_pass(kept, grad):
    return (grad,)

def back_keep(v):
    return (v, None)

def back_low(kept, grad):
    return (low(grad),)
low.defvjp(low_keep, low_pass)
low_back.defvjp(back_keep, back_low)
norm_eps = 1e-05
masked_score = -1e+30
exact = lax.Precision.HIGHEST

def norm_rows(values, norm_gain, norm_shift):
    average = lax.optimization_barrier(jnp.mean(values, axis=-1, keepdims=True))
    centred = values - average
    spread = lax.optimization_barrier(jnp.mean(centred * centred, axis=-1, keepdims=True))
    return centred * lax.rsqrt(spread + norm_eps) * norm_gain + norm_shift

def project(left_side, weight):
    return jnp.einsum('gsd,de->gse', left_side, weight, precision=exact)

def layer(params, inputs, valid_keys):
    first_gain, first_shift, query_weight, query_bias, key_weight, value_weight, value_bias, out_weight, out_bias, second_gain, second_shift, inner_weight, inner_bias, outer_weight, outer_bias = params
    group_size, seq_length, model_width = inputs.shape
    head_count = model_width // HD
    heads_shape = (group_size, seq_length, head_count, HD)
    normed = low(norm_rows(inputs, first_gain, first_shift))
    query_rows = low(low_back(project(normed, query_weight) + query_bias)).reshape(heads_shape)
    key_rows = low(low_back(project(normed, key_weight))).reshape(heads_shape)
    value_rows = low(low_back(project(normed, value_weight) + value_bias)).reshape(heads_shape)
    raw_scores = low_back(jnp.einsum('gqhd,gkhd->ghqk', query_rows, key_rows, precision=exact))
    scores = jnp.where(valid_keys[:, None, None, :], raw_scores * HD ** (-0.5), masked_score)
    row_top = lax.optimization_barrier(jnp.max(scores, axis=-1, keepdims=True))
    shifted = jnp.exp(scores - row_top)
    attn_probs = shifted / lax.optimization_barrier(jnp.sum(shifted, axis=-1, keepdims=True))
    context = jnp.einsum('ghqk,gkhd->gqhd', low(attn_probs), value_rows, precision=exact)
    context = low(low_back(context)).reshape(group_size, seq_length, model_width)
    attended = inputs + low_back(project(context, out_weight) + out_bias)
    second_normed = low(norm_rows(attended, second_gain, second_shift))
    inner_pre = low_back(project(second_normed, inner_weight) + inner_bias)
    activated = low(jax.nn.gelu(inner_pre, approximate=False))
    return attended + project(activated, outer_weight) + outer_bias

def reference(tokens, cap_lengths, first_gain, first_shift, query_weight, query_bias, key_weight, value_weight, value_bias, out_weight, out_bias, second_gain, second_shift, inner_weight, inner_bias, outer_weight, outer_bias, cotangent):
    params = (first_gain, first_shift, query_weight.astype(jnp.float32), query_bias, key_weight.astype(jnp.float32), value_weight.astype(jnp.float32), value_bias, out_weight.astype(jnp.float32), out_bias, second_gain, second_shift, inner_weight.astype(jnp.float32), inner_bias, outer_weight.astype(jnp.float32), outer_bias)
    group_size = math.gcd(ITEMS, 4)
    group_count = ITEMS // group_size
    key_positions = jnp.arange(SEQ, dtype=jnp.int32)
    valid_all = key_positions[None, :] < (1 + IMG + cap_lengths)[:, None]
    inputs_all = tokens.astype(jnp.float32).reshape(group_count, group_size, SEQ, D)
    cot_all = cotangent.astype(jnp.float32).reshape(group_count, group_size, SEQ, D)
    valid_blocks = valid_all.reshape(group_count, group_size, SEQ)
    zero_grads = jax.tree.map(jnp.zeros_like, params)

    def group_step(running, block_in):
        inputs, cot_block, valid_keys = block_in

        def wrapped(param_set, input_rows):
            return layer(param_set, input_rows, valid_keys)
        out_block, pull_back = jax.vjp(wrapped, params, inputs)
        param_grads, input_grad = pull_back(cot_block)
        running = jax.tree.map(jnp.add, running, param_grads)
        return (running, (out_block.astype(jnp.bfloat16), input_grad.astype(jnp.bfloat16)))
    totals, (out_blocks, grad_blocks) = lax.scan(group_step, zero_grads, (inputs_all, cot_all, valid_blocks))
    layer_out = out_blocks.reshape(ITEMS, SEQ, D)
    grad_tokens = grad_blocks.reshape(ITEMS, SEQ, D)
    return (layer_out, grad_tokens, totals[0], totals[1], totals[2], totals[3], totals[4], totals[5], totals[6], totals[7], totals[8], totals[9], totals[10], totals[11], totals[12], totals[13], totals[14])
```

```python
import functools

import jax
import jax.numpy as jnp
from jax import lax
from jax.experimental import pallas as pl
from jax.experimental.pallas import tpu as pltpu
from jax.sharding import PartitionSpec as P

HD = 64
IMG = 197
CAP = 512
STEP = 256
FF_STEP = 512
norm_eps = 1e-05
masked_score = -1e30
f32 = jnp.float32
bf16 = jnp.bfloat16
TOKEN = jax.ShapeDtypeStruct((8, 128), f32)
FREE = pl.BlockSpec(memory_space=pl.ANY)


def dot_nn(a, b):
    return lax.dot_general(a, b, (((1,), (0,)), ((), ())), preferred_element_type=f32)


def dot_nt(a, b):
    return lax.dot_general(a, b, (((1,), (1,)), ((), ())), preferred_element_type=f32)


def dot_tn(a, b):
    return lax.dot_general(a, b, (((0,), (0,)), ((), ())), preferred_element_type=f32)


def norm_core(rows):
    average = jnp.mean(rows, axis=-1, keepdims=True)
    centred = rows - average
    spread = jnp.mean(centred * centred, axis=-1, keepdims=True)
    scale = lax.rsqrt(spread + norm_eps)
    return centred * scale, scale


def norm_back(unit, scale, gain, grad):
    weighted = grad * gain
    first = jnp.mean(weighted, axis=-1, keepdims=True)
    second = jnp.mean(weighted * unit, axis=-1, keepdims=True)
    return scale * (weighted - first - unit * second)


def normal_cdf_pdf(v):
    size = jnp.abs(v) * 0.7071067811865476
    t = 1.0 / (1.0 + 0.3275911 * size)
    poly = t * (0.254829592 + t * (-0.284496736 + t * (1.421413741 + t * (-1.453152027 + t * 1.061405429))))
    bell = jnp.exp(-0.5 * v * v)
    tail = 0.5 * poly * bell
    return jnp.where(v >= 0, 1.0 - tail, tail), 0.3989422804014327 * bell


def cost(us):
    return pl.CostEstimate(flops=int(us * 0.5e9), bytes_accessed=int(us * 1.5e6), transcendentals=0)


def key_steps(limit, key_count, body):
    steps = key_count // STEP
    for n in range(1, steps + 1):
        low, high = (n - 1) * STEP, n * STEP
        cond = limit > low if n == steps else (limit <= high if n == 1 else (limit > low) & (limit <= high))
        pl.when(cond)(functools.partial(body, high))


def attend_kernel(
    limit_ref, z_ref,
    own_ref, r1_ref, l1_ref, r2_ref, l2_ref, far_ref,
    wq_ref, wk_ref, wv_ref, gain_ref, shift_ref, bq_ref, bv_ref,
    tok_ref, norm_ref, ownnorm_ref, q_ref, k_ref, v_ref, ctx_ref, lse_ref, logs_ref,
):
    item = pl.program_id(0)
    limit = limit_ref[item]
    z = z_ref[0]
    rows, width = own_ref.shape
    key_count = tok_ref.shape[0]
    tail = key_count - 3 * rows

    def place(src, at, cond):
        @pl.when(cond & (at < 3))
        def _():
            tok_ref[pl.ds(pl.multiple_of(at * rows, 16), rows), :] = src[...]

        @pl.when(cond & (at == 3))
        def _():
            tok_ref[3 * rows:key_count, :] = src[0:tail, :]

    place(own_ref, z, z >= 0)
    place(r1_ref, z - 1, z >= 1)
    place(l1_ref, z + 1, z <= 2)
    place(r2_ref, z - 2, z >= 2)
    place(l2_ref, z + 2, z <= 1)
    place(far_ref, 0, z == 3)
    place(far_ref, 3, z == 0)
    gain, shift = gain_ref[...], shift_ref[...]

    unit, _ = norm_core(own_ref[...].astype(f32))
    own_norm = (unit * gain + shift).astype(bf16)
    ownnorm_ref[...] = own_norm
    query = (dot_nn(own_norm, wq_ref[...]) + bq_ref[...]).astype(bf16)
    q_ref[...] = query * jnp.asarray(HD ** -0.5, bf16)

    def project(c, _):
        here = pl.ds(pl.multiple_of(c * STEP, STEP), STEP)
        unit, _ = norm_core(tok_ref[here, :].astype(f32))
        normed = (unit * gain + shift).astype(bf16)
        norm_ref[here, :] = normed
        k_ref[here, :] = dot_nn(normed, wk_ref[...]).astype(bf16)
        v_ref[here, :] = (dot_nn(normed, wv_ref[...]) + bv_ref[...]).astype(bf16)
        return 0

    lax.fori_loop(0, (limit + STEP - 1) // STEP, project, 0)

    def part(high):
        bias = jnp.where(lax.broadcasted_iota(jnp.int32, (1, high), 1) < limit, 0.0, masked_score)
        lane = lax.broadcasted_iota(jnp.int32, (rows, 2 * HD), 1)

        def pair(p):
            cols = pl.ds(pl.multiple_of(p * 2 * HD, 2 * HD), 2 * HD)
            q_pair = q_ref[:, cols]
            k_pair = k_ref[0:high, cols]
            v_pair = v_ref[0:high, cols]
            second = lane >= HD
            zero = jnp.zeros_like(q_pair)
            scores = [dot_nt(jnp.where(second == (h == 1), q_pair, zero), k_pair) + bias for h in range(2)]
            outs = []
            for h in range(2):
                top = jnp.max(scores[h], axis=1, keepdims=True)
                shifted = jnp.exp(scores[h] - top)
                total = jnp.sum(shifted, axis=1, keepdims=True)
                probs = (shifted * (1.0 / total)).astype(bf16)
                outs.append(dot_nn(probs, v_pair))
                logs_ref[...] = jnp.where(lane == 2 * p + h, top + jnp.log(total), logs_ref[...])
            ctx_ref[:, cols] = jnp.where(second, outs[1], outs[0]).astype(bf16)

        def pairs(i, _):
            pair(2 * i)
            pair(2 * i + 1)
            return 0

        lax.fori_loop(0, width // (4 * HD), pairs, 0)

    key_steps(limit, key_count, part)
    lse_ref[...] = logs_ref[...].T[0:lse_ref.shape[0], :]


def whole(shape):
    return pl.BlockSpec(shape, lambda *_: (0,) * len(shape))


def attend(limits, z, own, parts, weights, key_count):
    count, rows, width = own.shape
    row_spec = pl.BlockSpec((None, rows, width), lambda i, *_: (i, 0, 0))
    key_spec = pl.BlockSpec((None, key_count, width), lambda i, *_: (i, 0, 0))
    lse_spec = pl.BlockSpec((None, 16, rows), lambda i, *_: (i, 0, 0))
    wq, wk, wv, gain, shift, bq, bv = weights
    vec = whole((1, width))
    mat = whole((width, width))
    row = jax.ShapeDtypeStruct((count, rows, width), bf16)
    key = jax.ShapeDtypeStruct((count, key_count, width), bf16)
    return pl.pallas_call(
        attend_kernel,
        out_shape=(key, key, row, row, key, key, row, jax.ShapeDtypeStruct((count, 16, rows), f32)),
        grid_spec=pltpu.PrefetchScalarGridSpec(
            num_scalar_prefetch=2,
            grid=(count,),
            in_specs=[row_spec] * 6 + [mat] * 3 + [vec] * 4,
            out_specs=[key_spec, key_spec, row_spec, row_spec, key_spec, key_spec, row_spec, lse_spec],
            scratch_shapes=[pltpu.VMEM((rows, 2 * HD), f32)],
        ),
        compiler_params=pltpu.CompilerParams(vmem_limit_bytes=56 * 2**20),
        cost_estimate=cost(28),
        name="attend",
    )(limits, z, own, *parts, wq, wk, wv, gain, shift, bq, bv)


def feed_kernel(
    bit_ref, tok_ref, ctx_ref, cot_ref, wo_ref, bo_ref, gain_ref, shift_ref, w1_ref, b1_ref, w2_ref, b2_ref,
    out_ref, attg_ref, send_ref, keep_ref, norm_ref, branch_ref, ctxg_ref, small_ref, db1_ref,
    att_acc, grad_acc, unit_keep, scale_keep,
):
    step = pl.program_id(0)
    last = pl.num_programs(0) - 1

    @pl.when(step == 0)
    def _():
        attended = tok_ref[...].astype(f32) + (dot_nn(ctx_ref[...], wo_ref[...]) + bo_ref[...])
        unit, scale = norm_core(attended)
        norm_ref[...] = (unit * gain_ref[...] + shift_ref[...]).astype(bf16)
        unit_keep[...] = unit
        scale_keep[...] = jnp.broadcast_to(scale, scale_keep.shape)
        att_acc[...] = attended + b2_ref[...]
        grad_acc[...] = jnp.zeros_like(grad_acc)

    cot = cot_ref[...]
    inner = dot_nn(norm_ref[...], w1_ref[...]) + b1_ref[...]
    cdf, pdf = normal_cdf_pdf(inner)
    act = (inner * cdf).astype(bf16)
    act_grad = dot_nt(cot, w2_ref[...])
    pre = ((cdf + inner * pdf) * act_grad).astype(bf16)

    @pl.when(step <= last // 2)
    def _():
        send_ref[0] = act
        send_ref[1] = pre

    @pl.when(step > last // 2)
    def _():
        keep_ref[0] = act
        keep_ref[1] = pre

    db1_ref[...] = jnp.sum(pre.astype(f32), axis=0, keepdims=True)
    att_acc[...] += dot_nn(act, w2_ref[...])
    grad_acc[...] += dot_nt(pre, w1_ref[...])

    @pl.when(step == last)
    def _():
        out_ref[...] = att_acc[...].astype(bf16)
        unit, grad = unit_keep[...], grad_acc[...]
        cot_wide = cot_ref[...].astype(f32)
        attended_grad = cot_wide + norm_back(unit, scale_keep[:, 0:1], gain_ref[...], grad)
        attg_ref[...] = attended_grad
        branch = attended_grad.astype(bf16)
        branch_ref[...] = branch
        ctxg_ref[...] = dot_nt(branch, wo_ref[...]).astype(bf16)
        small_ref[0:1, :] = jnp.sum(grad * unit, axis=0, keepdims=True)
        small_ref[1:2, :] = jnp.sum(grad, axis=0, keepdims=True)
        small_ref[2:3, :] = jnp.sum(branch.astype(f32), axis=0, keepdims=True)
        small_ref[3:4, :] = jnp.sum(cot_wide, axis=0, keepdims=True)
        small_ref[4:8, :] = jnp.zeros((4, small_ref.shape[1]), f32)


def feed(bit, tok, ctx, cot, weights):
    wo, bo, gain, shift, w1, b1, w2, b2 = weights
    rows, width = tok.shape
    hidden = w1.shape[1]
    row = whole((rows, width))
    vec = whole((1, width))
    half = hidden // FF_STEP // 2

    def chunk(j, bit_ref):
        return jnp.where(j < half, (1 - bit_ref[0]) * half + j, bit_ref[0] * half + j - half)

    pair = jax.ShapeDtypeStruct((2, rows, hidden // 2), bf16)
    return pl.pallas_call(
        feed_kernel,
        out_shape=(
            jax.ShapeDtypeStruct((rows, width), bf16),
            jax.ShapeDtypeStruct((rows, width), f32),
            pair,
            pair,
            jax.ShapeDtypeStruct((rows, width), bf16),
            jax.ShapeDtypeStruct((rows, width), bf16),
            jax.ShapeDtypeStruct((rows, width), bf16),
            jax.ShapeDtypeStruct((8, width), f32),
            jax.ShapeDtypeStruct((1, hidden), f32),
        ),
        grid_spec=pltpu.PrefetchScalarGridSpec(
            num_scalar_prefetch=1,
            grid=(2 * half,),
            in_specs=[
                row, row, row, whole((width, width)), vec, vec, vec,
                pl.BlockSpec((width, FF_STEP), lambda j, b: (0, chunk(j, b))),
                pl.BlockSpec((1, FF_STEP), lambda j, b: (0, chunk(j, b))),
                pl.BlockSpec((FF_STEP, width), lambda j, b: (chunk(j, b), 0)),
                vec,
            ],
            out_specs=[
                row, row,
                pl.BlockSpec((2, rows, FF_STEP), lambda j, b: (0, 0, jnp.minimum(j, half - 1))),
                pl.BlockSpec((2, rows, FF_STEP), lambda j, b: (0, 0, jnp.maximum(j - half, 0))),
                row, row, row, whole((8, width)),
                pl.BlockSpec((1, FF_STEP), lambda j, b: (0, chunk(j, b))),
            ],
            scratch_shapes=[
                pltpu.VMEM((rows, width), f32),
                pltpu.VMEM((rows, width), f32),
                pltpu.VMEM((rows, width), f32),
                pltpu.VMEM((rows, 128), f32),
            ],
        ),
        compiler_params=pltpu.CompilerParams(vmem_limit_bytes=56 * 2**20),
        cost_estimate=cost(29),
        name="feed",
    )(bit, tok, ctx, cot, wo, bo, gain, shift, w1, b1, w2, b2)


def attend_back_kernel(
    limit_ref, z_ref,
    own_ref, q_ref, k_ref, v_ref, ctxg_ref, lse_ref, gain_ref, shift_ref,
    tok_any, wq_any, wk_any, wv_any, *rest, item,
):
    part_ref, dq_ref, dk_ref, dv_ref, small_ref, tok_ref, wq_ref, wk_ref, wv_ref, sems = rest[-10:]
    fetch = [
        pltpu.make_async_copy(src, dst, sems.at[i])
        for i, (src, dst) in enumerate((
            (tok_any.at[item], tok_ref), (wk_any, wk_ref), (wv_any, wv_ref), (wq_any, wq_ref)))
    ]
    for one in fetch:
        one.start()
    limit = limit_ref[0]
    z = z_ref[0]
    rows, width = own_ref.shape
    key_count = tok_ref.shape[0]

    def part(high):
        bias = jnp.where(lax.broadcasted_iota(jnp.int32, (high, 1), 0) < limit, 0.0, masked_score)
        lane = lax.broadcasted_iota(jnp.int32, (rows, 2 * HD), 1)

        lane_keys = lax.broadcasted_iota(jnp.int32, (high, 2 * HD), 1)

        def pair(p):
            cols = pl.ds(pl.multiple_of(p * 2 * HD, 2 * HD), 2 * HD)
            q_pair = q_ref[:, cols]
            k_pair = k_ref[0:high, cols]
            v_pair = v_ref[0:high, cols]
            g_pair = ctxg_ref[:, cols]
            k_turned = k_pair.T
            zero = jnp.zeros_like(q_pair)
            pre = []
            for h in range(2):
                mine = (lane >= HD) == (h == 1)
                pre.append((
                    dot_nt(k_pair, jnp.where(mine, q_pair, zero)) + bias,
                    dot_nt(v_pair, jnp.where(mine, g_pair, zero)),
                ))
            dqs, dks, dvs = [], [], []
            for h, (scores, prob_grad) in enumerate(pre):
                probs = jnp.exp(scores - lse_ref[pl.ds(2 * p + h, 1), :])
                delta = jnp.sum(probs * prob_grad, axis=0, keepdims=True)
                score_grad = (probs * (prob_grad - delta)).astype(bf16)
                dvs.append(dot_nn(probs.astype(bf16), g_pair))
                dks.append(dot_nn(score_grad, q_pair))
                dqs.append(dot_nn(k_turned[h * HD:(h + 1) * HD, :], score_grad))
            dq_ref[:, cols] = (jnp.concatenate(dqs, axis=0).T * (HD ** -0.5)).astype(bf16)
            dk_ref[0:high, cols] = jnp.where(lane_keys >= HD, dks[1], dks[0]).astype(bf16)
            dv_ref[0:high, cols] = jnp.where(lane_keys >= HD, dvs[1], dvs[0]).astype(bf16)

        def pairs(i, _):
            pair(2 * i)
            pair(2 * i + 1)
            return 0

        lax.fori_loop(0, width // (4 * HD), pairs, 0)

    key_steps(limit, key_count, part)

    for one in fetch:
        one.wait()
    small_ref[...] = jnp.zeros_like(small_ref)

    def inward(c, _):
        here = pl.ds(pl.multiple_of(c * STEP, STEP), STEP)
        unit, _ = norm_core(tok_ref[here, :].astype(f32))
        dk, dv = dk_ref[here, :], dv_ref[here, :]
        grad = dot_nt(dk, wk_ref[...]) + dot_nt(dv, wv_ref[...])
        small_ref[0:1, :] += jnp.sum(grad * unit, axis=0, keepdims=True)
        small_ref[1:2, :] += jnp.sum(grad, axis=0, keepdims=True)
        small_ref[3:4, :] += jnp.sum(dv.astype(f32), axis=0, keepdims=True)
        part_ref[here, :] = grad.astype(bf16)
        return 0

    def outward(c, _):
        part_ref[pl.ds(pl.multiple_of(c * STEP, STEP), STEP), :] = jnp.zeros((STEP, width), bf16)
        return 0

    used = (limit + STEP - 1) // STEP
    lax.fori_loop(0, used, inward, 0)
    lax.fori_loop(used, key_count // STEP, outward, 0)
    part_ref[key_count:, :] = jnp.zeros((part_ref.shape[0] - key_count, width), bf16)

    unit, _ = norm_core(own_ref[...].astype(f32))
    dq = dq_ref[...]
    grad = dot_nt(dq, wq_ref[...])
    small_ref[0:1, :] += jnp.sum(grad * unit, axis=0, keepdims=True)
    small_ref[1:2, :] += jnp.sum(grad, axis=0, keepdims=True)
    small_ref[2:3, :] = jnp.sum(dq.astype(f32), axis=0, keepdims=True)
    here = pl.ds(pl.multiple_of(z * rows, 16), rows)
    part_ref[here, :] = (part_ref[here, :].astype(f32) + grad).astype(bf16)


def attend_back(item, limits, z, own, tok, q, k, v, ctxg, lse, weights, into=None, after=()):
    count, rows, width = own.shape
    key_count = tok.shape[1]
    wq, wk, wv, gain, shift = weights
    row_spec = pl.BlockSpec((None, rows, width), lambda i, *_: (item, 0, 0))
    key_spec = pl.BlockSpec((None, key_count, width), lambda i, *_: (item, 0, 0))
    lse_spec = pl.BlockSpec((None, 16, rows), lambda i, *_: (item, 0, 0))
    vec, free = whole((1, width)), FREE
    into = () if into is None else tuple(into)
    return pl.pallas_call(
        functools.partial(attend_back_kernel, item=item),
        out_shape=(
            jax.ShapeDtypeStruct((4 * rows, width), bf16),
            jax.ShapeDtypeStruct((count, rows, width), bf16),
            jax.ShapeDtypeStruct((count, key_count, width), bf16),
            jax.ShapeDtypeStruct((count, key_count, width), bf16),
            jax.ShapeDtypeStruct((8, width), f32),
        ),
        grid_spec=pltpu.PrefetchScalarGridSpec(
            num_scalar_prefetch=2,
            grid=(1,),
            in_specs=[row_spec, row_spec, key_spec, key_spec, row_spec, lse_spec, vec, vec]
            + [free] * (4 + len(into) + len(after)),
            out_specs=[whole((4 * rows, width)), row_spec, key_spec, key_spec, whole((8, width))],
            scratch_shapes=[pltpu.VMEM((key_count, width), bf16)]
            + [pltpu.VMEM((width, width), bf16)] * 3 + [pltpu.SemaphoreType.DMA((4,))],
        ),
        input_output_aliases={14 + i: 1 + i for i in range(len(into))},
        compiler_params=pltpu.CompilerParams(vmem_limit_bytes=56 * 2**20),
        cost_estimate=cost(13),
        name="attend_back",
    )(limits[item:item + 1], z, own, q, k, v, ctxg, lse, gain, shift, tok, wq, wk, wv, *into, *after)


def feed_weight_kernel(kind_ref, ff_ref, recv_ref, norm_ref, normr_ref, cot_ref, cotr_ref, *rest, through):
    outs = rest[-3 - through:-1 - through]
    rest[-1][...] = jnp.zeros(TOKEN.shape, f32)
    step = pl.program_id(0)
    kind = kind_ref[step]

    def put(value):
        for i, out in enumerate(outs):
            @pl.when(step == i)
            def _():
                out[...] = value.astype(out.dtype)

    @pl.when(kind == 0)
    def _():
        put(dot_tn(ff_ref[...], cot_ref[...]) + dot_tn(recv_ref[...], cotr_ref[...]))

    @pl.when(kind != 0)
    def _():
        put(dot_tn(norm_ref[...], ff_ref[...]) + dot_tn(normr_ref[...], recv_ref[...]))


def feed_weights(kinds, ff, recv, norm, norm_recv, cot, cot_recv, after=(), through=()):
    rows, width = cot.shape
    row = whole((rows, width))
    unit = pl.BlockSpec((None, rows, width), lambda s, kind_ref: (kind_ref[s], 0, s))
    mat = whole((width, width))
    return pl.pallas_call(
        functools.partial(feed_weight_kernel, through=len(through)),
        out_shape=(jax.ShapeDtypeStruct((width, width), bf16),) * 2
        + tuple(jax.ShapeDtypeStruct(x.shape, x.dtype) for x in through) + (TOKEN,),
        grid_spec=pltpu.PrefetchScalarGridSpec(
            num_scalar_prefetch=1,
            grid=(2,),
            in_specs=[unit, unit, row, row, row, row] + [FREE] * (len(through) + len(after)),
            out_specs=[mat] * 2 + [FREE] * len(through) + [whole(TOKEN.shape)],
        ),
        input_output_aliases={7 + i: 2 + i for i in range(len(through))},
        compiler_params=pltpu.CompilerParams(vmem_limit_bytes=56 * 2**20),
        cost_estimate=cost(7),
        name="feed_weights",
    )(kinds, ff, recv, norm, norm_recv, cot, cot_recv, *through, *after)


def attend_weight_kernel(
    half_ref, limit_ref, norm_ref, own_ref, dq_ref, dk_ref, dv_ref, ctx_ref, branch_ref, *rest,
):
    acc_ref = rest[-1]
    outs = rest[-4:-2]
    rest[-2][...] = jnp.zeros(TOKEN.shape, f32)
    step = pl.program_id(0)
    item = step % 3
    unit = 2 * half_ref[0] + step // 3

    @pl.when(item == 0)
    def _():
        acc_ref[...] = jnp.zeros_like(acc_ref)

    def keys(grad):
        def chunk(c, _):
            here = pl.ds(pl.multiple_of(c * STEP, STEP), STEP)
            acc_ref[...] += dot_tn(norm_ref[here, :], grad[here, :])
            return 0
        lax.fori_loop(0, (limit_ref[item] + STEP - 1) // STEP, chunk, 0)

    def add(left, right):
        acc_ref[...] += dot_tn(left[...], right[...])

    pl.when(unit == 0)(lambda: add(own_ref, dq_ref))
    pl.when(unit == 1)(lambda: keys(dk_ref))
    pl.when(unit == 2)(lambda: keys(dv_ref))
    pl.when(unit == 3)(lambda: add(ctx_ref, branch_ref))

    for i in range(2):
        @pl.when(step == 2 + 3 * i)
        def _():
            outs[i][...] = acc_ref[...].astype(outs[i].dtype)


def attend_weights(half, limits, norm, own, dq, dk, dv, ctx, branch, after=()):
    count, rows, width = own.shape
    key_count = norm.shape[1]

    def by_item(size, *units):
        def at(s, half_ref, _):
            unit = 2 * half_ref[0] + s // 3
            used = unit == units[0]
            for one in units[1:]:
                used = used | (unit == one)
            return jnp.where(used, s % 3, 0), 0, 0
        return pl.BlockSpec((None, size, width), at)

    return pl.pallas_call(
        attend_weight_kernel,
        out_shape=(jax.ShapeDtypeStruct((width, width), bf16),) * 2 + (TOKEN,),
        grid_spec=pltpu.PrefetchScalarGridSpec(
            num_scalar_prefetch=2,
            grid=(6,),
            in_specs=[
                by_item(key_count, 1, 2), by_item(rows, 0), by_item(rows, 0), by_item(key_count, 1), by_item(key_count, 2),
                by_item(rows, 3), by_item(rows, 3),
            ] + [FREE] * len(after),
            out_specs=[whole((width, width))] * 2 + [whole(TOKEN.shape)],
            scratch_shapes=[pltpu.VMEM((width, width), f32)],
        ),
        compiler_params=pltpu.CompilerParams(vmem_limit_bytes=56 * 2**20),
        cost_estimate=cost(9),
        name="attend_weights",
    )(half, limits, norm, own, dq, dk, dv, ctx, branch, *after)


def close_kernel(tok_ref, attg_ref, m0_ref, m1_ref, m2_ref, gain_ref, *rest):
    out_ref = rest[-2]
    rest[-1][...] = jnp.zeros(TOKEN.shape, f32)
    for i, part_ref in enumerate((m0_ref, m1_ref, m2_ref)):
        @pl.when(pl.program_id(0) == i)
        def _():
            unit, scale = norm_core(tok_ref[...].astype(f32))
            grad = part_ref[...].astype(f32)
            out_ref[...] = (attg_ref[...] + norm_back(unit, scale, gain_ref[...], grad)).astype(bf16)


def close(tok, attg, parts, gain, after=()):
    count, rows, width = tok.shape
    row = pl.BlockSpec((None, rows, width), lambda i: (i, 0, 0))
    return pl.pallas_call(
        close_kernel,
        out_shape=(jax.ShapeDtypeStruct((count, rows, width), bf16), TOKEN),
        grid=(count,),
        in_specs=[row, row] + [whole((rows, width))] * 3 + [whole((1, width))]
        + [FREE] * len(after),
        out_specs=[row, whole(TOKEN.shape)],
        compiler_params=pltpu.CompilerParams(vmem_limit_bytes=56 * 2**20),
        cost_estimate=cost(4),
        name="close",
    )(tok, attg, *parts, gain, *after)


def place_pieces(src, dst, mask, pieces):
    size = src.shape[0] // pieces
    for i in range(pieces):
        at = pl.multiple_of(jnp.bitwise_xor(mask, i) * size, 8)
        dst[pl.ds(at, size), :] = src[i * size:(i + 1) * size, :].astype(f32)


def feed_place_kernel(at_ref, mine_ref, other_ref, *rest):
    outer_ref, inner_ref = rest[-3:-1]
    rest[-1][...] = jnp.zeros(TOKEN.shape, f32)
    step = pl.program_id(0)
    unit = step % 4
    core, mask = at_ref[0], at_ref[3 + unit % 2]

    def copy(dst):
        @pl.when(unit // 2 == core)
        def _():
            place_pieces(mine_ref, dst, mask, PIECES)

        @pl.when(unit // 2 != core)
        def _():
            place_pieces(other_ref, dst, mask, PIECES)

    pl.when(step < 4)(lambda: copy(outer_ref))
    pl.when(step >= 4)(lambda: copy(inner_ref))


PIECES = 8


def feed_place(at, mine, other, after=()):
    width = mine.shape[-1]

    def source(which):
        def index(s, at_ref):
            low = jnp.bitwise_xor(at_ref[0], which) == 0
            in_low = s % 4 < 2
            held = jnp.where(low, jnp.where(s < 4, 4, 5), s // 4 * 4 + 2)
            t = jnp.where(low == in_low, s, held)
            return t % 2, jnp.bitwise_xor(t // 4, at_ref[1 + t % 2]), 0
        return pl.BlockSpec((None, width, width), index)

    return pl.pallas_call(
        feed_place_kernel,
        out_shape=(jax.ShapeDtypeStruct((4 * width, width), f32), jax.ShapeDtypeStruct((width, 4 * width), f32), TOKEN),
        grid_spec=pltpu.PrefetchScalarGridSpec(
            num_scalar_prefetch=1,
            grid=(8,),
            in_specs=[source(0), source(1)] + [FREE] * len(after),
            out_specs=[
                pl.BlockSpec((width, width), lambda s, _: (jnp.minimum(s, 3), 0)),
                pl.BlockSpec((width, width), lambda s, _: (0, jnp.maximum(s - 4, 0))),
                whole(TOKEN.shape),
            ],
        ),
        compiler_params=pltpu.CompilerParams(vmem_limit_bytes=56 * 2**20),
        cost_estimate=cost(11),
        name="feed_place",
    )(at, mine, other, *after)


def attend_place_kernel(at_ref, mine_ref, other_ref, *rest):
    out_refs = rest[-4:]
    core = at_ref[0]
    half = mine_ref.shape[1] // 2
    for unit, dst in enumerate(out_refs):
        u = unit % 2
        for first in range(2):
            to = dst.at[pl.ds(pl.multiple_of(jnp.bitwise_xor(at_ref[1 + u], first) * half, 8), half), :]
            rows = slice(first * half, (first + 1) * half)

            @pl.when(core == unit // 2)
            def _():
                place_pieces(mine_ref.at[u, rows, :], to, at_ref[3 + u], PIECES)

            @pl.when(core != unit // 2)
            def _():
                place_pieces(other_ref.at[u, rows, :], to, at_ref[3 + u], PIECES)


def attend_place(at, mine, other, after=()):
    width = mine.shape[-1]
    return pl.pallas_call(
        attend_place_kernel,
        out_shape=(jax.ShapeDtypeStruct((width, width), f32),) * 4,
        grid_spec=pltpu.PrefetchScalarGridSpec(
            num_scalar_prefetch=1,
            grid=(1,),
            in_specs=[whole(mine.shape)] * 2 + [FREE] * len(after),
            out_specs=[whole((width, width))] * 4,
        ),
        compiler_params=pltpu.CompilerParams(vmem_limit_bytes=56 * 2**20),
        cost_estimate=cost(7),
        name="attend_place",
    )(at, mine, other, *after)


def swap(x, axis, bit):
    return lax.ppermute(x, axis, [(i, i ^ bit) for i in range(lax.axis_size(axis))])


def side_of(axis, bit):
    return (lax.axis_index(axis) // bit) % 2


def bits_of(axis, bit):
    bits = []
    while bit < lax.axis_size(axis):
        bits.append(bit)
        bit *= 2
    return bits


class Fold:
    def __init__(self, sides, keeps, recvs):
        self.scalars, self.ins = list(sides), [*keeps, *recvs]
        half = keeps[0].shape[0] // 2
        self.outs = [((half, keeps[0].shape[1]), bf16)] * 4

    def body(self, scalars, ins, outs):
        half = outs[0].shape[0]
        for u in range(2):
            for k, side in ((u, 1 - scalars[u]), (2 + u, scalars[u])):
                at = pl.ds(pl.multiple_of(side * half, 16), half)
                outs[k][...] = (ins[u][at, :].astype(f32) + ins[2 + u][at, :].astype(f32)).astype(bf16)

    def plain(self):
        half = self.outs[0][0][0]
        sums = [k.astype(f32) + r.astype(f32) for k, r in zip(self.ins[:2], self.ins[2:])]
        cut = lambda x, side: lax.dynamic_slice_in_dim(x, side * half, half, 0).astype(bf16)
        return [cut(x, 1 - side) for x, side in zip(sums, self.scalars)] + [cut(x, side) for x, side in zip(sums, self.scalars)]


class Across:
    def __init__(self, z, n, keeps, recvs):
        self.scalars, self.ins, self.n = [z], [*keeps, *recvs], n
        size, width = keeps[0].shape[0] // n, keeps[0].shape[1]
        self.outs = [((2, size, width), bf16)] * n

    def body(self, scalars, ins, outs):
        size = outs[0].shape[1]
        for m in range(self.n):
            at = pl.ds(pl.multiple_of(jnp.bitwise_xor(scalars[0], m) * size, 16), size)
            for u in range(2):
                outs[m][u] = (ins[u][at, :].astype(f32) + ins[2 + u][at, :].astype(f32)).astype(bf16)

    def plain(self):
        sums = jnp.stack([k.astype(f32) + r.astype(f32) for k, r in zip(self.ins[:2], self.ins[2:])])
        size = sums.shape[1] // self.n
        return [lax.dynamic_slice_in_dim(sums, (self.scalars[0] ^ m) * size, size, 1).astype(bf16) for m in range(self.n)]


class Total:
    def __init__(self, pieces):
        self.scalars, self.ins = [], list(pieces)
        self.outs = [(pieces[0].shape, bf16)]

    def body(self, scalars, ins, outs):
        value = ins[0][...].astype(f32)
        for one in ins[1:]:
            value = value + one[...].astype(f32)
        outs[0][...] = value.astype(bf16)

    def plain(self):
        return [sum(x.astype(f32) for x in self.ins).astype(bf16)]


class Gathered:
    def __init__(self, pieces):
        self.scalars, self.ins = [], list(pieces)
        _, size, width = pieces[0].shape
        self.outs = [((len(pieces) * size, width), bf16)] * 2

    def body(self, scalars, ins, outs):
        size = ins[0].shape[1]
        for m, piece in enumerate(ins):
            for u in range(2):
                outs[u][m * size:(m + 1) * size, :] = piece[u]

    def plain(self):
        return [jnp.concatenate([p[u] for p in self.ins], 0) for u in range(2)]


class Join:
    def __init__(self, mine, recvs, stacked):
        self.scalars, self.ins, self.stacked = [], [*mine, *recvs], stacked
        rows, width = mine[0].shape
        self.outs = [((2, 2 * rows, width), bf16)] if stacked else [((2 * rows, width), bf16)] * 2

    def body(self, scalars, ins, outs):
        for i in range(2):
            for u in range(2):
                src = ins[2 * i + u]
                rows = slice(i * src.shape[0], (i + 1) * src.shape[0])
                if self.stacked:
                    outs[0][u, rows, :] = src[...]
                else:
                    outs[u][rows, :] = src[...]

    def plain(self):
        both = [jnp.concatenate([self.ins[u], self.ins[2 + u]], 0) for u in range(2)]
        return [jnp.stack(both)] if self.stacked else both


class Add:
    def __init__(self, x, y):
        self.scalars, self.ins, self.outs = [], [x, y], [(x.shape, f32)]

    def body(self, scalars, ins, outs):
        outs[0][...] = ins[0][...] + ins[1][...]

    def plain(self):
        return [self.ins[0] + self.ins[1]]


class Pack:
    def __init__(self, backs, feed, wide):
        self.scalars, self.ins = [], [*backs, feed, wide]
        self.outs = [((16, feed.shape[1]), f32)]

    def body(self, scalars, ins, outs):
        width = outs[0].shape[1]
        value = ins[0][0:4, :]
        for one in ins[1:-2]:
            value = value + one[0:4, :]
        outs[0][0:4, :] = value
        outs[0][4:8, :] = ins[-2][0:4, :]
        count = ins[-1].shape[1] // width
        for j in range(count):
            outs[0][8 + j:9 + j, :] = ins[-1][:, j * width:(j + 1) * width]
        outs[0][8 + count:16, :] = jnp.zeros((8 - count, width), f32)


def stage_kernel(scalar_ref, *refs, ops, extra):
    ins = sum(len(op.ins) for op in ops)
    outs = refs[ins + extra:]
    at_s = at_i = at_o = 0
    for op in ops:
        op.body(
            [scalar_ref[at_s + i] for i in range(len(op.scalars))], refs[at_i:at_i + len(op.ins)],
            outs[at_o:at_o + len(op.outs)],
        )
        at_s, at_i, at_o = at_s + len(op.scalars), at_i + len(op.ins), at_o + len(op.outs)
    outs[at_o][...] = jnp.zeros(TOKEN.shape, f32)


def stage(ops, inside=True, after=(), through=()):
    plain = [op for op in ops if any(shape[-2] % 16 for shape, _ in op.outs)]
    done = {id(op): op.plain() for op in plain}
    run = [op for op in ops if id(op) not in done]
    spec = (lambda x: pl.BlockSpec(memory_space=pltpu.VMEM)) if inside else (lambda x: whole(x.shape))
    ins = [x for op in run for x in op.ins]
    outs = [o for op in run for o in op.outs]
    scalars = [x for op in run for x in op.scalars] or [jnp.zeros((), jnp.int32)]
    got = pl.pallas_call(
        functools.partial(stage_kernel, ops=run, extra=len(through) + len(after)),
        out_shape=tuple(pltpu.VMEM(shape, dtype) if inside else jax.ShapeDtypeStruct(shape, dtype) for shape, dtype in outs)
        + (TOKEN,) + tuple(jax.ShapeDtypeStruct(x.shape, x.dtype) for x in through),
        grid_spec=pltpu.PrefetchScalarGridSpec(
            num_scalar_prefetch=1,
            grid=(1,),
            in_specs=[spec(x) for x in ins] + [FREE] * (len(through) + len(after)),
            out_specs=[pl.BlockSpec(memory_space=pltpu.VMEM) if inside else whole(shape) for shape, _ in outs]
            + [whole(TOKEN.shape)] + [FREE] * len(through),
        ),
        input_output_aliases={1 + len(ins) + i: len(outs) + 1 + i for i in range(len(through))},
        compiler_params=pltpu.CompilerParams(vmem_limit_bytes=(16 if inside else 56) * 2**20),
        cost_estimate=cost(3),
        name="stage",
    )(jnp.stack(scalars).astype(jnp.int32), *ins, *through, *after)
    at, results = 0, []
    for op in ops:
        if id(op) in done:
            results.append(done[id(op)])
        else:
            results.append(list(got[at:at + len(op.outs)]))
            at += len(op.outs)
    return results, list(got[at + 1:]), got[at]


class Summing:
    def __init__(self, keeps, recvs, stage):
        bits = bits_of("items", 2)
        self.orders = (bits, bits[::-1])
        self.keeps, self.recvs = list(keeps), list(recvs)
        self.steps = [("planar", s) for s in range(stage, len(bits))] + [("across", None), ("total", None)]
        self.steps += [("up", s) for s in reversed(range(len(bits)))] + [("up", None)]
        self.at = 0
        self.mine = None

    @property
    def left(self):
        return len(self.steps) - self.at

    def op(self):
        kind, arg = self.steps[self.at]
        n = lax.axis_size("blk")
        if kind == "planar":
            return Fold([side_of("items", order[arg]) for order in self.orders], self.keeps, self.recvs)
        if kind == "across":
            return Across(lax.axis_index("blk"), n, self.keeps, self.recvs)
        if kind == "total":
            return Total(self.recvs)
        if self.mine is None:
            return Gathered(self.recvs)
        return Join(self.mine, self.recvs, arg is None)

    def take(self, outs):
        kind, arg = self.steps[self.at]
        self.at += 1
        n = lax.axis_size("blk")
        if kind == "planar":
            self.keeps = outs[2:]
            self.recvs = [swap(x, "items", order[arg]) for x, order in zip(outs, self.orders)]
        elif kind == "across":
            self.recvs = [outs[0]] + [swap(outs[m], "blk", m) for m in range(1, n)]
        elif kind == "total":
            self.recvs = [outs[0]] + [swap(outs[0], "blk", m) for m in range(1, n)]
        elif arg is None:
            self.mine = outs[0]
            self.recvs = swap(outs[0], "items", 1)
        else:
            self.mine = outs
            self.recvs = [swap(x, "items", order[arg]) for x, order in zip(outs, self.orders)]

    def sides(self, u):
        return [side_of("items", b) for b in self.orders[u]] + [side_of("blk", b) for b in reversed(bits_of("blk", 1))]

    def places(self):
        sides = [self.sides(u) for u in range(2)]
        masks = []
        for side in sides:
            mask = jnp.zeros((), jnp.int32)
            for one in side[1:]:
                mask = mask * 2 + one
            masks.append(mask)
        return jnp.stack([side_of("items", 1), sides[0][0], sides[1][0], *masks]).astype(jnp.int32)

    def ordered(self, x, u):
        sides = self.sides(u)
        index = jnp.zeros((1,), jnp.int32)
        for side in sides:
            index = index * 2 + side
        pieces = x.reshape(2 ** len(sides), -1, x.shape[-1])
        return jnp.take(pieces, jnp.arange(2 ** len(sides)) ^ index, axis=0).reshape(x.shape)

    def units(self, mine, other):
        core = side_of("items", 1)
        halves = [[self.ordered(x[u], u).astype(f32) for u in range(2)] for x in (mine, other)]
        low = [jnp.where(core == 0, halves[0][u], halves[1][u]) for u in range(2)]
        high = [jnp.where(core == 0, halves[1][u], halves[0][u]) for u in range(2)]
        return low + high


def gather_rows(x):
    z = lax.axis_index("blk")
    r1 = lax.ppermute(x, "blk", [(0, 1), (1, 2), (2, 3)])
    l1 = lax.ppermute(x, "blk", [(1, 0), (2, 1), (3, 2)])
    r2 = lax.ppermute(x, "blk", [(0, 2), (1, 3)])
    l2 = lax.ppermute(x, "blk", [(2, 0), (3, 1)])
    far = lax.ppermute(jnp.where(z == 2, r2, l2), "blk", [(2, 3), (1, 0)])
    return r1, l1, r2, l2, far


def local(
    tokens, cap_lengths, first_gain, first_shift, query_weight, query_bias, key_weight, value_weight, value_bias,
    out_weight, out_bias, second_gain, second_shift, inner_weight, inner_bias, outer_weight, outer_bias, cotangent,
):
    count, rows, width = tokens.shape
    hidden = inner_weight.shape[1]
    z = lax.axis_index("blk")
    z_arr = jnp.full((1,), z, jnp.int32)
    limits = 1 + IMG + cap_lengths
    key_count = min(-(-(1 + IMG + CAP) // STEP) * STEP, 4 * rows)
    vec = lambda v: v.reshape(1, -1)
    parts = gather_rows(tokens)
    cot_flat = cotangent.reshape(count * rows, width)
    cot_recv = swap(cot_flat, "items", 1)
    tok_all, norm_all, norm_own, q, k, v, ctx, lse = attend(
        limits, z_arr, tokens, parts,
        (query_weight, key_weight, value_weight, vec(first_gain), vec(first_shift), vec(query_bias), vec(value_bias)),
        key_count,
    )
    flat = lambda a: a.reshape(count * rows, width)
    core = side_of("items", 1)
    bit = core.reshape(1).astype(jnp.int32)
    out, attg, ff_send, ff_keep, norm2, branch, ctxg, small2, db1 = feed(
        bit, flat(tokens), flat(ctx), cot_flat,
        (out_weight, vec(out_bias), vec(second_gain), vec(second_shift), inner_weight, vec(inner_bias), outer_weight, vec(outer_bias)),
    )
    ctxg = ctxg.reshape(tokens.shape)
    ff_recv, norm2_recv = swap(ff_send, "items", 1), swap(norm2, "items", 1)
    back = functools.partial(
        attend_back, limits=limits, z=z_arr, own=tokens, tok=tok_all, q=q, k=k, v=v, ctxg=ctxg, lse=lse,
        weights=(query_weight, key_weight, value_weight, vec(first_gain), vec(first_shift)),
    )
    scatter = lambda x: lax.psum_scatter(x, "blk", scatter_dimension=0, tiled=True)
    bits = bits_of("items", 2)
    n_blk = lax.axis_size("blk")
    sides = jnp.stack([side_of("items", bits[0]), side_of("items", bits[-1])]).astype(jnp.int32)
    part0, *grads, small_a = back(0, after=(ff_send, norm2))
    ff = (ff_keep, ff_recv, norm2, norm2_recv, cot_flat, cot_recv)
    send0, send1, token = feed_weights(1 - sides, *ff, after=(small_a,))
    feed_recvs = [swap(send0, "items", bits[0]), swap(send1, "items", bits[-1])]
    *feed_keeps, part0, token = feed_weights(sides, *ff, after=(token,), through=(part0,))
    mine = [scatter(part0)]
    part1, *grads, small_b = back(1, into=grads, after=(token,))
    part2, *grads, small_c = back(2, into=grads)
    feed_sum = Summing(feed_keeps, feed_recvs, 1)
    small_op = Pack((small_a, small_b, small_c), small2, db1)
    while feed_sum.steps[feed_sum.at + 1][0] == "planar":
        (outs,), _, token = stage([feed_sum.op()], False)
        feed_sum.take(outs)
    (outs, (small,)), (part1,), token = stage([feed_sum.op(), small_op], False, through=(part1,), after=(small_c,))
    feed_sum.take(outs)
    mine.append(scatter(part1))
    ad = (limits, norm_all, norm_own, *grads, ctx, branch.reshape(tokens.shape))
    *sends, token = attend_weights(1 - bit, *ad, after=(token,))
    attend_recvs = [swap(x, "items", 1) for x in sends]
    *keeps, token = attend_weights(bit, *ad, after=(token,))
    attend_sum = Summing(keeps, attend_recvs, 0)
    small_bits = [("items", b) for b in bits_of("items", 1)] + [("blk", b) for b in bits_of("blk", 1)]
    small_recv = swap(small, *small_bits.pop(0))
    whole_slice = 2 ** (len(bits) + len(bits_of("blk", 1)) - 1) != PIECES
    placed, turn, ready = False, 0, {0: mine[0:1], 3: mine[1:2]}
    while feed_sum.left or attend_sum.left or small_recv is not None:
        users = [one for one in (feed_sum, attend_sum) if one.left]
        ops = [one.op() for one in users] + ([Add(small, small_recv)] if small_recv is not None else [])
        results, passed, token = stage(ops, turn > 0, after=(token, *ready.get(turn, ())), through=(part2,) if turn == 3 else ())
        mine += [scatter(x) for x in passed]
        turn += 1
        for one, outs in zip(users, results):
            one.take(outs)
        if small_recv is not None:
            small = results[-1][0]
            small_recv = swap(small, *small_bits.pop(0)) if small_bits else None
        if not feed_sum.left and not placed and feed_sum not in users and not whole_slice:
            grad_outer, grad_inner, token = feed_place(feed_sum.places(), feed_sum.mine, feed_sum.recvs, after=(token,))
            placed = True
    grad_tokens, token = close(tokens, attg.reshape(tokens.shape), mine, vec(first_gain), after=(token,))
    if not whole_slice:
        sum_q, sum_k, sum_v, sum_o = attend_place(attend_sum.places(), attend_sum.mine, attend_sum.recvs, after=(token,))
    else:
        feed_units = feed_sum.units(feed_sum.mine, feed_sum.recvs)
        grad_outer = jnp.concatenate([u[:width] for u in feed_units], 0)
        grad_inner = jnp.concatenate([u[width:] for u in feed_units], 1)
        sum_q, sum_k, sum_v, sum_o = attend_sum.units(attend_sum.mine, attend_sum.recvs)
    return (
        out.reshape(tokens.shape), grad_tokens,
        small[0], small[1],
        sum_q, small[2], sum_k, sum_v, small[3],
        sum_o, small[6],
        small[4], small[5],
        grad_inner, small[8:8 + hidden // width].reshape(hidden), grad_outer, small[7],
    )


def solution(mesh):
    row = P("items", "blk", None)
    return jax.shard_map(
        local,
        mesh=mesh,
        in_specs=(row, P("items")) + (P(),) * 15 + (row,),
        out_specs=(row, row) + (P(),) * 15,
        check_vma=False,
    )
```

```python
import functools

import jax
import jax.numpy as jnp
from jax import lax
from jax.experimental import pallas as pl
from jax.experimental.pallas import tpu as pltpu
from jax.sharding import PartitionSpec as P

HD = 64
IMG = 197
CAP = 512
STEP = 256
FF_STEP = 512
norm_eps = 1e-05
masked_score = -1e30
f32 = jnp.float32
bf16 = jnp.bfloat16
TOKEN = jax.ShapeDtypeStruct((8, 128), f32)
FREE = pl.BlockSpec(memory_space=pl.ANY)


def dot_nn(a, b):
    return lax.dot_general(a, b, (((1,), (0,)), ((), ())), preferred_element_type=f32)


def dot_nt(a, b):
    return lax.dot_general(a, b, (((1,), (1,)), ((), ())), preferred_element_type=f32)


def dot_tn(a, b):
    return lax.dot_general(a, b, (((0,), (0,)), ((), ())), preferred_element_type=f32)


def norm_core(rows):
    average = jnp.mean(rows, axis=-1, keepdims=True)
    centred = rows - average
    spread = jnp.mean(centred * centred, axis=-1, keepdims=True)
    scale = lax.rsqrt(spread + norm_eps)
    return centred * scale, scale


def norm_back(unit, scale, gain, grad):
    weighted = grad * gain
    first = jnp.mean(weighted, axis=-1, keepdims=True)
    second = jnp.mean(weighted * unit, axis=-1, keepdims=True)
    return scale * (weighted - first - unit * second)


def normal_cdf_pdf(v):
    size = jnp.abs(v) * 0.7071067811865476
    t = 1.0 / (1.0 + 0.3275911 * size)
    poly = t * (0.254829592 + t * (-0.284496736 + t * (1.421413741 + t * (-1.453152027 + t * 1.061405429))))
    bell = jnp.exp(-0.5 * v * v)
    tail = 0.5 * poly * bell
    return jnp.where(v >= 0, 1.0 - tail, tail), 0.3989422804014327 * bell


def cost(us):
    return pl.CostEstimate(flops=int(us * 5e+08), bytes_accessed=int(us * 1.5e+06), transcendentals=0)


def key_steps(limit, key_count, body):
    steps = key_count // STEP
    for n in range(1, steps + 1):
        low, high = (n - 1) * STEP, n * STEP
        cond = limit > low if n == steps else (limit <= high if n == 1 else (limit > low) & (limit <= high))
        pl.when(cond)(functools.partial(body, high))


def attend_kernel(
    limit_ref, z_ref,
    own_ref, r1_ref, l1_ref, r2_ref, l2_ref, far_ref,
    wq_ref, wk_ref, wv_ref, gain_ref, shift_ref, bq_ref, bv_ref,
    tok_ref, norm_ref, ownnorm_ref, q_ref, k_ref, v_ref, ctx_ref, lse_ref, logs_ref,
):
    item = pl.program_id(0)
    limit = limit_ref[item]
    z = z_ref[0]
    rows, width = own_ref.shape
    key_count = tok_ref.shape[0]
    tail = key_count - 3 * rows

    def place(src, at, cond):
        @pl.when(cond & (at < 3))
        def _():
            tok_ref[pl.ds(pl.multiple_of(at * rows, 16), rows), :] = src[...]

        @pl.when(cond & (at == 3))
        def _():
            tok_ref[3 * rows:key_count, :] = src[0:tail, :]

    place(own_ref, z, z >= 0)
    place(r1_ref, z - 1, z >= 1)
    place(l1_ref, z + 1, z <= 2)
    place(r2_ref, z - 2, z >= 2)
    place(l2_ref, z + 2, z <= 1)
    place(far_ref, 0, z == 3)
    place(far_ref, 3, z == 0)
    gain, shift = gain_ref[...], shift_ref[...]

    unit, _ = norm_core(own_ref[...].astype(f32))
    own_norm = (unit * gain + shift).astype(bf16)
    ownnorm_ref[...] = own_norm
    query = (dot_nn(own_norm, wq_ref[...]) + bq_ref[...]).astype(bf16)
    q_ref[...] = query * jnp.asarray(HD ** -0.5, bf16)

    def project(c, _):
        here = pl.ds(pl.multiple_of(c * STEP, STEP), STEP)
        unit, _ = norm_core(tok_ref[here, :].astype(f32))
        normed = (unit * gain + shift).astype(bf16)
        norm_ref[here, :] = normed
        k_ref[here, :] = dot_nn(normed, wk_ref[...]).astype(bf16)
        v_ref[here, :] = (dot_nn(normed, wv_ref[...]) + bv_ref[...]).astype(bf16)
        return 0

    lax.fori_loop(0, (limit + STEP - 1) // STEP, project, 0)

    def part(high):
        bias = jnp.where(lax.broadcasted_iota(jnp.int32, (1, high), 1) < limit, 0.0, masked_score)
        lane = lax.broadcasted_iota(jnp.int32, (rows, 2 * HD), 1)

        def pair(p):
            cols = pl.ds(pl.multiple_of(p * 2 * HD, 2 * HD), 2 * HD)
            q_pair = q_ref[:, cols]
            k_pair = k_ref[0:high, cols]
            v_pair = v_ref[0:high, cols]
            second = lane >= HD
            zero = jnp.zeros_like(q_pair)
            scores = [dot_nt(jnp.where(second == (h == 1), q_pair, zero), k_pair) + bias for h in range(2)]
            outs = []
            for h in range(2):
                top = jnp.max(scores[h], axis=1, keepdims=True)
                shifted = jnp.exp(scores[h] - top)
                total = jnp.sum(shifted, axis=1, keepdims=True)
                probs = (shifted * (1.0 / total)).astype(bf16)
                outs.append(dot_nn(probs, v_pair))
                logs_ref[...] = jnp.where(lane == 2 * p + h, top + jnp.log(total), logs_ref[...])
            ctx_ref[:, cols] = jnp.where(second, outs[1], outs[0]).astype(bf16)

        def pairs(i, _):
            pair(2 * i)
            pair(2 * i + 1)
            return 0

        lax.fori_loop(0, width // (4 * HD), pairs, 0)

    key_steps(limit, key_count, part)
    lse_ref[...] = logs_ref[...].T[0:lse_ref.shape[0], :]


def whole(shape):
    return pl.BlockSpec(shape, lambda *_: (0,) * len(shape))


def attend(limits, z, own, parts, weights, key_count):
    count, rows, width = own.shape
    row_spec = pl.BlockSpec((None, rows, width), lambda i, *_: (i, 0, 0))
    key_spec = pl.BlockSpec((None, key_count, width), lambda i, *_: (i, 0, 0))
    lse_spec = pl.BlockSpec((None, 16, rows), lambda i, *_: (i, 0, 0))
    wq, wk, wv, gain, shift, bq, bv = weights
    vec = whole((1, width))
    mat = whole((width, width))
    row = jax.ShapeDtypeStruct((count, rows, width), bf16)
    key = jax.ShapeDtypeStruct((count, key_count, width), bf16)
    return pl.pallas_call(
        attend_kernel,
        out_shape=(key, key, row, row, key, key, row, jax.ShapeDtypeStruct((count, 16, rows), f32)),
        grid_spec=pltpu.PrefetchScalarGridSpec(
            num_scalar_prefetch=2,
            grid=(count,),
            in_specs=[row_spec] * 6 + [mat] * 3 + [vec] * 4,
            out_specs=[key_spec, key_spec, row_spec, row_spec, key_spec, key_spec, row_spec, lse_spec],
            scratch_shapes=[pltpu.VMEM((rows, 2 * HD), f32)],
        ),
        compiler_params=pltpu.CompilerParams(vmem_limit_bytes=56 * 2**20),
        cost_estimate=cost(28),
        name="attend",
    )(limits, z, own, *parts, wq, wk, wv, gain, shift, bq, bv)


def feed_kernel(
    bit_ref, tok_ref, ctx_ref, cot_ref, wo_ref, bo_ref, gain_ref, shift_ref, w1_ref, b1_ref, w2_ref, b2_ref,
    out_ref, attg_ref, send_ref, keep_ref, norm_ref, branch_ref, ctxg_ref, small_ref, db1_ref,
    att_acc, grad_acc, unit_keep, scale_keep,
):
    step = pl.program_id(0)
    last = pl.num_programs(0) - 1

    @pl.when(step == 0)
    def _():
        attended = tok_ref[...].astype(f32) + (dot_nn(ctx_ref[...], wo_ref[...]) + bo_ref[...])
        unit, scale = norm_core(attended)
        norm_ref[...] = (unit * gain_ref[...] + shift_ref[...]).astype(bf16)
        unit_keep[...] = unit
        scale_keep[...] = jnp.broadcast_to(scale, scale_keep.shape)
        att_acc[...] = attended + b2_ref[...]
        grad_acc[...] = jnp.zeros_like(grad_acc)

    cot = cot_ref[...]
    inner = dot_nn(norm_ref[...], w1_ref[...]) + b1_ref[...]
    cdf, pdf = normal_cdf_pdf(inner)
    act = (inner * cdf).astype(bf16)
    act_grad = dot_nt(cot, w2_ref[...])
    pre = ((cdf + inner * pdf) * act_grad).astype(bf16)

    @pl.when(step <= last // 2)
    def _():
        send_ref[0] = act
        send_ref[1] = pre

    @pl.when(step > last // 2)
    def _():
        keep_ref[0] = act
        keep_ref[1] = pre

    db1_ref[...] = jnp.sum(pre.astype(f32), axis=0, keepdims=True)
    att_acc[...] += dot_nn(act, w2_ref[...])
    grad_acc[...] += dot_nt(pre, w1_ref[...])

    @pl.when(step == last)
    def _():
        out_ref[...] = att_acc[...].astype(bf16)
        unit, grad = unit_keep[...], grad_acc[...]
        cot_wide = cot_ref[...].astype(f32)
        attended_grad = cot_wide + norm_back(unit, scale_keep[:, 0:1], gain_ref[...], grad)
        attg_ref[...] = attended_grad
        branch = attended_grad.astype(bf16)
        branch_ref[...] = branch
        ctxg_ref[...] = dot_nt(branch, wo_ref[...]).astype(bf16)
        small_ref[0:1, :] = jnp.sum(grad * unit, axis=0, keepdims=True)
        small_ref[1:2, :] = jnp.sum(grad, axis=0, keepdims=True)
        small_ref[2:3, :] = jnp.sum(branch.astype(f32), axis=0, keepdims=True)
        small_ref[3:4, :] = jnp.sum(cot_wide, axis=0, keepdims=True)
        small_ref[4:8, :] = jnp.zeros((4, small_ref.shape[1]), f32)


def feed(bit, tok, ctx, cot, weights):
    wo, bo, gain, shift, w1, b1, w2, b2 = weights
    rows, width = tok.shape
    hidden = w1.shape[1]
    row = whole((rows, width))
    vec = whole((1, width))
    half = hidden // FF_STEP // 2

    def chunk(j, bit_ref):
        return jnp.where(j < half, (1 - bit_ref[0]) * half + j, bit_ref[0] * half + j - half)

    pair = jax.ShapeDtypeStruct((2, rows, hidden // 2), bf16)
    return pl.pallas_call(
        feed_kernel,
        out_shape=(
            jax.ShapeDtypeStruct((rows, width), bf16),
            jax.ShapeDtypeStruct((rows, width), f32),
            pair,
            pair,
            jax.ShapeDtypeStruct((rows, width), bf16),
            jax.ShapeDtypeStruct((rows, width), bf16),
            jax.ShapeDtypeStruct((rows, width), bf16),
            jax.ShapeDtypeStruct((8, width), f32),
            jax.ShapeDtypeStruct((1, hidden), f32),
        ),
        grid_spec=pltpu.PrefetchScalarGridSpec(
            num_scalar_prefetch=1,
            grid=(2 * half,),
            in_specs=[
                row, row, row, whole((width, width)), vec, vec, vec,
                pl.BlockSpec((width, FF_STEP), lambda j, b: (0, chunk(j, b))),
                pl.BlockSpec((1, FF_STEP), lambda j, b: (0, chunk(j, b))),
                pl.BlockSpec((FF_STEP, width), lambda j, b: (chunk(j, b), 0)),
                vec,
            ],
            out_specs=[
                row, row,
                pl.BlockSpec((2, rows, FF_STEP), lambda j, b: (0, 0, jnp.minimum(j, half - 1))),
                pl.BlockSpec((2, rows, FF_STEP), lambda j, b: (0, 0, jnp.maximum(j - half, 0))),
                row, row, row, whole((8, width)),
                pl.BlockSpec((1, FF_STEP), lambda j, b: (0, chunk(j, b))),
            ],
            scratch_shapes=[
                pltpu.VMEM((rows, width), f32),
                pltpu.VMEM((rows, width), f32),
                pltpu.VMEM((rows, width), f32),
                pltpu.VMEM((rows, 128), f32),
            ],
        ),
        compiler_params=pltpu.CompilerParams(vmem_limit_bytes=56 * 2**20),
        cost_estimate=cost(29),
        name="feed",
    )(bit, tok, ctx, cot, wo, bo, gain, shift, w1, b1, w2, b2)


def attend_back_kernel(
    limit_ref, z_ref,
    own_ref, q_ref, k_ref, v_ref, ctxg_ref, lse_ref, gain_ref, shift_ref,
    tok_any, wq_any, wk_any, wv_any, *rest, item,
):
    part_ref, dq_ref, dk_ref, dv_ref, small_ref, tok_ref, wq_ref, wk_ref, wv_ref, sems = rest[-10:]
    fetch = [
        pltpu.make_async_copy(src, dst, sems.at[i])
        for i, (src, dst) in enumerate((
            (tok_any.at[item], tok_ref), (wk_any, wk_ref), (wv_any, wv_ref), (wq_any, wq_ref)))
    ]
    for one in fetch:
        one.start()
    limit = limit_ref[0]
    z = z_ref[0]
    rows, width = own_ref.shape
    key_count = tok_ref.shape[0]

    def part(high):
        bias = jnp.where(lax.broadcasted_iota(jnp.int32, (high, 1), 0) < limit, 0.0, masked_score)
        lane = lax.broadcasted_iota(jnp.int32, (rows, 2 * HD), 1)

        lane_keys = lax.broadcasted_iota(jnp.int32, (high, 2 * HD), 1)

        def pair(p):
            cols = pl.ds(pl.multiple_of(p * 2 * HD, 2 * HD), 2 * HD)
            q_pair = q_ref[:, cols]
            k_pair = k_ref[0:high, cols]
            v_pair = v_ref[0:high, cols]
            g_pair = ctxg_ref[:, cols]
            k_turned = k_pair.T
            zero = jnp.zeros_like(q_pair)
            pre = []
            for h in range(2):
                mine = (lane >= HD) == (h == 1)
                pre.append((
                    dot_nt(k_pair, jnp.where(mine, q_pair, zero)) + bias,
                    dot_nt(v_pair, jnp.where(mine, g_pair, zero)),
                ))
            dqs, dks, dvs = [], [], []
            for h, (scores, prob_grad) in enumerate(pre):
                probs = jnp.exp(scores - lse_ref[pl.ds(2 * p + h, 1), :])
                delta = jnp.sum(probs * prob_grad, axis=0, keepdims=True)
                score_grad = (probs * (prob_grad - delta)).astype(bf16)
                dvs.append(dot_nn(probs.astype(bf16), g_pair))
                dks.append(dot_nn(score_grad, q_pair))
                dqs.append(dot_nn(k_turned[h * HD:(h + 1) * HD, :], score_grad))
            dq_ref[:, cols] = (jnp.concatenate(dqs, axis=0).T * (HD ** -0.5)).astype(bf16)
            dk_ref[0:high, cols] = jnp.where(lane_keys >= HD, dks[1], dks[0]).astype(bf16)
            dv_ref[0:high, cols] = jnp.where(lane_keys >= HD, dvs[1], dvs[0]).astype(bf16)

        def pairs(i, _):
            pair(2 * i)
            pair(2 * i + 1)
            return 0

        lax.fori_loop(0, width // (4 * HD), pairs, 0)

    key_steps(limit, key_count, part)

    for one in fetch:
        one.wait()
    small_ref[...] = jnp.zeros_like(small_ref)

    def inward(c, _):
        here = pl.ds(pl.multiple_of(c * STEP, STEP), STEP)
        unit, _ = norm_core(tok_ref[here, :].astype(f32))
        dk, dv = dk_ref[here, :], dv_ref[here, :]
        grad = dot_nt(dk, wk_ref[...]) + dot_nt(dv, wv_ref[...])
        small_ref[0:1, :] += jnp.sum(grad * unit, axis=0, keepdims=True)
        small_ref[1:2, :] += jnp.sum(grad, axis=0, keepdims=True)
        small_ref[3:4, :] += jnp.sum(dv.astype(f32), axis=0, keepdims=True)
        part_ref[here, :] = grad.astype(bf16)
        return 0

    def outward(c, _):
        part_ref[pl.ds(pl.multiple_of(c * STEP, STEP), STEP), :] = jnp.zeros((STEP, width), bf16)
        return 0

    used = (limit + STEP - 1) // STEP
    lax.fori_loop(0, used, inward, 0)
    lax.fori_loop(used, key_count // STEP, outward, 0)
    part_ref[key_count:, :] = jnp.zeros((part_ref.shape[0] - key_count, width), bf16)

    unit, _ = norm_core(own_ref[...].astype(f32))
    dq = dq_ref[...]
    grad = dot_nt(dq, wq_ref[...])
    small_ref[0:1, :] += jnp.sum(grad * unit, axis=0, keepdims=True)
    small_ref[1:2, :] += jnp.sum(grad, axis=0, keepdims=True)
    small_ref[2:3, :] = jnp.sum(dq.astype(f32), axis=0, keepdims=True)
    here = pl.ds(pl.multiple_of(z * rows, 16), rows)
    part_ref[here, :] = (part_ref[here, :].astype(f32) + grad).astype(bf16)


def attend_back(item, limits, z, own, tok, q, k, v, ctxg, lse, weights, into=None, after=()):
    count, rows, width = own.shape
    key_count = tok.shape[1]
    wq, wk, wv, gain, shift = weights
    row_spec = pl.BlockSpec((None, rows, width), lambda i, *_: (item, 0, 0))
    key_spec = pl.BlockSpec((None, key_count, width), lambda i, *_: (item, 0, 0))
    lse_spec = pl.BlockSpec((None, 16, rows), lambda i, *_: (item, 0, 0))
    vec, free = whole((1, width)), FREE
    into = () if into is None else tuple(into)
    return pl.pallas_call(
        functools.partial(attend_back_kernel, item=item),
        out_shape=(
            jax.ShapeDtypeStruct((4 * rows, width), bf16),
            jax.ShapeDtypeStruct((count, rows, width), bf16),
            jax.ShapeDtypeStruct((count, key_count, width), bf16),
            jax.ShapeDtypeStruct((count, key_count, width), bf16),
            jax.ShapeDtypeStruct((8, width), f32),
        ),
        grid_spec=pltpu.PrefetchScalarGridSpec(
            num_scalar_prefetch=2,
            grid=(1,),
            in_specs=[row_spec, row_spec, key_spec, key_spec, row_spec, lse_spec, vec, vec]
            + [free] * (4 + len(into) + len(after)),
            out_specs=[whole((4 * rows, width)), row_spec, key_spec, key_spec, whole((8, width))],
            scratch_shapes=[pltpu.VMEM((key_count, width), bf16)]
            + [pltpu.VMEM((width, width), bf16)] * 3 + [pltpu.SemaphoreType.DMA((4,))],
        ),
        input_output_aliases={14 + i: 1 + i for i in range(len(into))},
        compiler_params=pltpu.CompilerParams(vmem_limit_bytes=56 * 2**20),
        cost_estimate=cost(13),
        name="attend_back",
    )(limits[item:item + 1], z, own, q, k, v, ctxg, lse, gain, shift, tok, wq, wk, wv, *into, *after)


def feed_weight_kernel(kind_ref, ff_ref, recv_ref, norm_ref, normr_ref, cot_ref, cotr_ref, *rest):
    outs = rest[-5:-1]
    rest[-1][...] = jnp.zeros(TOKEN.shape, f32)
    step = pl.program_id(0)
    kind = kind_ref[step]

    def put(value):
        for i, out in enumerate(outs):
            @pl.when(step == i)
            def _():
                out[...] = value.astype(out.dtype)

    @pl.when(kind == 0)
    def _():
        put(dot_tn(ff_ref[...], cot_ref[...]) + dot_tn(recv_ref[...], cotr_ref[...]))

    @pl.when(kind != 0)
    def _():
        put(dot_tn(norm_ref[...], ff_ref[...]) + dot_tn(normr_ref[...], recv_ref[...]))


def feed_weights(kinds, ff, recv, norm, norm_recv, cot, cot_recv, after=()):
    rows, width = cot.shape
    row = whole((rows, width))
    unit = pl.BlockSpec((None, rows, width), lambda s, kind_ref: (kind_ref[s], 0, s % 2))
    mat = whole((width, width))
    return pl.pallas_call(
        feed_weight_kernel,
        out_shape=(jax.ShapeDtypeStruct((width, width), bf16),) * 4 + (TOKEN,),
        grid_spec=pltpu.PrefetchScalarGridSpec(
            num_scalar_prefetch=1,
            grid=(4,),
            in_specs=[unit, unit, row, row, row, row] + [FREE] * len(after),
            out_specs=[mat] * 4 + [whole(TOKEN.shape)],
        ),
        compiler_params=pltpu.CompilerParams(vmem_limit_bytes=56 * 2**20),
        cost_estimate=cost(13),
        name="feed_weights",
    )(kinds, ff, recv, norm, norm_recv, cot, cot_recv, *after)


def split_rows(small):
    high = small.astype(bf16)
    low = (small - high.astype(f32)).astype(bf16)
    return high, low, high.astype(f32) + low.astype(f32)


def attend_weight_kernel(
    half_ref, limit_ref, norm_ref, own_ref, dq_ref, dk_ref, dv_ref, ctx_ref, branch_ref, *rest, small,
):
    acc_ref = rest[-1]
    outs = rest[-4:-2]
    rest[-2][...] = jnp.zeros(TOKEN.shape, f32)
    step = pl.program_id(0)
    item = step % 3
    unit = 2 * half_ref[0] + step // 3
    key_count, width = norm_ref.shape

    if small:
        @pl.when(step == 0)
        def _():
            high, low, _ = split_rows(rest[0][...])
            count = high.shape[0]
            outs[0][width:width + count, :] = high
            outs[0][width + count:width + 2 * count, :] = low

    def put(value):
        @pl.when(item == 0)
        def _():
            acc_ref[...] = value

        @pl.when(item == 1)
        def _():
            acc_ref[...] += value

        for i in range(2):
            @pl.when(step == 2 + 3 * i)
            def _():
                outs[i][0:width, :] = (acc_ref[...] + value).astype(bf16)

    def keys(grad):
        key_steps(limit_ref[item], key_count, lambda high: put(dot_tn(norm_ref[0:high, :], grad[0:high, :])))

    pl.when(unit == 0)(lambda: put(dot_tn(own_ref[...], dq_ref[...])))
    pl.when(unit == 1)(lambda: keys(dk_ref))
    pl.when(unit == 2)(lambda: keys(dv_ref))
    pl.when(unit == 3)(lambda: put(dot_tn(ctx_ref[...], branch_ref[...])))


def attend_weights(half, limits, norm, own, dq, dk, dv, ctx, branch, small=None, after=()):
    count, rows, width = own.shape
    key_count = norm.shape[1]

    def by_item(size, *units):
        def at(s, half_ref, _):
            unit = 2 * half_ref[0] + s // 3
            used = unit == units[0]
            for one in units[1:]:
                used = used | (unit == one)
            return jnp.where(used, s % 3, 0), 0, 0
        return pl.BlockSpec((None, size, width), at)

    extra = 0 if small is None else 2 * small.shape[0]
    smalls = () if small is None else (small,)
    shapes = [(width + extra, width), (width, width)]
    return pl.pallas_call(
        functools.partial(attend_weight_kernel, small=small is not None),
        out_shape=tuple(jax.ShapeDtypeStruct(x, bf16) for x in shapes) + (TOKEN,),
        grid_spec=pltpu.PrefetchScalarGridSpec(
            num_scalar_prefetch=2,
            grid=(6,),
            in_specs=[
                by_item(key_count, 1, 2), by_item(rows, 0), by_item(rows, 0), by_item(key_count, 1), by_item(key_count, 2),
                by_item(rows, 3), by_item(rows, 3),
            ] + [whole(x.shape) for x in smalls] + [FREE] * len(after),
            out_specs=[whole(x) for x in shapes] + [whole(TOKEN.shape)],
            scratch_shapes=[pltpu.VMEM((width, width), f32)],
        ),
        compiler_params=pltpu.CompilerParams(vmem_limit_bytes=56 * 2**20),
        cost_estimate=cost(9),
        name="attend_weights",
    )(half, limits, norm, own, dq, dk, dv, ctx, branch, *smalls, *after)


def close_kernel(tok_ref, attg_ref, m0_ref, m1_ref, m2_ref, gain_ref, *rest):
    out_ref = rest[-2]
    rest[-1][...] = jnp.zeros(TOKEN.shape, f32)
    for i, part_ref in enumerate((m0_ref, m1_ref, m2_ref)):
        @pl.when(pl.program_id(0) == i)
        def _():
            unit, scale = norm_core(tok_ref[...].astype(f32))
            grad = part_ref[...].astype(f32)
            out_ref[...] = (attg_ref[...] + norm_back(unit, scale, gain_ref[...], grad)).astype(bf16)


def close(tok, attg, parts, gain, after=()):
    count, rows, width = tok.shape
    row = pl.BlockSpec((None, rows, width), lambda i: (i, 0, 0))
    return pl.pallas_call(
        close_kernel,
        out_shape=(jax.ShapeDtypeStruct((count, rows, width), bf16), TOKEN),
        grid=(count,),
        in_specs=[row, row] + [whole((rows, width))] * 3 + [whole((1, width))]
        + [FREE] * len(after),
        out_specs=[row, whole(TOKEN.shape)],
        compiler_params=pltpu.CompilerParams(vmem_limit_bytes=56 * 2**20),
        cost_estimate=cost(4),
        name="close",
    )(tok, attg, *parts, gain, *after)


def place_pieces(src, dst, mask, pieces):
    size = src.shape[0] // pieces
    for i in range(pieces):
        at = pl.multiple_of(jnp.bitwise_xor(mask, i) * size, 8)
        dst[pl.ds(at, size), :] = src[i * size:(i + 1) * size, :].astype(f32)


def feed_place_kernel(at_ref, mine_ref, other_ref, *rest):
    outer_ref, inner_ref = rest[-3:-1]
    rest[-1][...] = jnp.zeros(TOKEN.shape, f32)
    step = pl.program_id(0)
    unit = step % 4
    core, mask = at_ref[0], at_ref[3 + unit % 2]

    def copy(dst):
        @pl.when(unit // 2 == core)
        def _():
            place_pieces(mine_ref, dst, mask, PIECES)

        @pl.when(unit // 2 != core)
        def _():
            place_pieces(other_ref, dst, mask, PIECES)

    pl.when(step < 4)(lambda: copy(outer_ref))
    pl.when(step >= 4)(lambda: copy(inner_ref))


PIECES = 8


def feed_place(at, mine, other, after=()):
    width = mine.shape[-1]

    def source(which):
        def index(s, at_ref):
            low = jnp.bitwise_xor(at_ref[0], which) == 0
            in_low = s % 4 < 2
            held = jnp.where(low, jnp.where(s < 4, 4, 5), s // 4 * 4 + 2)
            t = jnp.where(low == in_low, s, held)
            return t % 2, jnp.bitwise_xor(t // 4, at_ref[1 + t % 2]), 0
        return pl.BlockSpec((None, width, width), index)

    return pl.pallas_call(
        feed_place_kernel,
        out_shape=(jax.ShapeDtypeStruct((4 * width, width), f32), jax.ShapeDtypeStruct((width, 4 * width), f32), TOKEN),
        grid_spec=pltpu.PrefetchScalarGridSpec(
            num_scalar_prefetch=1,
            grid=(8,),
            in_specs=[source(0), source(1)] + [FREE] * len(after),
            out_specs=[
                pl.BlockSpec((width, width), lambda s, _: (jnp.minimum(s, 3), 0)),
                pl.BlockSpec((width, width), lambda s, _: (0, jnp.maximum(s - 4, 0))),
                whole(TOKEN.shape),
            ],
        ),
        compiler_params=pltpu.CompilerParams(vmem_limit_bytes=24 * 2**20),
        cost_estimate=cost(0.1),
        name="feed_place",
    )(at, mine, other, *after)


def attend_place_kernel(at_ref, mine0_ref, mine1_ref, other0_ref, other1_ref, *rest):
    out_refs = rest[-5:-1]
    rest[-1][...] = jnp.zeros(TOKEN.shape, f32)
    core = at_ref[0]
    half = mine0_ref.shape[0] // 2
    for unit, dst in enumerate(out_refs):
        u = unit % 2
        for first in range(2):
            to = dst.at[pl.ds(pl.multiple_of(jnp.bitwise_xor(at_ref[1 + u], first) * half, 8), half), :]
            rows = slice(first * half, (first + 1) * half)
            for here, src in ((core == unit // 2, (mine0_ref, mine1_ref)[u]), (core != unit // 2, (other0_ref, other1_ref)[u])):
                @pl.when(here)
                def _():
                    place_pieces(src.at[rows, :], to, at_ref[3 + u], PIECES)


def attend_place(at, mine, other, after=()):
    width = mine[0].shape[-1]
    return pl.pallas_call(
        attend_place_kernel,
        out_shape=(jax.ShapeDtypeStruct((width, width), f32),) * 4 + (TOKEN,),
        grid_spec=pltpu.PrefetchScalarGridSpec(
            num_scalar_prefetch=1,
            grid=(1,),
            in_specs=[whole(mine[0].shape)] * 4 + [FREE] * len(after),
            out_specs=[whole((width, width))] * 4 + [whole(TOKEN.shape)],
        ),
        compiler_params=pltpu.CompilerParams(vmem_limit_bytes=40 * 2**20),
        cost_estimate=cost(0.1),
        name="attend_place",
    )(at, *mine, *other, *after)


def swap(x, axis, bit):
    return lax.ppermute(x, axis, [(i, i ^ bit) for i in range(lax.axis_size(axis))])


def side_of(axis, bit):
    return (lax.axis_index(axis) // bit) % 2


def bits_of(axis, bit):
    bits = []
    while bit < lax.axis_size(axis):
        bits.append(bit)
        bit *= 2
    return bits


def unite(small, got, at, count):
    high, low = got
    return split_rows(small)[2] + (high[at:at + count, :].astype(f32) + low[at + (low is high) * count:, :][0:count].astype(f32))


class Fold:
    def __init__(self, sides, keeps, recvs, small=None):
        self.scalars, self.ins = list(sides), [*keeps, *recvs]
        half, width = keeps[0].shape[0] // 2, keeps[0].shape[1]
        self.half, self.small = half, small is not None
        self.outs = [((half, width), bf16)] * 4
        if self.small:
            self.ins.append(small)
            self.outs = [((half + 2 * small.shape[0], width), bf16)] + self.outs[1:] + [(small.shape, f32)]

    def body(self, scalars, ins, outs):
        half = self.half
        for u in range(2):
            for k, side in ((u, 1 - scalars[u]), (2 + u, scalars[u])):
                at = pl.ds(pl.multiple_of(side * half, 16), half)
                outs[k][0:half, :] = (ins[u][at, :].astype(f32) + ins[2 + u][at, :].astype(f32)).astype(bf16)
        if self.small:
            n = ins[4].shape[0]
            value = unite(ins[4][...], (ins[2], ins[2]), 2 * half, n)
            outs[4][...] = value
            high, low, _ = split_rows(value)
            outs[0][half:half + n, :] = high
            outs[0][half + n:half + 2 * n, :] = low

    def plain(self):
        half, ins = self.half, self.ins
        sums = [ins[u].astype(f32) + ins[2 + u][0:2 * half].astype(f32) for u in range(2)]
        cut = lambda x, side: lax.dynamic_slice_in_dim(x, side * half, half, 0).astype(bf16)
        outs = [cut(x, 1 - side) for x, side in zip(sums, self.scalars)] + [cut(x, side) for x, side in zip(sums, self.scalars)]
        if self.small:
            value = unite(ins[4], (ins[2], ins[2]), 2 * half, ins[4].shape[0])
            high, low, _ = split_rows(value)
            outs = [jnp.concatenate([outs[0], high, low], 0)] + outs[1:] + [value]
        return outs


class Across:
    def __init__(self, z, n, keeps, recvs, small=None):
        self.scalars, self.ins, self.n = [z], [*keeps, *recvs], n
        size, width = keeps[0].shape[0] // n, keeps[0].shape[1]
        self.size, self.small = size, small is not None
        self.outs = [((2, size, width), bf16)] * n
        if self.small:
            self.ins.append(small)
            self.outs = [((2, size + small.shape[0], width), bf16)] * n + [(small.shape, f32)]

    def body(self, scalars, ins, outs):
        size, n = self.size, self.n
        for m in range(n):
            at = pl.ds(pl.multiple_of(jnp.bitwise_xor(scalars[0], m) * size, 16), size)
            for u in range(2):
                outs[m][u, 0:size, :] = (ins[u][at, :].astype(f32) + ins[2 + u][at, :].astype(f32)).astype(bf16)
        if self.small:
            rows = ins[4].shape[0]
            value = unite(ins[4][...], (ins[2], ins[2]), n * size, rows)
            outs[n][...] = value
            high, low, _ = split_rows(value)
            for m in range(n):
                outs[m][0, size:size + rows, :] = high
                outs[m][1, size:size + rows, :] = low

    def plain(self):
        size, n, ins = self.size, self.n, self.ins
        sums = jnp.stack([ins[u].astype(f32) + ins[2 + u][0:n * size].astype(f32) for u in range(2)])
        cuts = [lax.dynamic_slice_in_dim(sums, (self.scalars[0] ^ m) * size, size, 1).astype(bf16) for m in range(n)]
        if self.small:
            value = unite(ins[4], (ins[2], ins[2]), n * size, ins[4].shape[0])
            both = jnp.stack(split_rows(value)[:2])
            cuts = [jnp.concatenate([c, both], 1) for c in cuts] + [value]
        return cuts


class Total:
    def __init__(self, pieces, small=0):
        self.scalars, self.ins, self.small = [], list(pieces), small
        count, rows, width = pieces[0].shape
        self.size = rows - small
        self.outs = [((count, self.size, width), bf16)] + ([((small, width), f32)] if small else [])

    def sums(self, ins):
        value = ins[0][:, 0:self.size, :].astype(f32)
        for one in ins[1:]:
            value = value + one[:, 0:self.size, :].astype(f32)
        outs = [value.astype(bf16)]
        if self.small:
            parts = [x[0, self.size:, :].astype(f32) + x[1, self.size:, :].astype(f32) for x in ins]
            while len(parts) > 1:
                parts = [a + b for a, b in zip(parts[::2], parts[1::2])]
            outs.append(parts[0])
        return outs

    def body(self, scalars, ins, outs):
        for out, value in zip(outs, self.sums(ins)):
            out[...] = value

    def plain(self):
        return self.sums(self.ins)


class Gathered:
    def __init__(self, pieces):
        self.scalars, self.ins = [], list(pieces)
        _, size, width = pieces[0].shape
        self.outs = [((len(pieces) * size, width), bf16)] * 2

    def body(self, scalars, ins, outs):
        size = ins[0].shape[1]
        for m, piece in enumerate(ins):
            for u in range(2):
                outs[u][m * size:(m + 1) * size, :] = piece[u]

    def plain(self):
        return [jnp.concatenate([p[u] for p in self.ins], 0) for u in range(2)]


class Join:
    def __init__(self, mine, recvs, stacked):
        self.scalars, self.ins, self.stacked = [], [*mine, *recvs], stacked
        rows, width = mine[0].shape
        self.outs = [((2, 2 * rows, width), bf16)] if stacked else [((2 * rows, width), bf16)] * 2

    def body(self, scalars, ins, outs):
        for i in range(2):
            for u in range(2):
                src = ins[2 * i + u]
                rows = slice(i * src.shape[0], (i + 1) * src.shape[0])
                if self.stacked:
                    outs[0][u, rows, :] = src[...]
                else:
                    outs[u][rows, :] = src[...]

    def plain(self):
        both = [jnp.concatenate([self.ins[u], self.ins[2 + u]], 0) for u in range(2)]
        return [jnp.stack(both)] if self.stacked else both


class Pack:
    def __init__(self, backs, feed, wide):
        self.scalars, self.ins = [], [*backs, feed, wide]
        self.outs = [((16, feed.shape[1]), f32)]

    def body(self, scalars, ins, outs):
        width = outs[0].shape[1]
        value = ins[0][0:4, :]
        for one in ins[1:-2]:
            value = value + one[0:4, :]
        outs[0][0:4, :] = value
        outs[0][4:8, :] = ins[-2][0:4, :]
        count = ins[-1].shape[1] // width
        for j in range(count):
            outs[0][8 + j:9 + j, :] = ins[-1][:, j * width:(j + 1) * width]
        outs[0][8 + count:16, :] = jnp.zeros((8 - count, width), f32)


def stage_kernel(scalar_ref, *refs, ops, extra):
    ins = sum(len(op.ins) for op in ops)
    outs = refs[ins + extra:]
    at_s = at_i = at_o = 0
    for op in ops:
        op.body(
            [scalar_ref[at_s + i] for i in range(len(op.scalars))], refs[at_i:at_i + len(op.ins)],
            outs[at_o:at_o + len(op.outs)],
        )
        at_s, at_i, at_o = at_s + len(op.scalars), at_i + len(op.ins), at_o + len(op.outs)
    outs[at_o][...] = jnp.zeros(TOKEN.shape, f32)


def stage(ops, inside=True, after=(), through=()):
    plain = [op for op in ops if any(shape[-2] % 16 for shape, _ in op.outs)]
    done = {id(op): op.plain() for op in plain}
    run = [op for op in ops if id(op) not in done]
    spec = (lambda x: pl.BlockSpec(memory_space=pltpu.VMEM)) if inside else (lambda x: whole(x.shape))
    ins = [x for op in run for x in op.ins]
    outs = [o for op in run for o in op.outs]
    scalars = [x for op in run for x in op.scalars] or [jnp.zeros((), jnp.int32)]
    got = pl.pallas_call(
        functools.partial(stage_kernel, ops=run, extra=len(through) + len(after)),
        out_shape=tuple(pltpu.VMEM(shape, dtype) if inside else jax.ShapeDtypeStruct(shape, dtype) for shape, dtype in outs)
        + (TOKEN,) + tuple(jax.ShapeDtypeStruct(x.shape, x.dtype) for x in through),
        grid_spec=pltpu.PrefetchScalarGridSpec(
            num_scalar_prefetch=1,
            grid=(1,),
            in_specs=[spec(x) for x in ins] + [FREE] * (len(through) + len(after)),
            out_specs=[pl.BlockSpec(memory_space=pltpu.VMEM) if inside else whole(shape) for shape, _ in outs]
            + [whole(TOKEN.shape)] + [FREE] * len(through),
        ),
        input_output_aliases={1 + len(ins) + i: len(outs) + 1 + i for i in range(len(through))},
        compiler_params=pltpu.CompilerParams(vmem_limit_bytes=(16 if inside else 56) * 2**20),
        cost_estimate=cost(3),
        name="stage",
    )(jnp.stack(scalars).astype(jnp.int32), *ins, *through, *after)
    at, results = 0, []
    for op in ops:
        if id(op) in done:
            results.append(done[id(op)])
        else:
            results.append(list(got[at:at + len(op.outs)]))
            at += len(op.outs)
    return results, list(got[at + 1:]), got[at]


class Summing:
    def __init__(self, keeps, recvs, stage, small=None, apart=False):
        self.small, self.apart = small, apart
        bits = bits_of("items", 2)
        self.orders = (bits, bits[::-1])
        self.keeps, self.recvs = list(keeps), list(recvs)
        self.steps = [("planar", s) for s in range(stage, len(bits))] + [("across", None), ("total", None)]
        self.steps += [("up", s) for s in reversed(range(len(bits)))] + [("up", None)]
        self.at = 0
        self.mine = None

    @property
    def left(self):
        return len(self.steps) - self.at

    def op(self):
        kind, arg = self.steps[self.at]
        n = lax.axis_size("blk")
        if kind == "planar":
            return Fold([side_of("items", order[arg]) for order in self.orders], self.keeps, self.recvs, self.small)
        if kind == "across":
            return Across(lax.axis_index("blk"), n, self.keeps, self.recvs, self.small)
        if kind == "total":
            return Total(self.recvs, 0 if self.small is None else self.small.shape[0])
        if self.mine is None:
            return Gathered(self.recvs)
        return Join(self.mine, self.recvs, arg is None and not self.apart)

    def take(self, outs):
        kind, arg = self.steps[self.at]
        self.at += 1
        n = lax.axis_size("blk")
        if self.small is not None and kind in ("planar", "across", "total"):
            *outs, self.small = outs
        if kind == "planar":
            self.keeps = outs[2:4]
            self.recvs = [swap(x, "items", order[arg]) for x, order in zip(outs, self.orders)]
        elif kind == "across":
            self.recvs = [outs[0]] + [swap(outs[m], "blk", m) for m in range(1, n)]
        elif kind == "total":
            self.recvs = [outs[0]] + [swap(outs[0], "blk", m) for m in range(1, n)]
        elif arg is None and not self.apart:
            self.mine = outs[0]
            self.recvs = swap(outs[0], "items", 1)
        elif arg is None:
            self.mine = outs
            self.recvs = [swap(x, "items", 1) for x in outs]
        else:
            self.mine = outs
            self.recvs = [swap(x, "items", order[arg]) for x, order in zip(outs, self.orders)]

    def sides(self, u):
        return [side_of("items", b) for b in self.orders[u]] + [side_of("blk", b) for b in reversed(bits_of("blk", 1))]

    def places(self):
        sides = [self.sides(u) for u in range(2)]
        masks = []
        for side in sides:
            mask = jnp.zeros((), jnp.int32)
            for one in side[1:]:
                mask = mask * 2 + one
            masks.append(mask)
        return jnp.stack([side_of("items", 1), sides[0][0], sides[1][0], *masks]).astype(jnp.int32)

    def ordered(self, x, u):
        sides = self.sides(u)
        index = jnp.zeros((1,), jnp.int32)
        for side in sides:
            index = index * 2 + side
        pieces = x.reshape(2 ** len(sides), -1, x.shape[-1])
        return jnp.take(pieces, jnp.arange(2 ** len(sides)) ^ index, axis=0).reshape(x.shape)

    def units(self, mine, other):
        core = side_of("items", 1)
        halves = [[self.ordered(x[u], u).astype(f32) for u in range(2)] for x in (mine, other)]
        low = [jnp.where(core == 0, halves[0][u], halves[1][u]) for u in range(2)]
        high = [jnp.where(core == 0, halves[1][u], halves[0][u]) for u in range(2)]
        return low + high


def gather_rows(x):
    z = lax.axis_index("blk")
    r1 = lax.ppermute(x, "blk", [(0, 1), (1, 2), (2, 3)])
    l1 = lax.ppermute(x, "blk", [(1, 0), (2, 1), (3, 2)])
    r2 = lax.ppermute(x, "blk", [(0, 2), (1, 3)])
    l2 = lax.ppermute(x, "blk", [(2, 0), (3, 1)])
    far = lax.ppermute(jnp.where(z == 2, r2, l2), "blk", [(2, 3), (1, 0)])
    return r1, l1, r2, l2, far


def local(
    tokens, cap_lengths, first_gain, first_shift, query_weight, query_bias, key_weight, value_weight, value_bias,
    out_weight, out_bias, second_gain, second_shift, inner_weight, inner_bias, outer_weight, outer_bias, cotangent,
):
    count, rows, width = tokens.shape
    hidden = inner_weight.shape[1]
    z = lax.axis_index("blk")
    z_arr = jnp.full((1,), z, jnp.int32)
    limits = 1 + IMG + cap_lengths
    key_count = min(-(-(1 + IMG + CAP) // STEP) * STEP, 4 * rows)
    vec = lambda v: v.reshape(1, -1)
    parts = gather_rows(tokens)
    cot_flat = cotangent.reshape(count * rows, width)
    cot_recv = swap(cot_flat, "items", 1)
    tok_all, norm_all, norm_own, q, k, v, ctx, lse = attend(
        limits, z_arr, tokens, parts,
        (query_weight, key_weight, value_weight, vec(first_gain), vec(first_shift), vec(query_bias), vec(value_bias)),
        key_count,
    )
    flat = lambda a: a.reshape(count * rows, width)
    core = side_of("items", 1)
    bit = core.reshape(1).astype(jnp.int32)
    out, attg, ff_send, ff_keep, norm2, branch, ctxg, small2, db1 = feed(
        bit, flat(tokens), flat(ctx), cot_flat,
        (out_weight, vec(out_bias), vec(second_gain), vec(second_shift), inner_weight, vec(inner_bias), outer_weight, vec(outer_bias)),
    )
    ctxg = ctxg.reshape(tokens.shape)
    ff_recv, norm2_recv = swap(ff_send, "items", 1), swap(norm2, "items", 1)
    back = functools.partial(
        attend_back, limits=limits, z=z_arr, own=tokens, tok=tok_all, q=q, k=k, v=v, ctxg=ctxg, lse=lse,
        weights=(query_weight, key_weight, value_weight, vec(first_gain), vec(first_shift)),
    )
    scatter = lambda x: lax.psum_scatter(x, "blk", scatter_dimension=0, tiled=True)
    bits = bits_of("items", 2)
    n_blk = lax.axis_size("blk")
    sides = jnp.stack([side_of("items", bits[0]), side_of("items", bits[-1])]).astype(jnp.int32)
    part0, *grads, small_a = back(0, after=(ff_send, norm2))
    mine = [scatter(part0)]
    send0, send1, *feed_keeps, token = feed_weights(
        jnp.concatenate([1 - sides, sides]), ff_keep, ff_recv, norm2, norm2_recv, cot_flat, cot_recv, after=(small_a,)
    )
    feed_recvs = [swap(send0, "items", bits[0]), swap(send1, "items", bits[-1])]
    part1, *grads, small_b = back(1, into=grads, after=(token,))
    part2, *grads, small_c = back(2, into=grads)
    feed_sum = Summing(feed_keeps, feed_recvs, 1)
    small_op = Pack((small_a, small_b, small_c), small2, db1)
    while feed_sum.steps[feed_sum.at + 1][0] == "planar":
        (outs,), _, token = stage([feed_sum.op()], False)
        feed_sum.take(outs)
    (outs, (small,)), (part1,), token = stage([feed_sum.op(), small_op], False, through=(part1,), after=(small_c,))
    feed_sum.take(outs)
    mine.append(scatter(part1))
    ad = (limits, norm_all, norm_own, *grads, ctx, branch.reshape(tokens.shape))
    *sends, token = attend_weights(1 - bit, *ad, small=small, after=(token,))
    attend_recvs = [swap(x, "items", 1) for x in sends]
    *keeps, token = attend_weights(bit, *ad, after=(token,))
    attend_sum = Summing(keeps, attend_recvs, 0, small, True)
    whole_slice = 2 ** (len(bits) + len(bits_of("blk", 1)) - 1) != PIECES
    placed, turn, ready = False, 0, {0: [mine[0]], 2: [mine[1]]}
    while feed_sum.left or attend_sum.left:
        users = [one for one in (feed_sum, attend_sum) if one.left]
        results, passed, token = stage(
            [one.op() for one in users], 0 < turn < 6, after=(token, *ready.get(turn, ())), through=(part2,) if turn == 2 else ()
        )
        mine += [scatter(x) for x in passed]
        turn += 1
        for one, outs in zip(users, results):
            one.take(outs)
        if not feed_sum.left and not placed and feed_sum not in users and not whole_slice:
            grad_outer, grad_inner, token = feed_place(feed_sum.places(), feed_sum.mine, feed_sum.recvs, after=(token,))
            placed = True
    small = attend_sum.small
    if not whole_slice:
        sum_q, sum_k, sum_v, sum_o, token = attend_place(attend_sum.places(), attend_sum.mine, attend_sum.recvs, after=(token,))
    else:
        feed_units = feed_sum.units(feed_sum.mine, feed_sum.recvs)
        grad_outer = jnp.concatenate([u[:width] for u in feed_units], 0)
        grad_inner = jnp.concatenate([u[width:] for u in feed_units], 1)
        sum_q, sum_k, sum_v, sum_o = attend_sum.units(attend_sum.mine, attend_sum.recvs)
    grad_tokens, token = close(tokens, attg.reshape(tokens.shape), mine, vec(first_gain), after=(token,))
    return (
        out.reshape(tokens.shape), grad_tokens,
        small[0], small[1],
        sum_q, small[2], sum_k, sum_v, small[3],
        sum_o, small[6],
        small[4], small[5],
        grad_inner, small[8:8 + hidden // width].reshape(hidden), grad_outer, small[7],
    )


def solution(mesh):
    row = P("items", "blk", None)
    return jax.shard_map(
        local,
        mesh=mesh,
        in_specs=(row, P("items")) + (P(),) * 15 + (row,),
        out_specs=(row, row) + (P(),) * 15,
        check_vma=False,
    )
```

```python
import functools

import jax
import jax.numpy as jnp
from jax import lax
from jax.experimental import pallas as pl
from jax.experimental.pallas import tpu as pltpu
from jax.sharding import PartitionSpec as P

HD = 64
IMG = 197
CAP = 512
STEP = 256
FF_STEP = 512
norm_eps = 1e-05
masked_score = -1e30
f32 = jnp.float32
bf16 = jnp.bfloat16
TOKEN = jax.ShapeDtypeStruct((8, 128), f32)
FREE = pl.BlockSpec(memory_space=pl.ANY)


def dot_nn(a, b):
    return lax.dot_general(a, b, (((1,), (0,)), ((), ())), preferred_element_type=f32)


def dot_nt(a, b):
    return lax.dot_general(a, b, (((1,), (1,)), ((), ())), preferred_element_type=f32)


def dot_tn(a, b):
    return lax.dot_general(a, b, (((0,), (0,)), ((), ())), preferred_element_type=f32)


def norm_core(rows):
    average = jnp.mean(rows, axis=-1, keepdims=True)
    centred = rows - average
    spread = jnp.mean(centred * centred, axis=-1, keepdims=True)
    scale = lax.rsqrt(spread + norm_eps)
    return centred * scale, scale


def norm_back(unit, scale, gain, grad):
    weighted = grad * gain
    first = jnp.mean(weighted, axis=-1, keepdims=True)
    second = jnp.mean(weighted * unit, axis=-1, keepdims=True)
    return scale * (weighted - first - unit * second)


def normal_cdf_pdf(v):
    size = jnp.abs(v) * 0.7071067811865476
    t = 1.0 / (1.0 + 0.3275911 * size)
    poly = t * (0.254829592 + t * (-0.284496736 + t * (1.421413741 + t * (-1.453152027 + t * 1.061405429))))
    bell = jnp.exp(-0.5 * v * v)
    tail = 0.5 * poly * bell
    return jnp.where(v >= 0, 1.0 - tail, tail), 0.3989422804014327 * bell


def cost(us):
    return pl.CostEstimate(flops=int(us * 5e+08), bytes_accessed=int(us * 1.5e+06), transcendentals=0)


def key_steps(limit, key_count, body):
    steps = key_count // STEP
    for n in range(1, steps + 1):
        low, high = (n - 1) * STEP, n * STEP
        cond = limit > low if n == steps else (limit <= high if n == 1 else (limit > low) & (limit <= high))
        pl.when(cond)(functools.partial(body, high))


def attend_kernel(
    limit_ref, z_ref,
    own_ref, r1_ref, l1_ref, r2_ref, l2_ref, far_ref,
    wq_ref, wk_ref, wv_ref, gain_ref, shift_ref, bq_ref, bv_ref,
    tok_ref, norm_ref, ownnorm_ref, q_ref, k_ref, v_ref, ctx_ref, lse_ref, logs_ref,
):
    item = pl.program_id(0)
    limit = limit_ref[item]
    z = z_ref[0]
    rows, width = own_ref.shape
    key_count = tok_ref.shape[0]
    tail = key_count - 3 * rows

    def place(src, at, cond):
        @pl.when(cond & (at < 3))
        def _():
            tok_ref[pl.ds(pl.multiple_of(at * rows, 16), rows), :] = src[...]

        @pl.when(cond & (at == 3))
        def _():
            tok_ref[3 * rows:key_count, :] = src[0:tail, :]

    place(own_ref, z, z >= 0)
    place(r1_ref, z - 1, z >= 1)
    place(l1_ref, z + 1, z <= 2)
    place(r2_ref, z - 2, z >= 2)
    place(l2_ref, z + 2, z <= 1)
    place(far_ref, 0, z == 3)
    place(far_ref, 3, z == 0)
    gain, shift = gain_ref[...], shift_ref[...]

    unit, _ = norm_core(own_ref[...].astype(f32))
    own_norm = (unit * gain + shift).astype(bf16)
    ownnorm_ref[...] = own_norm
    query = (dot_nn(own_norm, wq_ref[...]) + bq_ref[...]).astype(bf16)
    q_ref[...] = query * jnp.asarray(HD ** -0.5, bf16)

    def project(c, _):
        here = pl.ds(pl.multiple_of(c * STEP, STEP), STEP)
        unit, _ = norm_core(tok_ref[here, :].astype(f32))
        normed = (unit * gain + shift).astype(bf16)
        norm_ref[here, :] = normed
        k_ref[here, :] = dot_nn(normed, wk_ref[...]).astype(bf16)
        v_ref[here, :] = (dot_nn(normed, wv_ref[...]) + bv_ref[...]).astype(bf16)
        return 0

    lax.fori_loop(0, (limit + STEP - 1) // STEP, project, 0)

    def part(high):
        bias = jnp.where(lax.broadcasted_iota(jnp.int32, (1, high), 1) < limit, 0.0, masked_score)
        lane = lax.broadcasted_iota(jnp.int32, (rows, 2 * HD), 1)

        def pair(p):
            cols = pl.ds(pl.multiple_of(p * 2 * HD, 2 * HD), 2 * HD)
            q_pair = q_ref[:, cols]
            k_pair = k_ref[0:high, cols]
            v_pair = v_ref[0:high, cols]
            second = lane >= HD
            zero = jnp.zeros_like(q_pair)
            scores = [dot_nt(jnp.where(second == (h == 1), q_pair, zero), k_pair) + bias for h in range(2)]
            outs = []
            for h in range(2):
                top = jnp.max(scores[h], axis=1, keepdims=True)
                shifted = jnp.exp(scores[h] - top)
                total = jnp.sum(shifted, axis=1, keepdims=True)
                probs = (shifted * (1.0 / total)).astype(bf16)
                outs.append(dot_nn(probs, v_pair))
                logs_ref[...] = jnp.where(lane == 2 * p + h, top + jnp.log(total), logs_ref[...])
            ctx_ref[:, cols] = jnp.where(second, outs[1], outs[0]).astype(bf16)

        def pairs(i, _):
            pair(2 * i)
            pair(2 * i + 1)
            return 0

        lax.fori_loop(0, width // (4 * HD), pairs, 0)

    key_steps(limit, key_count, part)
    lse_ref[...] = logs_ref[...].T[0:lse_ref.shape[0], :]


def whole(shape):
    return pl.BlockSpec(shape, lambda *_: (0,) * len(shape))


def attend(limits, z, own, parts, weights, key_count):
    count, rows, width = own.shape
    row_spec = pl.BlockSpec((None, rows, width), lambda i, *_: (i, 0, 0))
    key_spec = pl.BlockSpec((None, key_count, width), lambda i, *_: (i, 0, 0))
    lse_spec = pl.BlockSpec((None, 16, rows), lambda i, *_: (i, 0, 0))
    wq, wk, wv, gain, shift, bq, bv = weights
    vec = whole((1, width))
    mat = whole((width, width))
    row = jax.ShapeDtypeStruct((count, rows, width), bf16)
    key = jax.ShapeDtypeStruct((count, key_count, width), bf16)
    return pl.pallas_call(
        attend_kernel,
        out_shape=(key, key, row, row, key, key, row, jax.ShapeDtypeStruct((count, 16, rows), f32)),
        grid_spec=pltpu.PrefetchScalarGridSpec(
            num_scalar_prefetch=2,
            grid=(count,),
            in_specs=[row_spec] * 6 + [mat] * 3 + [vec] * 4,
            out_specs=[key_spec, key_spec, row_spec, row_spec, key_spec, key_spec, row_spec, lse_spec],
            scratch_shapes=[pltpu.VMEM((rows, 2 * HD), f32)],
        ),
        compiler_params=pltpu.CompilerParams(vmem_limit_bytes=56 * 2**20),
        cost_estimate=cost(28),
        name="attend",
    )(limits, z, own, *parts, wq, wk, wv, gain, shift, bq, bv)


def feed_kernel(
    bit_ref, tok_ref, ctx_ref, cot_ref, wo_ref, bo_ref, gain_ref, shift_ref, w1_ref, b1_ref, w2_ref, b2_ref,
    out_ref, attg_ref, send_ref, keep_ref, norm_ref, branch_ref, ctxg_ref, small_ref, db1_ref,
    att_acc, grad_acc, unit_keep, scale_keep,
):
    step = pl.program_id(0)
    last = pl.num_programs(0) - 1

    @pl.when(step == 0)
    def _():
        attended = tok_ref[...].astype(f32) + (dot_nn(ctx_ref[...], wo_ref[...]) + bo_ref[...])
        unit, scale = norm_core(attended)
        norm_ref[...] = (unit * gain_ref[...] + shift_ref[...]).astype(bf16)
        unit_keep[...] = unit
        scale_keep[...] = jnp.broadcast_to(scale, scale_keep.shape)
        att_acc[...] = attended + b2_ref[...]
        grad_acc[...] = jnp.zeros_like(grad_acc)

    cot = cot_ref[...]
    inner = dot_nn(norm_ref[...], w1_ref[...]) + b1_ref[...]
    cdf, pdf = normal_cdf_pdf(inner)
    act = (inner * cdf).astype(bf16)
    act_grad = dot_nt(cot, w2_ref[...])
    pre = ((cdf + inner * pdf) * act_grad).astype(bf16)

    @pl.when(step <= last // 2)
    def _():
        send_ref[0] = act
        send_ref[1] = pre

    @pl.when(step > last // 2)
    def _():
        keep_ref[0] = act
        keep_ref[1] = pre

    db1_ref[...] = jnp.sum(pre.astype(f32), axis=0, keepdims=True)
    att_acc[...] += dot_nn(act, w2_ref[...])
    grad_acc[...] += dot_nt(pre, w1_ref[...])

    @pl.when(step == last)
    def _():
        out_ref[...] = att_acc[...].astype(bf16)
        unit, grad = unit_keep[...], grad_acc[...]
        cot_wide = cot_ref[...].astype(f32)
        attended_grad = cot_wide + norm_back(unit, scale_keep[:, 0:1], gain_ref[...], grad)
        attg_ref[...] = attended_grad
        branch = attended_grad.astype(bf16)
        branch_ref[...] = branch
        ctxg_ref[...] = dot_nt(branch, wo_ref[...]).astype(bf16)
        small_ref[0:1, :] = jnp.sum(grad * unit, axis=0, keepdims=True)
        small_ref[1:2, :] = jnp.sum(grad, axis=0, keepdims=True)
        small_ref[2:3, :] = jnp.sum(branch.astype(f32), axis=0, keepdims=True)
        small_ref[3:4, :] = jnp.sum(cot_wide, axis=0, keepdims=True)
        small_ref[4:8, :] = jnp.zeros((4, small_ref.shape[1]), f32)


def feed(bit, tok, ctx, cot, weights):
    wo, bo, gain, shift, w1, b1, w2, b2 = weights
    rows, width = tok.shape
    hidden = w1.shape[1]
    row = whole((rows, width))
    vec = whole((1, width))
    half = hidden // FF_STEP // 2

    def chunk(j, bit_ref):
        return jnp.where(j < half, (1 - bit_ref[0]) * half + j, bit_ref[0] * half + j - half)

    pair = jax.ShapeDtypeStruct((2, rows, hidden // 2), bf16)
    return pl.pallas_call(
        feed_kernel,
        out_shape=(
            jax.ShapeDtypeStruct((rows, width), bf16),
            jax.ShapeDtypeStruct((rows, width), f32),
            pair,
            pair,
            jax.ShapeDtypeStruct((rows, width), bf16),
            jax.ShapeDtypeStruct((rows, width), bf16),
            jax.ShapeDtypeStruct((rows, width), bf16),
            jax.ShapeDtypeStruct((8, width), f32),
            jax.ShapeDtypeStruct((1, hidden), f32),
        ),
        grid_spec=pltpu.PrefetchScalarGridSpec(
            num_scalar_prefetch=1,
            grid=(2 * half,),
            in_specs=[
                row, row, row, whole((width, width)), vec, vec, vec,
                pl.BlockSpec((width, FF_STEP), lambda j, b: (0, chunk(j, b))),
                pl.BlockSpec((1, FF_STEP), lambda j, b: (0, chunk(j, b))),
                pl.BlockSpec((FF_STEP, width), lambda j, b: (chunk(j, b), 0)),
                vec,
            ],
            out_specs=[
                row, row,
                pl.BlockSpec((2, rows, FF_STEP), lambda j, b: (0, 0, jnp.minimum(j, half - 1))),
                pl.BlockSpec((2, rows, FF_STEP), lambda j, b: (0, 0, jnp.maximum(j - half, 0))),
                row, row, row, whole((8, width)),
                pl.BlockSpec((1, FF_STEP), lambda j, b: (0, chunk(j, b))),
            ],
            scratch_shapes=[
                pltpu.VMEM((rows, width), f32),
                pltpu.VMEM((rows, width), f32),
                pltpu.VMEM((rows, width), f32),
                pltpu.VMEM((rows, 128), f32),
            ],
        ),
        compiler_params=pltpu.CompilerParams(vmem_limit_bytes=56 * 2**20),
        cost_estimate=cost(29),
        name="feed",
    )(bit, tok, ctx, cot, wo, bo, gain, shift, w1, b1, w2, b2)


def attend_back_kernel(
    limit_ref, z_ref,
    own_ref, q_ref, k_ref, v_ref, ctxg_ref, lse_ref, gain_ref, shift_ref,
    tok_any, wq_any, wk_any, wv_any, *rest, item,
):
    part_ref, dq_ref, dk_ref, dv_ref, small_ref, tok_ref, wq_ref, wk_ref, wv_ref, sems = rest[-10:]
    fetch = [
        pltpu.make_async_copy(src, dst, sems.at[i])
        for i, (src, dst) in enumerate((
            (tok_any.at[item], tok_ref), (wk_any, wk_ref), (wv_any, wv_ref), (wq_any, wq_ref)))
    ]
    for one in fetch:
        one.start()
    limit = limit_ref[0]
    z = z_ref[0]
    rows, width = own_ref.shape
    key_count = tok_ref.shape[0]

    def part(high):
        bias = jnp.where(lax.broadcasted_iota(jnp.int32, (high, 1), 0) < limit, 0.0, masked_score)
        lane = lax.broadcasted_iota(jnp.int32, (rows, 2 * HD), 1)

        lane_keys = lax.broadcasted_iota(jnp.int32, (high, 2 * HD), 1)

        def pair(p):
            cols = pl.ds(pl.multiple_of(p * 2 * HD, 2 * HD), 2 * HD)
            q_pair = q_ref[:, cols]
            k_pair = k_ref[0:high, cols]
            v_pair = v_ref[0:high, cols]
            g_pair = ctxg_ref[:, cols]
            k_turned = k_pair.T
            zero = jnp.zeros_like(q_pair)
            pre = []
            for h in range(2):
                mine = (lane >= HD) == (h == 1)
                pre.append((
                    dot_nt(k_pair, jnp.where(mine, q_pair, zero)) + bias,
                    dot_nt(v_pair, jnp.where(mine, g_pair, zero)),
                ))
            dqs, dks, dvs = [], [], []
            for h, (scores, prob_grad) in enumerate(pre):
                probs = jnp.exp(scores - lse_ref[pl.ds(2 * p + h, 1), :])
                delta = jnp.sum(probs * prob_grad, axis=0, keepdims=True)
                score_grad = (probs * (prob_grad - delta)).astype(bf16)
                dvs.append(dot_nn(probs.astype(bf16), g_pair))
                dks.append(dot_nn(score_grad, q_pair))
                dqs.append(dot_nn(k_turned[h * HD:(h + 1) * HD, :], score_grad))
            dq_ref[:, cols] = (jnp.concatenate(dqs, axis=0).T * (HD ** -0.5)).astype(bf16)
            dk_ref[0:high, cols] = jnp.where(lane_keys >= HD, dks[1], dks[0]).astype(bf16)
            dv_ref[0:high, cols] = jnp.where(lane_keys >= HD, dvs[1], dvs[0]).astype(bf16)

        def pairs(i, _):
            pair(2 * i)
            pair(2 * i + 1)
            return 0

        lax.fori_loop(0, width // (4 * HD), pairs, 0)

    key_steps(limit, key_count, part)

    for one in fetch:
        one.wait()
    small_ref[...] = jnp.zeros_like(small_ref)

    def inward(c, _):
        here = pl.ds(pl.multiple_of(c * STEP, STEP), STEP)
        unit, _ = norm_core(tok_ref[here, :].astype(f32))
        dk, dv = dk_ref[here, :], dv_ref[here, :]
        grad = dot_nt(dk, wk_ref[...]) + dot_nt(dv, wv_ref[...])
        small_ref[0:1, :] += jnp.sum(grad * unit, axis=0, keepdims=True)
        small_ref[1:2, :] += jnp.sum(grad, axis=0, keepdims=True)
        small_ref[3:4, :] += jnp.sum(dv.astype(f32), axis=0, keepdims=True)
        part_ref[here, :] = grad.astype(bf16)
        return 0

    def outward(c, _):
        part_ref[pl.ds(pl.multiple_of(c * STEP, STEP), STEP), :] = jnp.zeros((STEP, width), bf16)
        return 0

    used = (limit + STEP - 1) // STEP
    lax.fori_loop(0, used, inward, 0)
    lax.fori_loop(used, key_count // STEP, outward, 0)
    part_ref[key_count:, :] = jnp.zeros((part_ref.shape[0] - key_count, width), bf16)

    unit, _ = norm_core(own_ref[...].astype(f32))
    dq = dq_ref[...]
    grad = dot_nt(dq, wq_ref[...])
    small_ref[0:1, :] += jnp.sum(grad * unit, axis=0, keepdims=True)
    small_ref[1:2, :] += jnp.sum(grad, axis=0, keepdims=True)
    small_ref[2:3, :] = jnp.sum(dq.astype(f32), axis=0, keepdims=True)
    here = pl.ds(pl.multiple_of(z * rows, 16), rows)
    part_ref[here, :] = (part_ref[here, :].astype(f32) + grad).astype(bf16)


def attend_back(item, limits, z, own, tok, q, k, v, ctxg, lse, weights, into=None, after=()):
    count, rows, width = own.shape
    key_count = tok.shape[1]
    wq, wk, wv, gain, shift = weights
    row_spec = pl.BlockSpec((None, rows, width), lambda i, *_: (item, 0, 0))
    key_spec = pl.BlockSpec((None, key_count, width), lambda i, *_: (item, 0, 0))
    lse_spec = pl.BlockSpec((None, 16, rows), lambda i, *_: (item, 0, 0))
    vec, free = whole((1, width)), FREE
    into = () if into is None else tuple(into)
    return pl.pallas_call(
        functools.partial(attend_back_kernel, item=item),
        out_shape=(
            jax.ShapeDtypeStruct((4 * rows, width), bf16),
            jax.ShapeDtypeStruct((count, rows, width), bf16),
            jax.ShapeDtypeStruct((count, key_count, width), bf16),
            jax.ShapeDtypeStruct((count, key_count, width), bf16),
            jax.ShapeDtypeStruct((8, width), f32),
        ),
        grid_spec=pltpu.PrefetchScalarGridSpec(
            num_scalar_prefetch=2,
            grid=(1,),
            in_specs=[row_spec, row_spec, key_spec, key_spec, row_spec, lse_spec, vec, vec]
            + [free] * (4 + len(into) + len(after)),
            out_specs=[whole((4 * rows, width)), row_spec, key_spec, key_spec, whole((8, width))],
            scratch_shapes=[pltpu.VMEM((key_count, width), bf16)]
            + [pltpu.VMEM((width, width), bf16)] * 3 + [pltpu.SemaphoreType.DMA((4,))],
        ),
        input_output_aliases={14 + i: 1 + i for i in range(len(into))},
        compiler_params=pltpu.CompilerParams(vmem_limit_bytes=56 * 2**20),
        cost_estimate=cost(13),
        name="attend_back",
    )(limits[item:item + 1], z, own, q, k, v, ctxg, lse, gain, shift, tok, wq, wk, wv, *into, *after)


def feed_weight_kernel(kind_ref, ff_ref, recv_ref, norm_ref, normr_ref, cot_ref, cotr_ref, *rest):
    outs = rest[-5:-1]
    rest[-1][...] = jnp.zeros(TOKEN.shape, f32)
    step = pl.program_id(0)
    kind = kind_ref[step]

    def put(value):
        for i, out in enumerate(outs):
            @pl.when(step == i)
            def _():
                out[...] = value.astype(out.dtype)

    @pl.when(kind == 0)
    def _():
        put(dot_tn(ff_ref[...], cot_ref[...]) + dot_tn(recv_ref[...], cotr_ref[...]))

    @pl.when(kind != 0)
    def _():
        put(dot_tn(norm_ref[...], ff_ref[...]) + dot_tn(normr_ref[...], recv_ref[...]))


def feed_weights(kinds, ff, recv, norm, norm_recv, cot, cot_recv, after=()):
    rows, width = cot.shape
    row = whole((rows, width))
    unit = pl.BlockSpec((None, rows, width), lambda s, kind_ref: (kind_ref[s], 0, s % 2))
    mat = whole((width, width))
    return pl.pallas_call(
        feed_weight_kernel,
        out_shape=(jax.ShapeDtypeStruct((width, width), bf16),) * 4 + (TOKEN,),
        grid_spec=pltpu.PrefetchScalarGridSpec(
            num_scalar_prefetch=1,
            grid=(4,),
            in_specs=[unit, unit, row, row, row, row] + [FREE] * len(after),
            out_specs=[mat] * 4 + [whole(TOKEN.shape)],
        ),
        compiler_params=pltpu.CompilerParams(vmem_limit_bytes=56 * 2**20),
        cost_estimate=cost(13),
        name="feed_weights",
    )(kinds, ff, recv, norm, norm_recv, cot, cot_recv, *after)


def split_rows(small):
    high = small.astype(bf16)
    low = (small - high.astype(f32)).astype(bf16)
    return high, low, high.astype(f32) + low.astype(f32)


def attend_weight_kernel(
    half_ref, limit_ref, norm_ref, own_ref, dq_ref, dk_ref, dv_ref, ctx_ref, branch_ref, *rest, small,
):
    acc_ref = rest[-1]
    outs = rest[-4:-2]
    rest[-2][...] = jnp.zeros(TOKEN.shape, f32)
    step = pl.program_id(0)
    item = step % 3
    unit = 2 * half_ref[0] + step // 3
    key_count, width = norm_ref.shape

    if small:
        @pl.when(step == 0)
        def _():
            high, low, _ = split_rows(rest[0][...])
            count = high.shape[0]
            outs[0][width:width + count, :] = high
            outs[0][width + count:width + 2 * count, :] = low

    def put(value):
        @pl.when(item == 0)
        def _():
            acc_ref[...] = value

        @pl.when(item == 1)
        def _():
            acc_ref[...] += value

        for i in range(2):
            @pl.when(step == 2 + 3 * i)
            def _():
                outs[i][0:width, :] = (acc_ref[...] + value).astype(bf16)

    def keys(grad):
        key_steps(limit_ref[item], key_count, lambda high: put(dot_tn(norm_ref[0:high, :], grad[0:high, :])))

    pl.when(unit == 0)(lambda: put(dot_tn(own_ref[...], dq_ref[...])))
    pl.when(unit == 1)(lambda: keys(dk_ref))
    pl.when(unit == 2)(lambda: keys(dv_ref))
    pl.when(unit == 3)(lambda: put(dot_tn(ctx_ref[...], branch_ref[...])))


def attend_weights(half, limits, norm, own, dq, dk, dv, ctx, branch, small=None, after=()):
    count, rows, width = own.shape
    key_count = norm.shape[1]

    def by_item(size, *units):
        def at(s, half_ref, _):
            unit = 2 * half_ref[0] + s // 3
            used = unit == units[0]
            for one in units[1:]:
                used = used | (unit == one)
            return jnp.where(used, s % 3, 0), 0, 0
        return pl.BlockSpec((None, size, width), at)

    extra = 0 if small is None else 2 * small.shape[0]
    smalls = () if small is None else (small,)
    shapes = [(width + extra, width), (width, width)]
    return pl.pallas_call(
        functools.partial(attend_weight_kernel, small=small is not None),
        out_shape=tuple(jax.ShapeDtypeStruct(x, bf16) for x in shapes) + (TOKEN,),
        grid_spec=pltpu.PrefetchScalarGridSpec(
            num_scalar_prefetch=2,
            grid=(6,),
            in_specs=[
                by_item(key_count, 1, 2), by_item(rows, 0), by_item(rows, 0), by_item(key_count, 1), by_item(key_count, 2),
                by_item(rows, 3), by_item(rows, 3),
            ] + [whole(x.shape) for x in smalls] + [FREE] * len(after),
            out_specs=[whole(x) for x in shapes] + [whole(TOKEN.shape)],
            scratch_shapes=[pltpu.VMEM((width, width), f32)],
        ),
        compiler_params=pltpu.CompilerParams(vmem_limit_bytes=56 * 2**20),
        cost_estimate=cost(9),
        name="attend_weights",
    )(half, limits, norm, own, dq, dk, dv, ctx, branch, *smalls, *after)


def close_kernel(tok_ref, attg_ref, m0_ref, m1_ref, m2_ref, gain_ref, *rest):
    out_ref = rest[-2]
    rest[-1][...] = jnp.zeros(TOKEN.shape, f32)
    for i, part_ref in enumerate((m0_ref, m1_ref, m2_ref)):
        @pl.when(pl.program_id(0) == i)
        def _():
            unit, scale = norm_core(tok_ref[...].astype(f32))
            grad = part_ref[...].astype(f32)
            out_ref[...] = (attg_ref[...] + norm_back(unit, scale, gain_ref[...], grad)).astype(bf16)


def close(tok, attg, parts, gain, after=()):
    count, rows, width = tok.shape
    row = pl.BlockSpec((None, rows, width), lambda i: (i, 0, 0))
    return pl.pallas_call(
        close_kernel,
        out_shape=(jax.ShapeDtypeStruct((count, rows, width), bf16), TOKEN),
        grid=(count,),
        in_specs=[row, row] + [whole((rows, width))] * 3 + [whole((1, width))]
        + [FREE] * len(after),
        out_specs=[row, whole(TOKEN.shape)],
        compiler_params=pltpu.CompilerParams(vmem_limit_bytes=56 * 2**20),
        cost_estimate=cost(4),
        name="close",
    )(tok, attg, *parts, gain, *after)


def place_pieces(src, dst, mask, pieces):
    size = src.shape[0] // pieces
    for i in range(pieces):
        at = pl.multiple_of(jnp.bitwise_xor(mask, i) * size, 8)
        dst[pl.ds(at, size), :] = src[i * size:(i + 1) * size, :].astype(f32)


def feed_place_kernel(at_ref, mine_ref, other_ref, *rest):
    outer_ref, inner_ref = rest[-3:-1]
    rest[-1][...] = jnp.zeros(TOKEN.shape, f32)
    step = pl.program_id(0)
    unit = step % 4
    core, mask = at_ref[0], at_ref[3 + unit % 2]

    def copy(dst):
        @pl.when(unit // 2 == core)
        def _():
            place_pieces(mine_ref, dst, mask, PIECES)

        @pl.when(unit // 2 != core)
        def _():
            place_pieces(other_ref, dst, mask, PIECES)

    pl.when(step < 4)(lambda: copy(outer_ref))
    pl.when(step >= 4)(lambda: copy(inner_ref))


PIECES = 8


def feed_place(at, mine, other, after=()):
    width = mine.shape[-1]

    def source(which):
        def index(s, at_ref):
            low = jnp.bitwise_xor(at_ref[0], which) == 0
            in_low = s % 4 < 2
            held = jnp.where(low, jnp.where(s < 4, 4, 5), s // 4 * 4 + 2)
            t = jnp.where(low == in_low, s, held)
            return t % 2, jnp.bitwise_xor(t // 4, at_ref[1 + t % 2]), 0
        return pl.BlockSpec((None, width, width), index)

    return pl.pallas_call(
        feed_place_kernel,
        out_shape=(jax.ShapeDtypeStruct((4 * width, width), f32), jax.ShapeDtypeStruct((width, 4 * width), f32), TOKEN),
        grid_spec=pltpu.PrefetchScalarGridSpec(
            num_scalar_prefetch=1,
            grid=(8,),
            in_specs=[source(0), source(1)] + [FREE] * len(after),
            out_specs=[
                pl.BlockSpec((width, width), lambda s, _: (jnp.minimum(s, 3), 0)),
                pl.BlockSpec((width, width), lambda s, _: (0, jnp.maximum(s - 4, 0))),
                whole(TOKEN.shape),
            ],
        ),
        compiler_params=pltpu.CompilerParams(vmem_limit_bytes=24 * 2**20),
        cost_estimate=cost(0.1),
        name="feed_place",
    )(at, mine, other, *after)


def attend_place_kernel(at_ref, mine0_ref, mine1_ref, other0_ref, other1_ref, *rest):
    out_refs = rest[-5:-1]
    rest[-1][...] = jnp.zeros(TOKEN.shape, f32)
    core = at_ref[0]
    half = mine0_ref.shape[0] // 2
    for unit, dst in enumerate(out_refs):
        u = unit % 2
        for first in range(2):
            to = dst.at[pl.ds(pl.multiple_of(jnp.bitwise_xor(at_ref[1 + u], first) * half, 8), half), :]
            rows = slice(first * half, (first + 1) * half)
            for here, src in ((core == unit // 2, (mine0_ref, mine1_ref)[u]), (core != unit // 2, (other0_ref, other1_ref)[u])):
                @pl.when(here)
                def _():
                    place_pieces(src.at[rows, :], to, at_ref[3 + u], PIECES)


def attend_place(at, mine, other, after=()):
    width = mine[0].shape[-1]
    return pl.pallas_call(
        attend_place_kernel,
        out_shape=(jax.ShapeDtypeStruct((width, width), f32),) * 4 + (TOKEN,),
        grid_spec=pltpu.PrefetchScalarGridSpec(
            num_scalar_prefetch=1,
            grid=(1,),
            in_specs=[pl.BlockSpec(memory_space=pltpu.VMEM)] * 4 + [FREE] * len(after),
            out_specs=[whole((width, width))] * 4 + [whole(TOKEN.shape)],
        ),
        compiler_params=pltpu.CompilerParams(vmem_limit_bytes=40 * 2**20),
        cost_estimate=cost(0.1),
        name="attend_place",
    )(at, *mine, *other, *after)


def swap(x, axis, bit):
    return lax.ppermute(x, axis, [(i, i ^ bit) for i in range(lax.axis_size(axis))])


def side_of(axis, bit):
    return (lax.axis_index(axis) // bit) % 2


def bits_of(axis, bit):
    bits = []
    while bit < lax.axis_size(axis):
        bits.append(bit)
        bit *= 2
    return bits


def unite(small, got, at, count):
    high, low = got
    return split_rows(small)[2] + (high[at:at + count, :].astype(f32) + low[at + (low is high) * count:, :][0:count].astype(f32))


class Fold:
    def __init__(self, sides, keeps, recvs, small=None):
        self.scalars, self.ins = list(sides), [*keeps, *recvs]
        half, width = keeps[0].shape[0] // 2, keeps[0].shape[1]
        self.half, self.small = half, small is not None
        self.outs = [((half, width), bf16)] * 4
        if self.small:
            self.ins.append(small)
            self.outs = [((half + 2 * small.shape[0], width), bf16)] + self.outs[1:] + [(small.shape, f32)]

    def body(self, scalars, ins, outs):
        half = self.half
        for u in range(2):
            for k, side in ((u, 1 - scalars[u]), (2 + u, scalars[u])):
                at = pl.ds(pl.multiple_of(side * half, 16), half)
                outs[k][0:half, :] = (ins[u][at, :].astype(f32) + ins[2 + u][at, :].astype(f32)).astype(bf16)
        if self.small:
            n = ins[4].shape[0]
            value = unite(ins[4][...], (ins[2], ins[2]), 2 * half, n)
            outs[4][...] = value
            high, low, _ = split_rows(value)
            outs[0][half:half + n, :] = high
            outs[0][half + n:half + 2 * n, :] = low

    def plain(self):
        half, ins = self.half, self.ins
        sums = [ins[u].astype(f32) + ins[2 + u][0:2 * half].astype(f32) for u in range(2)]
        cut = lambda x, side: lax.dynamic_slice_in_dim(x, side * half, half, 0).astype(bf16)
        outs = [cut(x, 1 - side) for x, side in zip(sums, self.scalars)] + [cut(x, side) for x, side in zip(sums, self.scalars)]
        if self.small:
            value = unite(ins[4], (ins[2], ins[2]), 2 * half, ins[4].shape[0])
            high, low, _ = split_rows(value)
            outs = [jnp.concatenate([outs[0], high, low], 0)] + outs[1:] + [value]
        return outs


class Across:
    def __init__(self, z, n, keeps, recvs, small=None):
        self.scalars, self.ins, self.n = [z], [*keeps, *recvs], n
        size, width = keeps[0].shape[0] // n, keeps[0].shape[1]
        self.size, self.small = size, small is not None
        self.outs = [((2, size, width), bf16)] * n
        if self.small:
            self.ins.append(small)
            self.outs = [((2, size + small.shape[0], width), bf16)] * n + [(small.shape, f32)]

    def body(self, scalars, ins, outs):
        size, n = self.size, self.n
        for m in range(n):
            at = pl.ds(pl.multiple_of(jnp.bitwise_xor(scalars[0], m) * size, 16), size)
            for u in range(2):
                outs[m][u, 0:size, :] = (ins[u][at, :].astype(f32) + ins[2 + u][at, :].astype(f32)).astype(bf16)
        if self.small:
            rows = ins[4].shape[0]
            value = unite(ins[4][...], (ins[2], ins[2]), n * size, rows)
            outs[n][...] = value
            high, low, _ = split_rows(value)
            for m in range(n):
                outs[m][0, size:size + rows, :] = high
                outs[m][1, size:size + rows, :] = low

    def plain(self):
        size, n, ins = self.size, self.n, self.ins
        sums = jnp.stack([ins[u].astype(f32) + ins[2 + u][0:n * size].astype(f32) for u in range(2)])
        cuts = [lax.dynamic_slice_in_dim(sums, (self.scalars[0] ^ m) * size, size, 1).astype(bf16) for m in range(n)]
        if self.small:
            value = unite(ins[4], (ins[2], ins[2]), n * size, ins[4].shape[0])
            both = jnp.stack(split_rows(value)[:2])
            cuts = [jnp.concatenate([c, both], 1) for c in cuts] + [value]
        return cuts


class Total:
    def __init__(self, pieces, small=0):
        self.scalars, self.ins, self.small = [], list(pieces), small
        count, rows, width = pieces[0].shape
        self.size = rows - small
        self.outs = [((count, self.size, width), bf16)] + ([((small, width), f32)] if small else [])

    def sums(self, ins):
        value = ins[0][:, 0:self.size, :].astype(f32)
        for one in ins[1:]:
            value = value + one[:, 0:self.size, :].astype(f32)
        outs = [value.astype(bf16)]
        if self.small:
            parts = [x[0, self.size:, :].astype(f32) + x[1, self.size:, :].astype(f32) for x in ins]
            while len(parts) > 1:
                parts = [a + b for a, b in zip(parts[::2], parts[1::2])]
            outs.append(parts[0])
        return outs

    def body(self, scalars, ins, outs):
        for out, value in zip(outs, self.sums(ins)):
            out[...] = value

    def plain(self):
        return self.sums(self.ins)


class Gathered:
    def __init__(self, pieces):
        self.scalars, self.ins = [], list(pieces)
        _, size, width = pieces[0].shape
        self.outs = [((len(pieces) * size, width), bf16)] * 2

    def body(self, scalars, ins, outs):
        size = ins[0].shape[1]
        for m, piece in enumerate(ins):
            for u in range(2):
                outs[u][m * size:(m + 1) * size, :] = piece[u]

    def plain(self):
        return [jnp.concatenate([p[u] for p in self.ins], 0) for u in range(2)]


class Join:
    def __init__(self, mine, recvs, stacked):
        self.scalars, self.ins, self.stacked = [], [*mine, *recvs], stacked
        rows, width = mine[0].shape
        self.outs = [((2, 2 * rows, width), bf16)] if stacked else [((2 * rows, width), bf16)] * 2

    def body(self, scalars, ins, outs):
        for i in range(2):
            for u in range(2):
                src = ins[2 * i + u]
                rows = slice(i * src.shape[0], (i + 1) * src.shape[0])
                if self.stacked:
                    outs[0][u, rows, :] = src[...]
                else:
                    outs[u][rows, :] = src[...]

    def plain(self):
        both = [jnp.concatenate([self.ins[u], self.ins[2 + u]], 0) for u in range(2)]
        return [jnp.stack(both)] if self.stacked else both


class Pack:
    def __init__(self, backs, feed, wide):
        self.scalars, self.ins = [], [*backs, feed, wide]
        self.outs = [((16, feed.shape[1]), f32)]

    def body(self, scalars, ins, outs):
        width = outs[0].shape[1]
        value = ins[0][0:4, :]
        for one in ins[1:-2]:
            value = value + one[0:4, :]
        outs[0][0:4, :] = value
        outs[0][4:8, :] = ins[-2][0:4, :]
        count = ins[-1].shape[1] // width
        for j in range(count):
            outs[0][8 + j:9 + j, :] = ins[-1][:, j * width:(j + 1) * width]
        outs[0][8 + count:16, :] = jnp.zeros((8 - count, width), f32)


def stage_kernel(scalar_ref, *refs, ops, extra):
    ins = sum(len(op.ins) for op in ops)
    outs = refs[ins + extra:]
    at_s = at_i = at_o = 0
    for op in ops:
        op.body(
            [scalar_ref[at_s + i] for i in range(len(op.scalars))], refs[at_i:at_i + len(op.ins)],
            outs[at_o:at_o + len(op.outs)],
        )
        at_s, at_i, at_o = at_s + len(op.scalars), at_i + len(op.ins), at_o + len(op.outs)
    outs[at_o][...] = jnp.zeros(TOKEN.shape, f32)


def stage(ops, inside=True, given=None, after=(), through=()):
    plain = [op for op in ops if any(shape[-2] % 16 for shape, _ in op.outs)]
    done = {id(op): op.plain() for op in plain}
    run = [op for op in ops if id(op) not in done]
    given = inside if given is None else given
    spec = (lambda x: pl.BlockSpec(memory_space=pltpu.VMEM)) if inside else (lambda x: whole(x.shape))
    ins = [x for op in run for x in op.ins]
    outs = [o for op in run for o in op.outs]
    scalars = [x for op in run for x in op.scalars] or [jnp.zeros((), jnp.int32)]
    got = pl.pallas_call(
        functools.partial(stage_kernel, ops=run, extra=len(through) + len(after)),
        out_shape=tuple(pltpu.VMEM(shape, dtype) if given else jax.ShapeDtypeStruct(shape, dtype) for shape, dtype in outs)
        + (TOKEN,) + tuple(jax.ShapeDtypeStruct(x.shape, x.dtype) for x in through),
        grid_spec=pltpu.PrefetchScalarGridSpec(
            num_scalar_prefetch=1,
            grid=(1,),
            in_specs=[spec(x) for x in ins] + [FREE] * (len(through) + len(after)),
            out_specs=[pl.BlockSpec(memory_space=pltpu.VMEM) if given else whole(shape) for shape, _ in outs]
            + [whole(TOKEN.shape)] + [FREE] * len(through),
        ),
        input_output_aliases={1 + len(ins) + i: len(outs) + 1 + i for i in range(len(through))},
        compiler_params=pltpu.CompilerParams(vmem_limit_bytes=(16 if inside else 32 if given else 56) * 2**20),
        cost_estimate=cost(3),
        name="stage",
    )(jnp.stack(scalars).astype(jnp.int32), *ins, *through, *after)
    at, results = 0, []
    for op in ops:
        if id(op) in done:
            results.append(done[id(op)])
        else:
            results.append(list(got[at:at + len(op.outs)]))
            at += len(op.outs)
    return results, list(got[at + 1:]), got[at]


class Summing:
    def __init__(self, keeps, recvs, stage, small=None, apart=False):
        self.small, self.apart = small, apart
        bits = bits_of("items", 2)
        self.orders = (bits, bits[::-1])
        self.keeps, self.recvs = list(keeps), list(recvs)
        self.steps = [("planar", s) for s in range(stage, len(bits))] + [("across", None), ("total", None)]
        self.steps += [("up", s) for s in reversed(range(len(bits)))] + [("up", None)]
        self.at = 0
        self.mine = None

    @property
    def left(self):
        return len(self.steps) - self.at

    def op(self):
        kind, arg = self.steps[self.at]
        n = lax.axis_size("blk")
        if kind == "planar":
            return Fold([side_of("items", order[arg]) for order in self.orders], self.keeps, self.recvs, self.small)
        if kind == "across":
            return Across(lax.axis_index("blk"), n, self.keeps, self.recvs, self.small)
        if kind == "total":
            return Total(self.recvs, 0 if self.small is None else self.small.shape[0])
        if self.mine is None:
            return Gathered(self.recvs)
        return Join(self.mine, self.recvs, arg is None and not self.apart)

    def take(self, outs):
        kind, arg = self.steps[self.at]
        self.at += 1
        n = lax.axis_size("blk")
        if self.small is not None and kind in ("planar", "across", "total"):
            *outs, self.small = outs
        if kind == "planar":
            self.keeps = outs[2:4]
            self.recvs = [swap(x, "items", order[arg]) for x, order in zip(outs, self.orders)]
        elif kind == "across":
            self.recvs = [outs[0]] + [swap(outs[m], "blk", m) for m in range(1, n)]
        elif kind == "total":
            self.recvs = [outs[0]] + [swap(outs[0], "blk", m) for m in range(1, n)]
        elif arg is None and not self.apart:
            self.mine = outs[0]
            self.recvs = swap(outs[0], "items", 1)
        elif arg is None:
            self.mine = outs
            self.recvs = [swap(x, "items", 1) for x in outs]
        else:
            self.mine = outs
            self.recvs = [swap(x, "items", order[arg]) for x, order in zip(outs, self.orders)]

    def sides(self, u):
        return [side_of("items", b) for b in self.orders[u]] + [side_of("blk", b) for b in reversed(bits_of("blk", 1))]

    def places(self):
        sides = [self.sides(u) for u in range(2)]
        masks = []
        for side in sides:
            mask = jnp.zeros((), jnp.int32)
            for one in side[1:]:
                mask = mask * 2 + one
            masks.append(mask)
        return jnp.stack([side_of("items", 1), sides[0][0], sides[1][0], *masks]).astype(jnp.int32)

    def ordered(self, x, u):
        sides = self.sides(u)
        index = jnp.zeros((1,), jnp.int32)
        for side in sides:
            index = index * 2 + side
        pieces = x.reshape(2 ** len(sides), -1, x.shape[-1])
        return jnp.take(pieces, jnp.arange(2 ** len(sides)) ^ index, axis=0).reshape(x.shape)

    def units(self, mine, other):
        core = side_of("items", 1)
        halves = [[self.ordered(x[u], u).astype(f32) for u in range(2)] for x in (mine, other)]
        low = [jnp.where(core == 0, halves[0][u], halves[1][u]) for u in range(2)]
        high = [jnp.where(core == 0, halves[1][u], halves[0][u]) for u in range(2)]
        return low + high


def gather_rows(x):
    z = lax.axis_index("blk")
    r1 = lax.ppermute(x, "blk", [(0, 1), (1, 2), (2, 3)])
    l1 = lax.ppermute(x, "blk", [(1, 0), (2, 1), (3, 2)])
    r2 = lax.ppermute(x, "blk", [(0, 2), (1, 3)])
    l2 = lax.ppermute(x, "blk", [(2, 0), (3, 1)])
    far = lax.ppermute(jnp.where(z == 2, r2, l2), "blk", [(2, 3), (1, 0)])
    return r1, l1, r2, l2, far


def local(
    tokens, cap_lengths, first_gain, first_shift, query_weight, query_bias, key_weight, value_weight, value_bias,
    out_weight, out_bias, second_gain, second_shift, inner_weight, inner_bias, outer_weight, outer_bias, cotangent,
):
    count, rows, width = tokens.shape
    hidden = inner_weight.shape[1]
    z = lax.axis_index("blk")
    z_arr = jnp.full((1,), z, jnp.int32)
    limits = 1 + IMG + cap_lengths
    key_count = min(-(-(1 + IMG + CAP) // STEP) * STEP, 4 * rows)
    vec = lambda v: v.reshape(1, -1)
    parts = gather_rows(tokens)
    cot_flat = cotangent.reshape(count * rows, width)
    cot_recv = swap(cot_flat, "items", 1)
    tok_all, norm_all, norm_own, q, k, v, ctx, lse = attend(
        limits, z_arr, tokens, parts,
        (query_weight, key_weight, value_weight, vec(first_gain), vec(first_shift), vec(query_bias), vec(value_bias)),
        key_count,
    )
    flat = lambda a: a.reshape(count * rows, width)
    core = side_of("items", 1)
    bit = core.reshape(1).astype(jnp.int32)
    out, attg, ff_send, ff_keep, norm2, branch, ctxg, small2, db1 = feed(
        bit, flat(tokens), flat(ctx), cot_flat,
        (out_weight, vec(out_bias), vec(second_gain), vec(second_shift), inner_weight, vec(inner_bias), outer_weight, vec(outer_bias)),
    )
    ctxg = ctxg.reshape(tokens.shape)
    ff_recv, norm2_recv = swap(ff_send, "items", 1), swap(norm2, "items", 1)
    back = functools.partial(
        attend_back, limits=limits, z=z_arr, own=tokens, tok=tok_all, q=q, k=k, v=v, ctxg=ctxg, lse=lse,
        weights=(query_weight, key_weight, value_weight, vec(first_gain), vec(first_shift)),
    )
    scatter = lambda x: lax.psum_scatter(x, "blk", scatter_dimension=0, tiled=True)
    bits = bits_of("items", 2)
    n_blk = lax.axis_size("blk")
    sides = jnp.stack([side_of("items", bits[0]), side_of("items", bits[-1])]).astype(jnp.int32)
    part0, *grads, small_a = back(0, after=(ff_send, norm2))
    mine = [scatter(part0)]
    send0, send1, *feed_keeps, token = feed_weights(
        jnp.concatenate([1 - sides, sides]), ff_keep, ff_recv, norm2, norm2_recv, cot_flat, cot_recv, after=(small_a,)
    )
    feed_recvs = [swap(send0, "items", bits[0]), swap(send1, "items", bits[-1])]
    part1, *grads, small_b = back(1, into=grads, after=(token,))
    part2, *grads, small_c = back(2, into=grads)
    feed_sum = Summing(feed_keeps, feed_recvs, 1)
    small_op = Pack((small_a, small_b, small_c), small2, db1)
    while feed_sum.steps[feed_sum.at + 1][0] == "planar":
        (outs,), _, token = stage([feed_sum.op()], False)
        feed_sum.take(outs)
    (outs, (small,)), (part1,), token = stage([feed_sum.op(), small_op], False, through=(part1,), after=(small_c,))
    feed_sum.take(outs)
    mine.append(scatter(part1))
    ad = (limits, norm_all, norm_own, *grads, ctx, branch.reshape(tokens.shape))
    *sends, token = attend_weights(1 - bit, *ad, small=small, after=(token,))
    attend_recvs = [swap(x, "items", 1) for x in sends]
    *keeps, token = attend_weights(bit, *ad, after=(token,))
    attend_sum = Summing(keeps, attend_recvs, 0, small, True)
    whole_slice = 2 ** (len(bits) + len(bits_of("blk", 1)) - 1) != PIECES
    placed, turn, ready = False, 0, {0: [mine[0]], 2: [mine[1]]}
    while feed_sum.left or attend_sum.left:
        users = [one for one in (feed_sum, attend_sum) if one.left]
        results, passed, token = stage(
            [one.op() for one in users], turn > 0, True, after=(token, *ready.get(turn, ())), through=(part2,) if turn == 2 else ()
        )
        mine += [scatter(x) for x in passed]
        turn += 1
        for one, outs in zip(users, results):
            one.take(outs)
        if not feed_sum.left and not placed and feed_sum not in users and not whole_slice:
            grad_outer, grad_inner, token = feed_place(feed_sum.places(), feed_sum.mine, feed_sum.recvs, after=(token,))
            placed = True
    small = attend_sum.small
    if not whole_slice:
        sum_q, sum_k, sum_v, sum_o, token = attend_place(attend_sum.places(), attend_sum.mine, attend_sum.recvs, after=(token,))
    else:
        feed_units = feed_sum.units(feed_sum.mine, feed_sum.recvs)
        grad_outer = jnp.concatenate([u[:width] for u in feed_units], 0)
        grad_inner = jnp.concatenate([u[width:] for u in feed_units], 1)
        sum_q, sum_k, sum_v, sum_o = attend_sum.units(attend_sum.mine, attend_sum.recvs)
    grad_tokens, token = close(tokens, attg.reshape(tokens.shape), mine, vec(first_gain), after=(token,))
    return (
        out.reshape(tokens.shape), grad_tokens,
        small[0], small[1],
        sum_q, small[2], sum_k, sum_v, small[3],
        sum_o, small[6],
        small[4], small[5],
        grad_inner, small[8:8 + hidden // width].reshape(hidden), grad_outer, small[7],
    )


def solution(mesh):
    row = P("items", "blk", None)
    return jax.shard_map(
        local,
        mesh=mesh,
        in_specs=(row, P("items")) + (P(),) * 15 + (row,),
        out_specs=(row, row) + (P(),) * 15,
        check_vma=False,
    )
```

```python
import functools

import jax
import jax.numpy as jnp
from jax import lax
from jax.experimental import pallas as pl
from jax.experimental.pallas import tpu as pltpu
from jax.sharding import PartitionSpec as P

HD = 64
IMG = 197
CAP = 512
STEP = 256
FF_STEP = 768
norm_eps = 1e-05
masked_score = -1e30
f32 = jnp.float32
bf16 = jnp.bfloat16
TOKEN = jax.ShapeDtypeStruct((8, 128), f32)
FREE = pl.BlockSpec(memory_space=pl.ANY)


def dot_nn(a, b):
    return lax.dot_general(a, b, (((1,), (0,)), ((), ())), preferred_element_type=f32)


def dot_nt(a, b):
    return lax.dot_general(a, b, (((1,), (1,)), ((), ())), preferred_element_type=f32)


def dot_tn(a, b):
    return lax.dot_general(a, b, (((0,), (0,)), ((), ())), preferred_element_type=f32)


def norm_core(rows):
    average = jnp.mean(rows, axis=-1, keepdims=True)
    centred = rows - average
    spread = jnp.mean(centred * centred, axis=-1, keepdims=True)
    scale = lax.rsqrt(spread + norm_eps)
    return centred * scale, scale


def norm_back(unit, scale, gain, grad):
    weighted = grad * gain
    first = jnp.mean(weighted, axis=-1, keepdims=True)
    second = jnp.mean(weighted * unit, axis=-1, keepdims=True)
    return scale * (weighted - first - unit * second)


def normal_cdf_pdf(v):
    size = jnp.abs(v) * 0.7071067811865476
    t = 1.0 / (1.0 + 0.3275911 * size)
    poly = t * (0.254829592 + t * (-0.284496736 + t * (1.421413741 + t * (-1.453152027 + t * 1.061405429))))
    bell = jnp.exp(-0.5 * v * v)
    tail = 0.5 * poly * bell
    return jnp.where(v >= 0, 1.0 - tail, tail), 0.3989422804014327 * bell


def cost(us):
    return pl.CostEstimate(flops=int(us * 5e+08), bytes_accessed=int(us * 1.5e+06), transcendentals=0)


def key_steps(limit, key_count, body):
    steps = key_count // STEP
    for n in range(1, steps + 1):
        low, high = (n - 1) * STEP, n * STEP
        cond = limit > low if n == steps else (limit <= high if n == 1 else (limit > low) & (limit <= high))
        pl.when(cond)(functools.partial(body, high))


def attend_kernel(
    limit_ref, z_ref,
    own_ref, r1_ref, l1_ref, r2_ref, l2_ref, far_ref,
    wq_ref, wk_ref, wv_ref, gain_ref, shift_ref, bq_ref, bv_ref,
    tok_ref, norm_ref, ownnorm_ref, q_ref, k_ref, v_ref, ctx_ref, lse_ref, logs_ref,
):
    item = pl.program_id(0)
    limit = limit_ref[item]
    z = z_ref[0]
    rows, width = own_ref.shape
    key_count = tok_ref.shape[0]
    tail = key_count - 3 * rows

    def place(src, at, cond):
        @pl.when(cond & (at < 3))
        def _():
            tok_ref[pl.ds(pl.multiple_of(at * rows, 16), rows), :] = src[...]

        @pl.when(cond & (at == 3))
        def _():
            tok_ref[3 * rows:key_count, :] = src[0:tail, :]

    place(own_ref, z, z >= 0)
    place(r1_ref, z - 1, z >= 1)
    place(l1_ref, z + 1, z <= 2)
    place(r2_ref, z - 2, z >= 2)
    place(l2_ref, z + 2, z <= 1)
    place(far_ref, 0, z == 3)
    place(far_ref, 3, z == 0)
    gain, shift = gain_ref[...], shift_ref[...]

    unit, _ = norm_core(own_ref[...].astype(f32))
    own_norm = (unit * gain + shift).astype(bf16)
    ownnorm_ref[...] = own_norm
    query = (dot_nn(own_norm, wq_ref[...]) + bq_ref[...]).astype(bf16)
    q_ref[...] = query * jnp.asarray(HD ** -0.5, bf16)

    def project(c, _):
        here = pl.ds(pl.multiple_of(c * STEP, STEP), STEP)
        unit, _ = norm_core(tok_ref[here, :].astype(f32))
        normed = (unit * gain + shift).astype(bf16)
        norm_ref[here, :] = normed
        k_ref[here, :] = dot_nn(normed, wk_ref[...]).astype(bf16)
        v_ref[here, :] = (dot_nn(normed, wv_ref[...]) + bv_ref[...]).astype(bf16)
        return 0

    lax.fori_loop(0, (limit + STEP - 1) // STEP, project, 0)

    def part(high):
        bias = jnp.where(lax.broadcasted_iota(jnp.int32, (1, high), 1) < limit, 0.0, masked_score)
        lane = lax.broadcasted_iota(jnp.int32, (rows, 2 * HD), 1)

        def pair(p):
            cols = pl.ds(pl.multiple_of(p * 2 * HD, 2 * HD), 2 * HD)
            q_pair = q_ref[:, cols]
            k_pair = k_ref[0:high, cols]
            v_pair = v_ref[0:high, cols]
            second = lane >= HD
            zero = jnp.zeros_like(q_pair)
            scores = [dot_nt(jnp.where(second == (h == 1), q_pair, zero), k_pair) + bias for h in range(2)]
            outs = []
            for h in range(2):
                top = jnp.max(scores[h], axis=1, keepdims=True)
                shifted = jnp.exp(scores[h] - top)
                total = jnp.sum(shifted, axis=1, keepdims=True)
                probs = (shifted * (1.0 / total)).astype(bf16)
                outs.append(dot_nn(probs, v_pair))
                logs_ref[...] = jnp.where(lane == 2 * p + h, top + jnp.log(total), logs_ref[...])
            ctx_ref[:, cols] = jnp.where(second, outs[1], outs[0]).astype(bf16)

        def pairs(i, _):
            for j in range(3):
                pair(3 * i + j)
            return 0

        lax.fori_loop(0, width // (6 * HD), pairs, 0)

    key_steps(limit, key_count, part)
    lse_ref[...] = logs_ref[...].T[0:lse_ref.shape[0], :]


def whole(shape):
    return pl.BlockSpec(shape, lambda *_: (0,) * len(shape))


def attend(limits, z, own, parts, weights, key_count):
    count, rows, width = own.shape
    row_spec = pl.BlockSpec((None, rows, width), lambda i, *_: (i, 0, 0))
    key_spec = pl.BlockSpec((None, key_count, width), lambda i, *_: (i, 0, 0))
    lse_spec = pl.BlockSpec((None, 16, rows), lambda i, *_: (i, 0, 0))
    wq, wk, wv, gain, shift, bq, bv = weights
    vec = whole((1, width))
    mat = whole((width, width))
    row = jax.ShapeDtypeStruct((count, rows, width), bf16)
    key = jax.ShapeDtypeStruct((count, key_count, width), bf16)
    return pl.pallas_call(
        attend_kernel,
        out_shape=(key, key, row, row, key, key, row, jax.ShapeDtypeStruct((count, 16, rows), f32)),
        grid_spec=pltpu.PrefetchScalarGridSpec(
            num_scalar_prefetch=2,
            grid=(count,),
            in_specs=[row_spec] * 6 + [mat] * 3 + [vec] * 4,
            out_specs=[key_spec, key_spec, row_spec, row_spec, key_spec, key_spec, row_spec, lse_spec],
            scratch_shapes=[pltpu.VMEM((rows, 2 * HD), f32)],
        ),
        compiler_params=pltpu.CompilerParams(vmem_limit_bytes=56 * 2**20),
        cost_estimate=cost(28),
        name="attend",
    )(limits, z, own, *parts, wq, wk, wv, gain, shift, bq, bv)


def feed_kernel(
    bit_ref, tok_ref, ctx_ref, cot_ref, wo_ref, bo_ref, gain_ref, shift_ref, w1_ref, b1_ref, w2_ref, b2_ref,
    out_ref, attg_ref, send_ref, keep_ref, norm_ref, branch_ref, ctxg_ref, small_ref, db1_ref,
    att_acc, grad_acc, unit_keep, scale_keep,
):
    step = pl.program_id(0)
    last = pl.num_programs(0) - 1

    @pl.when(step == 0)
    def _():
        attended = tok_ref[...].astype(f32) + (dot_nn(ctx_ref[...], wo_ref[...]) + bo_ref[...])
        unit, scale = norm_core(attended)
        norm_ref[...] = (unit * gain_ref[...] + shift_ref[...]).astype(bf16)
        unit_keep[...] = unit
        scale_keep[...] = jnp.broadcast_to(scale, scale_keep.shape)
        att_acc[...] = attended + b2_ref[...]
        grad_acc[...] = jnp.zeros_like(grad_acc)

    cot = cot_ref[...]
    inner = dot_nn(norm_ref[...], w1_ref[...]) + b1_ref[...]
    cdf, pdf = normal_cdf_pdf(inner)
    act = (inner * cdf).astype(bf16)
    act_grad = dot_nt(cot, w2_ref[...])
    pre = ((cdf + inner * pdf) * act_grad).astype(bf16)

    @pl.when(step <= last // 2)
    def _():
        send_ref[0] = act
        send_ref[1] = pre

    @pl.when(step > last // 2)
    def _():
        keep_ref[0] = act
        keep_ref[1] = pre

    db1_ref[...] = jnp.sum(pre.astype(f32), axis=0, keepdims=True)
    att_acc[...] += dot_nn(act, w2_ref[...])
    grad_acc[...] += dot_nt(pre, w1_ref[...])

    @pl.when(step == last)
    def _():
        out_ref[...] = att_acc[...].astype(bf16)
        unit, grad = unit_keep[...], grad_acc[...]
        cot_wide = cot_ref[...].astype(f32)
        attended_grad = cot_wide + norm_back(unit, scale_keep[:, 0:1], gain_ref[...], grad)
        attg_ref[...] = attended_grad
        branch = attended_grad.astype(bf16)
        branch_ref[...] = branch
        ctxg_ref[...] = dot_nt(branch, wo_ref[...]).astype(bf16)
        small_ref[0:1, :] = jnp.sum(grad * unit, axis=0, keepdims=True)
        small_ref[1:2, :] = jnp.sum(grad, axis=0, keepdims=True)
        small_ref[2:3, :] = jnp.sum(branch.astype(f32), axis=0, keepdims=True)
        small_ref[3:4, :] = jnp.sum(cot_wide, axis=0, keepdims=True)
        small_ref[4:8, :] = jnp.zeros((4, small_ref.shape[1]), f32)


def feed(bit, tok, ctx, cot, weights):
    wo, bo, gain, shift, w1, b1, w2, b2 = weights
    rows, width = tok.shape
    hidden = w1.shape[1]
    row = whole((rows, width))
    vec = whole((1, width))
    half = hidden // FF_STEP // 2

    def chunk(j, bit_ref):
        return jnp.where(j < half, (1 - bit_ref[0]) * half + j, bit_ref[0] * half + j - half)

    pair = jax.ShapeDtypeStruct((2, rows, hidden // 2), bf16)
    return pl.pallas_call(
        feed_kernel,
        out_shape=(
            jax.ShapeDtypeStruct((rows, width), bf16),
            jax.ShapeDtypeStruct((rows, width), f32),
            pair,
            pair,
            jax.ShapeDtypeStruct((rows, width), bf16),
            jax.ShapeDtypeStruct((rows, width), bf16),
            jax.ShapeDtypeStruct((rows, width), bf16),
            jax.ShapeDtypeStruct((8, width), f32),
            jax.ShapeDtypeStruct((1, hidden), f32),
        ),
        grid_spec=pltpu.PrefetchScalarGridSpec(
            num_scalar_prefetch=1,
            grid=(2 * half,),
            in_specs=[
                row, row, row, whole((width, width)), vec, vec, vec,
                pl.BlockSpec((width, FF_STEP), lambda j, b: (0, chunk(j, b))),
                pl.BlockSpec((1, FF_STEP), lambda j, b: (0, chunk(j, b))),
                pl.BlockSpec((FF_STEP, width), lambda j, b: (chunk(j, b), 0)),
                vec,
            ],
            out_specs=[
                row, row,
                pl.BlockSpec((2, rows, FF_STEP), lambda j, b: (0, 0, jnp.minimum(j, half - 1))),
                pl.BlockSpec((2, rows, FF_STEP), lambda j, b: (0, 0, jnp.maximum(j - half, 0))),
                row, row, row, whole((8, width)),
                pl.BlockSpec((1, FF_STEP), lambda j, b: (0, chunk(j, b))),
            ],
            scratch_shapes=[
                pltpu.VMEM((rows, width), f32),
                pltpu.VMEM((rows, width), f32),
                pltpu.VMEM((rows, width), f32),
                pltpu.VMEM((rows, 128), f32),
            ],
        ),
        compiler_params=pltpu.CompilerParams(vmem_limit_bytes=56 * 2**20),
        cost_estimate=cost(29),
        name="feed",
    )(bit, tok, ctx, cot, wo, bo, gain, shift, w1, b1, w2, b2)


def attend_back_kernel(
    limit_ref, z_ref,
    own_ref, q_ref, k_ref, v_ref, ctxg_ref, lse_ref, gain_ref, shift_ref,
    tok_any, wq_any, wk_any, wv_any, *rest, item,
):
    part_ref, dq_ref, dk_ref, dv_ref, small_ref, tok_ref, wq_ref, wk_ref, wv_ref, sems = rest[-10:]
    fetch = [
        pltpu.make_async_copy(src, dst, sems.at[i])
        for i, (src, dst) in enumerate((
            (tok_any.at[item], tok_ref), (wk_any, wk_ref), (wv_any, wv_ref), (wq_any, wq_ref)))
    ]
    for one in fetch:
        one.start()
    limit = limit_ref[0]
    z = z_ref[0]
    rows, width = own_ref.shape
    key_count = tok_ref.shape[0]

    def part(high):
        bias = jnp.where(lax.broadcasted_iota(jnp.int32, (high, 1), 0) < limit, 0.0, masked_score)
        lane = lax.broadcasted_iota(jnp.int32, (rows, 2 * HD), 1)

        lane_keys = lax.broadcasted_iota(jnp.int32, (high, 2 * HD), 1)

        def pair(p):
            cols = pl.ds(pl.multiple_of(p * 2 * HD, 2 * HD), 2 * HD)
            q_pair = q_ref[:, cols]
            k_pair = k_ref[0:high, cols]
            v_pair = v_ref[0:high, cols]
            g_pair = ctxg_ref[:, cols]
            k_turned = k_pair.T
            zero = jnp.zeros_like(q_pair)
            pre = []
            for h in range(2):
                mine = (lane >= HD) == (h == 1)
                pre.append((
                    dot_nt(k_pair, jnp.where(mine, q_pair, zero)) + bias,
                    dot_nt(v_pair, jnp.where(mine, g_pair, zero)),
                ))
            dqs, dks, dvs = [], [], []
            for h, (scores, prob_grad) in enumerate(pre):
                probs = jnp.exp(scores - lse_ref[pl.ds(2 * p + h, 1), :])
                delta = jnp.sum(probs * prob_grad, axis=0, keepdims=True)
                score_grad = (probs * (prob_grad - delta)).astype(bf16)
                dvs.append(dot_nn(probs.astype(bf16), g_pair))
                dks.append(dot_nn(score_grad, q_pair))
                dqs.append(dot_nn(k_turned[h * HD:(h + 1) * HD, :], score_grad))
            dq_ref[:, cols] = (jnp.concatenate(dqs, axis=0).T * (HD ** -0.5)).astype(bf16)
            dk_ref[0:high, cols] = jnp.where(lane_keys >= HD, dks[1], dks[0]).astype(bf16)
            dv_ref[0:high, cols] = jnp.where(lane_keys >= HD, dvs[1], dvs[0]).astype(bf16)

        def pairs(i, _):
            pair(2 * i)
            pair(2 * i + 1)
            return 0

        lax.fori_loop(0, width // (4 * HD), pairs, 0)

    key_steps(limit, key_count, part)

    for one in fetch:
        one.wait()
    small_ref[...] = jnp.zeros_like(small_ref)

    def inward(c, _):
        here = pl.ds(pl.multiple_of(c * STEP, STEP), STEP)
        unit, _ = norm_core(tok_ref[here, :].astype(f32))
        dk, dv = dk_ref[here, :], dv_ref[here, :]
        grad = dot_nt(dk, wk_ref[...]) + dot_nt(dv, wv_ref[...])
        small_ref[0:1, :] += jnp.sum(grad * unit, axis=0, keepdims=True)
        small_ref[1:2, :] += jnp.sum(grad, axis=0, keepdims=True)
        small_ref[3:4, :] += jnp.sum(dv.astype(f32), axis=0, keepdims=True)
        part_ref[here, :] = grad.astype(bf16)
        return 0

    def outward(c, _):
        part_ref[pl.ds(pl.multiple_of(c * STEP, STEP), STEP), :] = jnp.zeros((STEP, width), bf16)
        return 0

    used = (limit + STEP - 1) // STEP
    lax.fori_loop(0, used, inward, 0)
    lax.fori_loop(used, key_count // STEP, outward, 0)
    part_ref[key_count:, :] = jnp.zeros((part_ref.shape[0] - key_count, width), bf16)

    unit, _ = norm_core(own_ref[...].astype(f32))
    dq = dq_ref[...]
    grad = dot_nt(dq, wq_ref[...])
    small_ref[0:1, :] += jnp.sum(grad * unit, axis=0, keepdims=True)
    small_ref[1:2, :] += jnp.sum(grad, axis=0, keepdims=True)
    small_ref[2:3, :] = jnp.sum(dq.astype(f32), axis=0, keepdims=True)
    here = pl.ds(pl.multiple_of(z * rows, 16), rows)
    part_ref[here, :] = (part_ref[here, :].astype(f32) + grad).astype(bf16)


def attend_back(item, limits, z, own, tok, q, k, v, ctxg, lse, weights, into=None, after=()):
    count, rows, width = own.shape
    key_count = tok.shape[1]
    wq, wk, wv, gain, shift = weights
    row_spec = pl.BlockSpec((None, rows, width), lambda i, *_: (item, 0, 0))
    key_spec = pl.BlockSpec((None, key_count, width), lambda i, *_: (item, 0, 0))
    lse_spec = pl.BlockSpec((None, 16, rows), lambda i, *_: (item, 0, 0))
    vec, free = whole((1, width)), FREE
    into = () if into is None else tuple(into)
    return pl.pallas_call(
        functools.partial(attend_back_kernel, item=item),
        out_shape=(
            jax.ShapeDtypeStruct((4 * rows, width), bf16),
            jax.ShapeDtypeStruct((count, rows, width), bf16),
            jax.ShapeDtypeStruct((count, key_count, width), bf16),
            jax.ShapeDtypeStruct((count, key_count, width), bf16),
            jax.ShapeDtypeStruct((8, width), f32),
        ),
        grid_spec=pltpu.PrefetchScalarGridSpec(
            num_scalar_prefetch=2,
            grid=(1,),
            in_specs=[row_spec, row_spec, key_spec, key_spec, row_spec, lse_spec, vec, vec]
            + [free] * (4 + len(into) + len(after)),
            out_specs=[whole((4 * rows, width)), row_spec, key_spec, key_spec, whole((8, width))],
            scratch_shapes=[pltpu.VMEM((key_count, width), bf16)]
            + [pltpu.VMEM((width, width), bf16)] * 3 + [pltpu.SemaphoreType.DMA((4,))],
        ),
        input_output_aliases={14 + i: 1 + i for i in range(len(into))},
        compiler_params=pltpu.CompilerParams(vmem_limit_bytes=56 * 2**20),
        cost_estimate=cost(13),
        name="attend_back",
    )(limits[item:item + 1], z, own, q, k, v, ctxg, lse, gain, shift, tok, wq, wk, wv, *into, *after)


def feed_weight_kernel(kind_ref, ff_ref, recv_ref, norm_ref, normr_ref, cot_ref, cotr_ref, *rest):
    outs = rest[-5:-1]
    rest[-1][...] = jnp.zeros(TOKEN.shape, f32)
    step = pl.program_id(0)
    kind = kind_ref[step]

    def put(value):
        for i, out in enumerate(outs):
            @pl.when(step == i)
            def _():
                out[...] = value.astype(out.dtype)

    @pl.when(kind == 0)
    def _():
        put(dot_tn(ff_ref[...], cot_ref[...]) + dot_tn(recv_ref[...], cotr_ref[...]))

    @pl.when(kind != 0)
    def _():
        put(dot_tn(norm_ref[...], ff_ref[...]) + dot_tn(normr_ref[...], recv_ref[...]))


def feed_weights(kinds, ff, recv, norm, norm_recv, cot, cot_recv, after=()):
    rows, width = cot.shape
    row = whole((rows, width))
    unit = pl.BlockSpec((None, rows, width), lambda s, kind_ref: (kind_ref[s], 0, s % 2))
    mat = whole((width, width))
    return pl.pallas_call(
        feed_weight_kernel,
        out_shape=(jax.ShapeDtypeStruct((width, width), bf16),) * 4 + (TOKEN,),
        grid_spec=pltpu.PrefetchScalarGridSpec(
            num_scalar_prefetch=1,
            grid=(4,),
            in_specs=[unit, unit, row, row, row, row] + [FREE] * len(after),
            out_specs=[mat] * 4 + [whole(TOKEN.shape)],
        ),
        compiler_params=pltpu.CompilerParams(vmem_limit_bytes=56 * 2**20),
        cost_estimate=cost(13),
        name="feed_weights",
    )(kinds, ff, recv, norm, norm_recv, cot, cot_recv, *after)


def split_rows(small):
    high = small.astype(bf16)
    low = (small - high.astype(f32)).astype(bf16)
    return high, low, high.astype(f32) + low.astype(f32)


def attend_weight_kernel(
    half_ref, limit_ref, norm_ref, own_ref, dq_ref, dk_ref, dv_ref, ctx_ref, branch_ref, *rest, small,
):
    acc_ref = rest[-1]
    outs = rest[-4:-2]
    rest[-2][...] = jnp.zeros(TOKEN.shape, f32)
    step = pl.program_id(0)
    item = step % 3
    unit = 2 * half_ref[0] + step // 3
    key_count, width = norm_ref.shape

    if small:
        @pl.when(step == 0)
        def _():
            high, low, _ = split_rows(rest[0][...])
            count = high.shape[0]
            outs[0][width:width + count, :] = high
            outs[0][width + count:width + 2 * count, :] = low

    def put(value):
        @pl.when(item == 0)
        def _():
            acc_ref[...] = value

        @pl.when(item == 1)
        def _():
            acc_ref[...] += value

        for i in range(2):
            @pl.when(step == 2 + 3 * i)
            def _():
                outs[i][0:width, :] = (acc_ref[...] + value).astype(bf16)

    def keys(grad):
        key_steps(limit_ref[item], key_count, lambda high: put(dot_tn(norm_ref[0:high, :], grad[0:high, :])))

    pl.when(unit == 0)(lambda: put(dot_tn(own_ref[...], dq_ref[...])))
    pl.when(unit == 1)(lambda: keys(dk_ref))
    pl.when(unit == 2)(lambda: keys(dv_ref))
    pl.when(unit == 3)(lambda: put(dot_tn(ctx_ref[...], branch_ref[...])))


def attend_weights(half, limits, norm, own, dq, dk, dv, ctx, branch, small=None, after=()):
    count, rows, width = own.shape
    key_count = norm.shape[1]

    def by_item(size, *units):
        def at(s, half_ref, _):
            unit = 2 * half_ref[0] + s // 3
            used = unit == units[0]
            for one in units[1:]:
                used = used | (unit == one)
            return jnp.where(used, s % 3, 0), 0, 0
        return pl.BlockSpec((None, size, width), at)

    extra = 0 if small is None else 2 * small.shape[0]
    smalls = () if small is None else (small,)
    shapes = [(width + extra, width), (width, width)]
    return pl.pallas_call(
        functools.partial(attend_weight_kernel, small=small is not None),
        out_shape=tuple(jax.ShapeDtypeStruct(x, bf16) for x in shapes) + (TOKEN,),
        grid_spec=pltpu.PrefetchScalarGridSpec(
            num_scalar_prefetch=2,
            grid=(6,),
            in_specs=[
                by_item(key_count, 1, 2), by_item(rows, 0), by_item(rows, 0), by_item(key_count, 1), by_item(key_count, 2),
                by_item(rows, 3), by_item(rows, 3),
            ] + [whole(x.shape) for x in smalls] + [FREE] * len(after),
            out_specs=[whole(x) for x in shapes] + [whole(TOKEN.shape)],
            scratch_shapes=[pltpu.VMEM((width, width), f32)],
        ),
        compiler_params=pltpu.CompilerParams(vmem_limit_bytes=56 * 2**20),
        cost_estimate=cost(9),
        name="attend_weights",
    )(half, limits, norm, own, dq, dk, dv, ctx, branch, *smalls, *after)


def close_kernel(tok_ref, attg_ref, m0_ref, m1_ref, m2_ref, gain_ref, *rest):
    out_ref = rest[-2]
    rest[-1][...] = jnp.zeros(TOKEN.shape, f32)
    for i, part_ref in enumerate((m0_ref, m1_ref, m2_ref)):
        @pl.when(pl.program_id(0) == i)
        def _():
            unit, scale = norm_core(tok_ref[...].astype(f32))
            grad = part_ref[...].astype(f32)
            out_ref[...] = (attg_ref[...] + norm_back(unit, scale, gain_ref[...], grad)).astype(bf16)


def close(tok, attg, parts, gain, after=()):
    count, rows, width = tok.shape
    row = pl.BlockSpec((None, rows, width), lambda i: (i, 0, 0))
    return pl.pallas_call(
        close_kernel,
        out_shape=(jax.ShapeDtypeStruct((count, rows, width), bf16), TOKEN),
        grid=(count,),
        in_specs=[row, row] + [whole((rows, width))] * 3 + [whole((1, width))]
        + [FREE] * len(after),
        out_specs=[row, whole(TOKEN.shape)],
        compiler_params=pltpu.CompilerParams(vmem_limit_bytes=56 * 2**20),
        cost_estimate=cost(4),
        name="close",
    )(tok, attg, *parts, gain, *after)


def place_pieces(src, dst, mask, pieces):
    size = src.shape[0] // pieces
    for i in range(pieces):
        at = pl.multiple_of(jnp.bitwise_xor(mask, i) * size, 8)
        dst[pl.ds(at, size), :] = src[i * size:(i + 1) * size, :].astype(f32)


def feed_place_kernel(at_ref, mine_ref, other_ref, *rest):
    outer_ref, inner_ref = rest[-3:-1]
    rest[-1][...] = jnp.zeros(TOKEN.shape, f32)
    step = pl.program_id(0)
    unit = step % 4
    core, mask = at_ref[0], at_ref[3 + unit % 2]

    def copy(dst):
        @pl.when(unit // 2 == core)
        def _():
            place_pieces(mine_ref, dst, mask, PIECES)

        @pl.when(unit // 2 != core)
        def _():
            place_pieces(other_ref, dst, mask, PIECES)

    pl.when(step < 4)(lambda: copy(outer_ref))
    pl.when(step >= 4)(lambda: copy(inner_ref))


PIECES = 8


def feed_place(at, mine, other, after=()):
    width = mine.shape[-1]

    def source(which):
        def index(s, at_ref):
            low = jnp.bitwise_xor(at_ref[0], which) == 0
            in_low = s % 4 < 2
            held = jnp.where(low, jnp.where(s < 4, 4, 5), s // 4 * 4 + 2)
            t = jnp.where(low == in_low, s, held)
            return t % 2, jnp.bitwise_xor(t // 4, at_ref[1 + t % 2]), 0
        return pl.BlockSpec((None, width, width), index)

    return pl.pallas_call(
        feed_place_kernel,
        out_shape=(jax.ShapeDtypeStruct((4 * width, width), f32), jax.ShapeDtypeStruct((width, 4 * width), f32), TOKEN),
        grid_spec=pltpu.PrefetchScalarGridSpec(
            num_scalar_prefetch=1,
            grid=(8,),
            in_specs=[source(0), source(1)] + [FREE] * len(after),
            out_specs=[
                pl.BlockSpec((width, width), lambda s, _: (jnp.minimum(s, 3), 0)),
                pl.BlockSpec((width, width), lambda s, _: (0, jnp.maximum(s - 4, 0))),
                whole(TOKEN.shape),
            ],
        ),
        compiler_params=pltpu.CompilerParams(vmem_limit_bytes=24 * 2**20),
        cost_estimate=cost(0.1),
        name="feed_place",
    )(at, mine, other, *after)


def attend_place_kernel(at_ref, mine0_ref, mine1_ref, other0_ref, other1_ref, *rest):
    out_refs = rest[-5:-1]
    rest[-1][...] = jnp.zeros(TOKEN.shape, f32)
    core = at_ref[0]
    half = mine0_ref.shape[0] // 2
    for unit, dst in enumerate(out_refs):
        u = unit % 2
        for first in range(2):
            to = dst.at[pl.ds(pl.multiple_of(jnp.bitwise_xor(at_ref[1 + u], first) * half, 8), half), :]
            rows = slice(first * half, (first + 1) * half)
            for here, src in ((core == unit // 2, (mine0_ref, mine1_ref)[u]), (core != unit // 2, (other0_ref, other1_ref)[u])):
                @pl.when(here)
                def _():
                    place_pieces(src.at[rows, :], to, at_ref[3 + u], PIECES)


def attend_place(at, mine, other, after=()):
    width = mine[0].shape[-1]
    return pl.pallas_call(
        attend_place_kernel,
        out_shape=(jax.ShapeDtypeStruct((width, width), f32),) * 4 + (TOKEN,),
        grid_spec=pltpu.PrefetchScalarGridSpec(
            num_scalar_prefetch=1,
            grid=(1,),
            in_specs=[pl.BlockSpec(memory_space=pltpu.VMEM)] * 4 + [FREE] * len(after),
            out_specs=[whole((width, width))] * 4 + [whole(TOKEN.shape)],
        ),
        compiler_params=pltpu.CompilerParams(vmem_limit_bytes=40 * 2**20),
        cost_estimate=cost(0.1),
        name="attend_place",
    )(at, *mine, *other, *after)


def swap(x, axis, bit):
    return lax.ppermute(x, axis, [(i, i ^ bit) for i in range(lax.axis_size(axis))])


def side_of(axis, bit):
    return (lax.axis_index(axis) // bit) % 2


def bits_of(axis, bit):
    bits = []
    while bit < lax.axis_size(axis):
        bits.append(bit)
        bit *= 2
    return bits


def unite(small, got, at, count):
    high, low = got
    return split_rows(small)[2] + (high[at:at + count, :].astype(f32) + low[at + (low is high) * count:, :][0:count].astype(f32))


class Fold:
    def __init__(self, sides, keeps, recvs, small=None):
        self.scalars, self.ins = list(sides), [*keeps, *recvs]
        half, width = keeps[0].shape[0] // 2, keeps[0].shape[1]
        self.half, self.small = half, small is not None
        self.outs = [((half, width), bf16)] * 4
        if self.small:
            self.ins.append(small)
            self.outs = [((half + 2 * small.shape[0], width), bf16)] + self.outs[1:] + [(small.shape, f32)]

    def body(self, scalars, ins, outs):
        half = self.half
        for u in range(2):
            for k, side in ((u, 1 - scalars[u]), (2 + u, scalars[u])):
                at = pl.ds(pl.multiple_of(side * half, 16), half)
                outs[k][0:half, :] = (ins[u][at, :].astype(f32) + ins[2 + u][at, :].astype(f32)).astype(bf16)
        if self.small:
            n = ins[4].shape[0]
            value = unite(ins[4][...], (ins[2], ins[2]), 2 * half, n)
            outs[4][...] = value
            high, low, _ = split_rows(value)
            outs[0][half:half + n, :] = high
            outs[0][half + n:half + 2 * n, :] = low

    def plain(self):
        half, ins = self.half, self.ins
        sums = [ins[u].astype(f32) + ins[2 + u][0:2 * half].astype(f32) for u in range(2)]
        cut = lambda x, side: lax.dynamic_slice_in_dim(x, side * half, half, 0).astype(bf16)
        outs = [cut(x, 1 - side) for x, side in zip(sums, self.scalars)] + [cut(x, side) for x, side in zip(sums, self.scalars)]
        if self.small:
            value = unite(ins[4], (ins[2], ins[2]), 2 * half, ins[4].shape[0])
            high, low, _ = split_rows(value)
            outs = [jnp.concatenate([outs[0], high, low], 0)] + outs[1:] + [value]
        return outs


class Across:
    def __init__(self, z, n, keeps, recvs, small=None):
        self.scalars, self.ins, self.n = [z], [*keeps, *recvs], n
        size, width = keeps[0].shape[0] // n, keeps[0].shape[1]
        self.size, self.small = size, small is not None
        self.outs = [((2, size, width), bf16)] * n
        if self.small:
            self.ins.append(small)
            self.outs = [((2, size + small.shape[0], width), bf16)] * n + [(small.shape, f32)]

    def body(self, scalars, ins, outs):
        size, n = self.size, self.n
        for m in range(n):
            at = pl.ds(pl.multiple_of(jnp.bitwise_xor(scalars[0], m) * size, 16), size)
            for u in range(2):
                outs[m][u, 0:size, :] = (ins[u][at, :].astype(f32) + ins[2 + u][at, :].astype(f32)).astype(bf16)
        if self.small:
            rows = ins[4].shape[0]
            value = unite(ins[4][...], (ins[2], ins[2]), n * size, rows)
            outs[n][...] = value
            high, low, _ = split_rows(value)
            for m in range(n):
                outs[m][0, size:size + rows, :] = high
                outs[m][1, size:size + rows, :] = low

    def plain(self):
        size, n, ins = self.size, self.n, self.ins
        sums = jnp.stack([ins[u].astype(f32) + ins[2 + u][0:n * size].astype(f32) for u in range(2)])
        cuts = [lax.dynamic_slice_in_dim(sums, (self.scalars[0] ^ m) * size, size, 1).astype(bf16) for m in range(n)]
        if self.small:
            value = unite(ins[4], (ins[2], ins[2]), n * size, ins[4].shape[0])
            both = jnp.stack(split_rows(value)[:2])
            cuts = [jnp.concatenate([c, both], 1) for c in cuts] + [value]
        return cuts


class Total:
    def __init__(self, pieces, small=0):
        self.scalars, self.ins, self.small = [], list(pieces), small
        count, rows, width = pieces[0].shape
        self.size = rows - small
        self.outs = [((count, self.size, width), bf16)] + ([((small, width), f32)] if small else [])

    def sums(self, ins):
        value = ins[0][:, 0:self.size, :].astype(f32)
        for one in ins[1:]:
            value = value + one[:, 0:self.size, :].astype(f32)
        outs = [value.astype(bf16)]
        if self.small:
            parts = [x[0, self.size:, :].astype(f32) + x[1, self.size:, :].astype(f32) for x in ins]
            while len(parts) > 1:
                parts = [a + b for a, b in zip(parts[::2], parts[1::2])]
            outs.append(parts[0])
        return outs

    def body(self, scalars, ins, outs):
        for out, value in zip(outs, self.sums(ins)):
            out[...] = value

    def plain(self):
        return self.sums(self.ins)


class Gathered:
    def __init__(self, pieces):
        self.scalars, self.ins = [], list(pieces)
        _, size, width = pieces[0].shape
        self.outs = [((len(pieces) * size, width), bf16)] * 2

    def body(self, scalars, ins, outs):
        size = ins[0].shape[1]
        for m, piece in enumerate(ins):
            for u in range(2):
                outs[u][m * size:(m + 1) * size, :] = piece[u]

    def plain(self):
        return [jnp.concatenate([p[u] for p in self.ins], 0) for u in range(2)]


class Join:
    def __init__(self, mine, recvs, stacked):
        self.scalars, self.ins, self.stacked = [], [*mine, *recvs], stacked
        rows, width = mine[0].shape
        self.outs = [((2, 2 * rows, width), bf16)] if stacked else [((2 * rows, width), bf16)] * 2

    def body(self, scalars, ins, outs):
        for i in range(2):
            for u in range(2):
                src = ins[2 * i + u]
                rows = slice(i * src.shape[0], (i + 1) * src.shape[0])
                if self.stacked:
                    outs[0][u, rows, :] = src[...]
                else:
                    outs[u][rows, :] = src[...]

    def plain(self):
        both = [jnp.concatenate([self.ins[u], self.ins[2 + u]], 0) for u in range(2)]
        return [jnp.stack(both)] if self.stacked else both


class Pack:
    def __init__(self, backs, feed, wide):
        self.scalars, self.ins = [], [*backs, feed, wide]
        self.outs = [((16, feed.shape[1]), f32)]

    def body(self, scalars, ins, outs):
        width = outs[0].shape[1]
        value = ins[0][0:4, :]
        for one in ins[1:-2]:
            value = value + one[0:4, :]
        outs[0][0:4, :] = value
        outs[0][4:8, :] = ins[-2][0:4, :]
        count = ins[-1].shape[1] // width
        for j in range(count):
            outs[0][8 + j:9 + j, :] = ins[-1][:, j * width:(j + 1) * width]
        outs[0][8 + count:16, :] = jnp.zeros((8 - count, width), f32)


def stage_kernel(scalar_ref, *refs, ops, extra):
    ins = sum(len(op.ins) for op in ops)
    outs = refs[ins + extra:]
    at_s = at_i = at_o = 0
    for op in ops:
        op.body(
            [scalar_ref[at_s + i] for i in range(len(op.scalars))], refs[at_i:at_i + len(op.ins)],
            outs[at_o:at_o + len(op.outs)],
        )
        at_s, at_i, at_o = at_s + len(op.scalars), at_i + len(op.ins), at_o + len(op.outs)
    outs[at_o][...] = jnp.zeros(TOKEN.shape, f32)


def stage(ops, inside=True, given=None, after=(), through=()):
    plain = [op for op in ops if any(shape[-2] % 16 for shape, _ in op.outs)]
    done = {id(op): op.plain() for op in plain}
    run = [op for op in ops if id(op) not in done]
    given = inside if given is None else given
    spec = (lambda x: pl.BlockSpec(memory_space=pltpu.VMEM)) if inside else (lambda x: whole(x.shape))
    ins = [x for op in run for x in op.ins]
    outs = [o for op in run for o in op.outs]
    scalars = [x for op in run for x in op.scalars] or [jnp.zeros((), jnp.int32)]
    got = pl.pallas_call(
        functools.partial(stage_kernel, ops=run, extra=len(through) + len(after)),
        out_shape=tuple(pltpu.VMEM(shape, dtype) if given else jax.ShapeDtypeStruct(shape, dtype) for shape, dtype in outs)
        + (TOKEN,) + tuple(jax.ShapeDtypeStruct(x.shape, x.dtype) for x in through),
        grid_spec=pltpu.PrefetchScalarGridSpec(
            num_scalar_prefetch=1,
            grid=(1,),
            in_specs=[spec(x) for x in ins] + [FREE] * (len(through) + len(after)),
            out_specs=[pl.BlockSpec(memory_space=pltpu.VMEM) if given else whole(shape) for shape, _ in outs]
            + [whole(TOKEN.shape)] + [FREE] * len(through),
        ),
        input_output_aliases={1 + len(ins) + i: len(outs) + 1 + i for i in range(len(through))},
        compiler_params=pltpu.CompilerParams(vmem_limit_bytes=(16 if inside else 32 if given else 56) * 2**20),
        cost_estimate=cost(3),
        name="stage",
    )(jnp.stack(scalars).astype(jnp.int32), *ins, *through, *after)
    at, results = 0, []
    for op in ops:
        if id(op) in done:
            results.append(done[id(op)])
        else:
            results.append(list(got[at:at + len(op.outs)]))
            at += len(op.outs)
    return results, list(got[at + 1:]), got[at]


class Summing:
    def __init__(self, keeps, recvs, stage, small=None, apart=False):
        self.small, self.apart = small, apart
        bits = bits_of("items", 2)
        self.orders = (bits, bits[::-1])
        self.keeps, self.recvs = list(keeps), list(recvs)
        self.steps = [("planar", s) for s in range(stage, len(bits))] + [("across", None), ("total", None)]
        self.steps += [("up", s) for s in reversed(range(len(bits)))] + [("up", None)]
        self.at = 0
        self.mine = None

    @property
    def left(self):
        return len(self.steps) - self.at

    def op(self):
        kind, arg = self.steps[self.at]
        n = lax.axis_size("blk")
        if kind == "planar":
            return Fold([side_of("items", order[arg]) for order in self.orders], self.keeps, self.recvs, self.small)
        if kind == "across":
            return Across(lax.axis_index("blk"), n, self.keeps, self.recvs, self.small)
        if kind == "total":
            return Total(self.recvs, 0 if self.small is None else self.small.shape[0])
        if self.mine is None:
            return Gathered(self.recvs)
        return Join(self.mine, self.recvs, arg is None and not self.apart)

    def take(self, outs):
        kind, arg = self.steps[self.at]
        self.at += 1
        n = lax.axis_size("blk")
        if self.small is not None and kind in ("planar", "across", "total"):
            *outs, self.small = outs
        if kind == "planar":
            self.keeps = outs[2:4]
            self.recvs = [swap(x, "items", order[arg]) for x, order in zip(outs, self.orders)]
        elif kind == "across":
            self.recvs = [outs[0]] + [swap(outs[m], "blk", m) for m in range(1, n)]
        elif kind == "total":
            self.recvs = [outs[0]] + [swap(outs[0], "blk", m) for m in range(1, n)]
        elif arg is None and not self.apart:
            self.mine = outs[0]
            self.recvs = swap(outs[0], "items", 1)
        elif arg is None:
            self.mine = outs
            self.recvs = [swap(x, "items", 1) for x in outs]
        else:
            self.mine = outs
            self.recvs = [swap(x, "items", order[arg]) for x, order in zip(outs, self.orders)]

    def sides(self, u):
        return [side_of("items", b) for b in self.orders[u]] + [side_of("blk", b) for b in reversed(bits_of("blk", 1))]

    def places(self):
        sides = [self.sides(u) for u in range(2)]
        masks = []
        for side in sides:
            mask = jnp.zeros((), jnp.int32)
            for one in side[1:]:
                mask = mask * 2 + one
            masks.append(mask)
        return jnp.stack([side_of("items", 1), sides[0][0], sides[1][0], *masks]).astype(jnp.int32)

    def ordered(self, x, u):
        sides = self.sides(u)
        index = jnp.zeros((1,), jnp.int32)
        for side in sides:
            index = index * 2 + side
        pieces = x.reshape(2 ** len(sides), -1, x.shape[-1])
        return jnp.take(pieces, jnp.arange(2 ** len(sides)) ^ index, axis=0).reshape(x.shape)

    def units(self, mine, other):
        core = side_of("items", 1)
        halves = [[self.ordered(x[u], u).astype(f32) for u in range(2)] for x in (mine, other)]
        low = [jnp.where(core == 0, halves[0][u], halves[1][u]) for u in range(2)]
        high = [jnp.where(core == 0, halves[1][u], halves[0][u]) for u in range(2)]
        return low + high


def gather_rows(x):
    z = lax.axis_index("blk")
    r1 = lax.ppermute(x, "blk", [(0, 1), (1, 2), (2, 3)])
    l1 = lax.ppermute(x, "blk", [(1, 0), (2, 1), (3, 2)])
    r2 = lax.ppermute(x, "blk", [(0, 2), (1, 3)])
    l2 = lax.ppermute(x, "blk", [(2, 0), (3, 1)])
    far = lax.ppermute(jnp.where(z == 2, r2, l2), "blk", [(2, 3), (1, 0)])
    return r1, l1, r2, l2, far


def local(
    tokens, cap_lengths, first_gain, first_shift, query_weight, query_bias, key_weight, value_weight, value_bias,
    out_weight, out_bias, second_gain, second_shift, inner_weight, inner_bias, outer_weight, outer_bias, cotangent,
):
    count, rows, width = tokens.shape
    hidden = inner_weight.shape[1]
    z = lax.axis_index("blk")
    z_arr = jnp.full((1,), z, jnp.int32)
    limits = 1 + IMG + cap_lengths
    key_count = min(-(-(1 + IMG + CAP) // STEP) * STEP, 4 * rows)
    vec = lambda v: v.reshape(1, -1)
    parts = gather_rows(tokens)
    cot_flat = cotangent.reshape(count * rows, width)
    cot_recv = swap(cot_flat, "items", 1)
    tok_all, norm_all, norm_own, q, k, v, ctx, lse = attend(
        limits, z_arr, tokens, parts,
        (query_weight, key_weight, value_weight, vec(first_gain), vec(first_shift), vec(query_bias), vec(value_bias)),
        key_count,
    )
    flat = lambda a: a.reshape(count * rows, width)
    core = side_of("items", 1)
    bit = core.reshape(1).astype(jnp.int32)
    out, attg, ff_send, ff_keep, norm2, branch, ctxg, small2, db1 = feed(
        bit, flat(tokens), flat(ctx), cot_flat,
        (out_weight, vec(out_bias), vec(second_gain), vec(second_shift), inner_weight, vec(inner_bias), outer_weight, vec(outer_bias)),
    )
    ctxg = ctxg.reshape(tokens.shape)
    ff_recv, norm2_recv = swap(ff_send, "items", 1), swap(norm2, "items", 1)
    back = functools.partial(
        attend_back, limits=limits, z=z_arr, own=tokens, tok=tok_all, q=q, k=k, v=v, ctxg=ctxg, lse=lse,
        weights=(query_weight, key_weight, value_weight, vec(first_gain), vec(first_shift)),
    )
    scatter = lambda x: lax.psum_scatter(x, "blk", scatter_dimension=0, tiled=True)
    bits = bits_of("items", 2)
    n_blk = lax.axis_size("blk")
    sides = jnp.stack([side_of("items", bits[0]), side_of("items", bits[-1])]).astype(jnp.int32)
    part0, *grads, small_a = back(0, after=(ff_send, norm2))
    mine = [scatter(part0)]
    send0, send1, *feed_keeps, token = feed_weights(
        jnp.concatenate([1 - sides, sides]), ff_keep, ff_recv, norm2, norm2_recv, cot_flat, cot_recv, after=(small_a,)
    )
    feed_recvs = [swap(send0, "items", bits[0]), swap(send1, "items", bits[-1])]
    part1, *grads, small_b = back(1, into=grads, after=(token,))
    part2, *grads, small_c = back(2, into=grads)
    feed_sum = Summing(feed_keeps, feed_recvs, 1)
    small_op = Pack((small_a, small_b, small_c), small2, db1)
    while feed_sum.steps[feed_sum.at + 1][0] == "planar":
        (outs,), _, token = stage([feed_sum.op()], False)
        feed_sum.take(outs)
    (outs, (small,)), (part1,), token = stage([feed_sum.op(), small_op], False, through=(part1,), after=(small_c,))
    feed_sum.take(outs)
    mine.append(scatter(part1))
    ad = (limits, norm_all, norm_own, *grads, ctx, branch.reshape(tokens.shape))
    *sends, token = attend_weights(1 - bit, *ad, small=small, after=(token,))
    attend_recvs = [swap(x, "items", 1) for x in sends]
    *keeps, token = attend_weights(bit, *ad, after=(token,))
    attend_sum = Summing(keeps, attend_recvs, 0, small, True)
    whole_slice = 2 ** (len(bits) + len(bits_of("blk", 1)) - 1) != PIECES
    placed, turn, ready = False, 0, {0: [mine[0]], 2: [mine[1]]}
    while feed_sum.left or attend_sum.left:
        users = [one for one in (feed_sum, attend_sum) if one.left]
        results, passed, token = stage(
            [one.op() for one in users], turn > 0, True, after=(token, *ready.get(turn, ())), through=(part2,) if turn == 2 else ()
        )
        mine += [scatter(x) for x in passed]
        turn += 1
        for one, outs in zip(users, results):
            one.take(outs)
        if not feed_sum.left and not placed and feed_sum not in users and not whole_slice:
            grad_outer, grad_inner, token = feed_place(feed_sum.places(), feed_sum.mine, feed_sum.recvs, after=(token,))
            placed = True
    small = attend_sum.small
    if not whole_slice:
        sum_q, sum_k, sum_v, sum_o, token = attend_place(attend_sum.places(), attend_sum.mine, attend_sum.recvs, after=(token,))
    else:
        feed_units = feed_sum.units(feed_sum.mine, feed_sum.recvs)
        grad_outer = jnp.concatenate([u[:width] for u in feed_units], 0)
        grad_inner = jnp.concatenate([u[width:] for u in feed_units], 1)
        sum_q, sum_k, sum_v, sum_o = attend_sum.units(attend_sum.mine, attend_sum.recvs)
    grad_tokens, token = close(tokens, attg.reshape(tokens.shape), mine, vec(first_gain), after=(token,))
    return (
        out.reshape(tokens.shape), grad_tokens,
        small[0], small[1],
        sum_q, small[2], sum_k, sum_v, small[3],
        sum_o, small[6],
        small[4], small[5],
        grad_inner, small[8:8 + hidden // width].reshape(hidden), grad_outer, small[7],
    )


def solution(mesh):
    row = P("items", "blk", None)
    return jax.shard_map(
        local,
        mesh=mesh,
        in_specs=(row, P("items")) + (P(),) * 15 + (row,),
        out_specs=(row, row) + (P(),) * 15,
        check_vma=False,
    )
```
